32 devices in a mesh: slab: 8 (over z, y), face: 4 (over x, core).
Axes of the slice: x: 2, y: 2, z: 4, core: 2. Of those that a mesh axis runs over, the one named last changes fastest.
Arguments:
- rhs: bfloat16 [4, 8, 128, 4096], P(None, 'slab', None, 'face'), may hold values from -6 to 6
- inflow: bfloat16 [8, 128, 1024], P('slab', None, 'face'), may hold values from -6 to 6
- diag_tiles: bfloat16 [8, 32, 128, 128], P('slab', 'face')
- off_tiles: bfloat16 [8, 32, 4, 128, 128], P('slab', 'face'), may hold values from -0.5 to 0.5
- cols: int32 [8, 32, 4], P('slab', 'face'), may hold values from 0 to 31, as said below
- inverse_tiles: bfloat16 [8, 32, 128, 128], P('slab', 'face')
- coupling: bfloat16 [8, 8, 128, 128], P('slab', 'face'), may hold values from -1 to 1
- iface: int32 [8], P('face'), may hold values from 0 to 7, as said below
Outputs:
- solution: bfloat16 [4, 8, 128, 4096], P(None, 'slab', None, 'face')
The draws below stay inside these ranges and needn't reach their ends.
Inputs may be any that keep to these rules, and one draw needn't show every extreme that they name: `cols`: each column index lies within 2 tile rows of the block of 8 tile rows that holds its row; a block's first tile row reaches the tile row 2 before the block and its last reaches the tile row 2 after the block, wherever the slab has them. The 2 entries of one block of iface are distinct.
All inputs are finite; a program needn't handle non-finite values.
Results may differ from the reference program's by a relative error of at most 0.01.
Values may be sent and summed in bfloat16 or wider, within the bound.
No kernel may reach another device: no remote copies, remote signals or barrier semaphores. Data moves between devices by JAX's collectives and lax.ppermute only.
A program may use at most 64 MiB of HBM per device.

```python
import jax
import jax.numpy as jnp
from jax import lax

TILE = 128
SRC = 128
TILES_DEV = 8
NEIGH = 4
HALO_T = 2
IF_T = 2
TICKS = 4
SLABS = 8
TILES_SLAB = 32
ROWS_SLAB = 4096
IF_SLAB = 8


def draw_diag_tiles(key, part):
    noise_key = jax.random.fold_in(key, 11)
    shape = (SLABS, TILES_SLAB, TILE, TILE)
    noise = 0.08 * jax.random.normal(noise_key, shape, jnp.float32)
    level = 4.0 * jnp.ones((SLABS, TILES_SLAB, 1, 1), jnp.float32)
    return (level * jnp.eye(TILE, dtype=jnp.float32) + noise).astype(jnp.bfloat16)


def draw_inverse_tiles(key, part):
    noise_key = jax.random.fold_in(key, 13)
    shape = (SLABS, TILES_SLAB, TILE, TILE)
    noise = 0.006 * jax.random.normal(noise_key, shape, jnp.float32)
    level = 0.2 * jnp.ones((SLABS, TILES_SLAB, 1, 1), jnp.float32)
    return (level * jnp.eye(TILE, dtype=jnp.float32) + noise).astype(jnp.bfloat16)


def draw_cols(key, part):
    rows = jnp.arange(TILES_SLAB, dtype=jnp.int32)
    start = rows // TILES_DEV * TILES_DEV - HALO_T
    span = TILES_DEV + 2 * HALO_T
    picks = jax.random.randint(jax.random.fold_in(key, 21), (SLABS, TILES_SLAB, NEIGH), 0, span, dtype=jnp.int32)
    local = rows % TILES_DEV
    first = jnp.where(local == 0, 0, jnp.where(local == TILES_DEV - 1, span - 1, picks[:, :, 0]))
    picks = picks.at[:, :, 0].set(first.astype(jnp.int32))
    return jnp.clip(start[None, :, None] + picks, 0, TILES_SLAB - 1).astype(jnp.int32)


def draw_iface(key, part):
    blocks = IF_SLAB // IF_T
    keys = jax.random.split(jax.random.fold_in(key, 31), blocks)

    def one_block(block_key):
        return jax.random.permutation(block_key, TILES_DEV).astype(jnp.int32)
    orders = jax.vmap(one_block)(keys)
    offset = orders[:, :1] + (jnp.arange(blocks, dtype=jnp.int32) % 2)[:, None]
    rolled = (orders - offset) % TILES_DEV
    return rolled[:, :IF_T].reshape(-1).astype(jnp.int32)


def block_scale(key, shape, cuts, least, high):
    factor_of = 1.0
    for position, blocks in cuts:
        draws = jax.random.uniform(jax.random.fold_in(jax.random.fold_in(key, 6), position), (blocks,), jnp.float32, least / len(cuts), high / len(cuts))
        factor_of = factor_of * jnp.repeat(jnp.exp(draws), shape[position] // blocks).reshape((-1,) + (1,) * (len(shape) - 1 - position))
    return factor_of


def bell_draw(own_key, extent, spread, limit, cuts=(), kind=jnp.bfloat16):
    factor_of = block_scale(own_key, extent, cuts, -0.22, 0.18) if cuts else 1.0
    entries = jax.random.normal(own_key, extent, jnp.float32) * spread * factor_of
    return jnp.minimum(jnp.maximum(entries, -limit), limit).astype(kind)


def setup_inputs(seed: int = 0) -> dict:
    arg_keys = jax.random.split(jax.random.key(seed), 9)
    rhs = bell_draw(arg_keys[0], (TICKS, SLABS, SRC, ROWS_SLAB), 1.0, 6.0, ((1, 8), (3, 4)))
    inflow = bell_draw(arg_keys[1], (SLABS, SRC, IF_SLAB * TILE), 1.0, 6.0, ((0, 8), (2, 4)))
    diag_tiles = draw_diag_tiles(jax.random.fold_in(arg_keys[8], 71), 0)
    off_tiles = bell_draw(arg_keys[3], (SLABS, TILES_SLAB, NEIGH, TILE, TILE), 0.08, 0.5, ((0, 8), (1, 4)))
    cols = draw_cols(jax.random.fold_in(arg_keys[8], 71), 0)
    inverse_tiles = draw_inverse_tiles(jax.random.fold_in(arg_keys[8], 71), 0)
    coupling = bell_draw(arg_keys[6], (SLABS, IF_SLAB, TILE, TILE), (TILE // 4) ** -0.5, 1.0, ((0, 8), (1, 4)))
    iface = draw_iface(jax.random.fold_in(arg_keys[8], 71), 0)
    return dict(rhs=rhs, inflow=inflow, diag_tiles=diag_tiles, off_tiles=off_tiles, cols=cols, inverse_tiles=inverse_tiles, coupling=coupling, iface=iface)


def tile_apply(tiles, values):
    return jnp.einsum("rij,srj->sri", tiles.astype(jnp.float32), values.astype(jnp.float32))


def slab_tick(rhs_slab, incoming, diag_slab, off_slab, cols_slab, inverse_slab, coupling_slab, iface):
    count = diag_slab.shape[0]
    width = diag_slab.shape[1]
    sources = rhs_slab.shape[0]
    inbound = incoming.reshape(sources, -1, width).astype(jnp.float32)
    coupled = jnp.einsum("qij,sqj->sqi", coupling_slab.astype(jnp.float32), inbound)
    targets = ((jnp.arange(IF_SLAB, dtype=jnp.int32) // IF_T) * TILES_DEV + iface).astype(jnp.int32)
    right = rhs_slab.reshape(sources, count, width).astype(jnp.float32)
    right = right.at[:, targets].add(-coupled)
    right = right.astype(jnp.bfloat16)
    field = tile_apply(inverse_slab, right).astype(jnp.bfloat16)
    for sweep in range(2):
        gathered = field[:, cols_slab]
        product = tile_apply(diag_slab, field) + jnp.einsum("rkij,srkj->sri", off_slab.astype(jnp.float32), gathered.astype(jnp.float32))
        correction = (right.astype(jnp.float32) - product).astype(jnp.bfloat16)
        field = (field.astype(jnp.float32) + tile_apply(inverse_slab, correction)).astype(jnp.bfloat16)
    sent = field[:, targets].reshape(sources, -1)
    return field.reshape(sources, count * width), sent


def reference(rhs, inflow, diag_tiles, off_tiles, cols, inverse_tiles, coupling, iface):
    incoming = inflow
    results = []
    for tick in range(TICKS):
        def one_slab(pieces):
            return slab_tick(pieces[0], pieces[1], pieces[2], pieces[3], pieces[4], pieces[5], pieces[6], iface)

        fields, sent = lax.map(one_slab, (rhs[tick], incoming, diag_tiles, off_tiles, cols, inverse_tiles, coupling))
        results.append(fields)
        incoming = jnp.concatenate([jnp.zeros_like(sent[:1]), sent[:-1]], axis=0)
    return jnp.stack(results)
```

```python
import functools

import jax
import jax.numpy as jnp
from jax import lax
from jax.experimental import pallas as pl
from jax.experimental.pallas import tpu as pltpu
from jax.sharding import PartitionSpec as P

HALO = 2
BF = jnp.bfloat16
F32 = jnp.float32


def dot_nt(a, b):
    return lax.dot_general(a, b, (((1,), (1,)), ((), ())), preferred_element_type=F32)


def dot_nn(a, b):
    return lax.dot_general(a, b, (((1,), (0,)), ((), ())), preferred_element_type=F32)


class Dims:
    def __init__(self, ticks, sources, count, neigh, width, nq, faces):
        self.ticks, self.sources, self.count, self.neigh = ticks, sources, count, neigh
        self.width, self.nq, self.faces = width, nq, faces
        self.batch = ticks * sources
        self.group = nq * width
        self.slots = max(4, min(faces, 5))
        self.shifts = None if faces <= 4 else (-2, -1, 0, 1, 2)
        self.hops = 4 if faces <= 4 else 5
        self.ext = count + 2 * HALO
        self.at_iface = count * neigh
        self.at_face = self.at_iface + nq

    def source_face(self, face, hop):
        return face ^ hop if self.shifts is None else face + self.shifts[hop]

    def slot(self, face):
        return lax.rem(face + 2 * self.slots, self.slots)


def sweep_rows(d, meta, right_at, ext, diag, off, inv, store, starts, rows):
    def one(r, carry):
        w = jnp.concatenate([diag[r]] + [off[r, k] for k in range(d.neigh)], axis=1)
        inverse = inv[r]
        c = [meta[r * d.neigh + k] for k in range(d.neigh)]
        for s in starts:
            span = pl.ds(s, rows)
            own = ext[r + HALO, span, :]
            x = jnp.concatenate([own] + [ext[c[k], span, :] for k in range(d.neigh)], axis=1)
            correction = (right_at(r, span).astype(F32) - dot_nt(x, w)).astype(BF)
            store(r, span, (own.astype(F32) + dot_nt(correction, inverse)).astype(BF))
        return carry

    lax.fori_loop(0, d.count, one, 0)


def edge_rows(d, parity):
    last = d.count - HALO
    return last * (1 - parity), last * parity


def place_halo(d, parity, ext, pair, cross, span, source):
    up = d.count + HALO
    ext[pl.ds(up * (1 - parity), HALO), span, :] = pair[:, source, :]
    ext[pl.ds(up * parity, HALO), span, :] = cross[:, source, :]


def first_kernel(d, meta, rhs, inflow, inv, coupling, right, field, grows, gfield, pair, cross):
    face = meta[d.at_face]
    parity = lax.rem(face, 2)
    w = d.width
    for t in range(d.ticks):
        for r in range(d.count):
            right[r, t * d.sources : (t + 1) * d.sources, :] = rhs[t, :, r * w : (r + 1) * w]
    for q in range(d.nq):
        row = meta[d.at_iface + q]
        coupled = dot_nt(inflow[:, q * w : (q + 1) * w], coupling[q])
        right[row, 0 : d.sources, :] = (right[row, 0 : d.sources, :].astype(F32) - coupled).astype(BF)
        turned = coupling[q].astype(F32).T.astype(BF)
        grows[q] = turned
        gfield[q] = dot_nt(turned, inv[row]).astype(BF)

    def one(r, carry):
        field[r] = dot_nt(right[r], inv[r]).astype(BF)
        return carry

    lax.fori_loop(0, d.count, one, 0)
    for start, buffer in zip(edge_rows(d, parity), (pair, cross)):
        for e in range(HALO):
            buffer[e, 0 : d.batch, :] = field[start + e]
            for q in range(d.nq):
                hit = meta[d.at_iface + q] == start + e
                buffer[e, d.batch + q * w : d.batch + (q + 1) * w, :] = jnp.where(hit, gfield[q], jnp.zeros((w, w), BF))


def batch_kernel(d, last, meta, right, field, pair_in, cross_in, diag, off, inv, *rest):
    if last:
        out, faces_out, sent, ext = rest
    else:
        out, pair, cross, ext = rest
    parity = lax.rem(meta[d.at_face], 2)
    span = pl.ds(0, d.batch)
    ext[HALO : HALO + d.count] = field[...]
    place_halo(d, parity, ext, pair_in, cross_in, span, span)

    def store(r, span, value):
        out[r, span, :] = value

    sweep_rows(
        d, meta, lambda r, span: right[r, span, :], ext, diag, off, inv, store, range(0, d.batch, d.group), d.group
    )
    if last:
        for q in range(d.nq):
            row = meta[d.at_iface + q]
            for t in range(d.ticks):
                faces_out[t, q] = out[row, t * d.sources : (t + 1) * d.sources, :]
            sent[q] = out[row, 0 : d.sources, :]
    else:
        for start, buffer in zip(edge_rows(d, parity), (pair, cross)):
            buffer[...] = out[pl.ds(start, HALO)]


def group_start(d, face):
    return pl.multiple_of(d.slot(face) * d.group, d.group)


def fill_grows(d, meta, grows, gright, face):
    gright[...] = jnp.zeros_like(gright)
    for q in range(d.nq):
        row = meta[d.at_iface + q]
        gright[row, pl.ds(group_start(d, face) + q * d.width, d.width), :] = grows[q]


def coupling_first_kernel(d, meta, grows, gfield, pair_in, cross_in, diag, off, inv, out, pair, cross, ext, gright):
    face = meta[d.at_face]
    parity = lax.rem(face, 2)
    fill_grows(d, meta, grows, gright, face)
    ext[...] = jnp.zeros_like(ext)
    out[...] = jnp.zeros_like(out)
    for q in range(d.nq):
        row = meta[d.at_iface + q] + HALO
        ext[row, pl.ds(group_start(d, face) + q * d.width, d.width), :] = gfield[q]
    up = d.count + HALO
    source = pl.ds(d.batch, d.group)
    pair_face, cross_face = face + 1 - 2 * parity, face - 1 + 2 * parity
    ext[pl.ds(up * (1 - parity), HALO), pl.ds(group_start(d, pair_face), d.group), :] = pair_in[:, source, :]
    ext[pl.ds(up * parity, HALO), pl.ds(group_start(d, cross_face), d.group), :] = cross_in[:, source, :]

    def store(r, span, value):
        out[r, span, :] = value

    starts = [group_start(d, face + shift) for shift in (-1, 0, 1)]
    sweep_rows(d, meta, lambda r, span: gright[r, span, :], ext, diag, off, inv, store, starts, d.group)
    for start, buffer in zip(edge_rows(d, parity), (pair, cross)):
        for i, s in enumerate(starts):
            buffer[:, i * d.group : (i + 1) * d.group, :] = out[pl.ds(start, HALO), pl.ds(s, d.group), :]


def coupling_last_kernel(d, meta, grows, gfirst, pair_in, cross_in, diag, off, inv, out, chain, ext, gright):
    face = meta[d.at_face]
    parity = lax.rem(face, 2)
    fill_grows(d, meta, grows, gright, face)
    ext[...] = jnp.zeros_like(ext)
    ext[HALO : HALO + d.count] = gfirst[...]
    up = d.count + HALO
    neighbours = ((up * (1 - parity), face + 1 - 2 * parity, pair_in), (up * parity, face - 1 + 2 * parity, cross_in))
    for start, other, block in neighbours:
        for i, shift in enumerate((-1, 0, 1)):
            ext[pl.ds(start, HALO), pl.ds(group_start(d, other + shift), d.group), :] = block[
                :, i * d.group : (i + 1) * d.group, :
            ]

    def store(r, span, value):
        out[span, pl.ds(pl.multiple_of(r * d.width, d.width), d.width)] = value

    starts = range(0, d.slots * d.group, d.group)
    sweep_rows(d, meta, lambda r, span: gright[r, span, :], ext, diag, off, inv, store, starts, d.group)
    for q in range(d.nq):
        lane = pl.multiple_of(meta[d.at_iface + q] * d.width, d.width)
        chain[:, q * d.width : (q + 1) * d.width] = out[:, pl.ds(lane, d.width)]


def chain_kernel(d, tick, meta, chain, faces_out, *rest):
    arrived, sent = rest[:-1], rest[-1]
    face = meta[d.at_face]
    total = jnp.zeros((d.sources, d.group), F32)
    for hop, block in enumerate(arrived):
        x = jnp.concatenate([block[q] for q in range(d.nq)], axis=1)
        total += dot_nn(x, chain[pl.ds(group_start(d, d.source_face(face, hop)), d.group), :])
    for q in range(d.nq):
        sent[q] = (faces_out[tick, q].astype(F32) - total[:, q * d.width : (q + 1) * d.width]).astype(BF)


def final_kernel(d, meta, fields, coupled, *rest):
    arrived, out = rest[:-1], rest[-1]
    face = meta[d.at_face]
    w = d.width
    for r in range(d.count):
        out[0, :, r * w : (r + 1) * w] = fields[r, 0 : d.sources, :]
    for t in range(1, d.ticks):
        blocks = arrived[(t - 1) * d.hops : t * d.hops]
        total = jnp.zeros((d.sources, d.count * w), F32)
        for hop, block in enumerate(blocks):
            x = jnp.concatenate([block[q] for q in range(d.nq)], axis=1)
            total += dot_nn(x, coupled[pl.ds(group_start(d, d.source_face(face, hop)), d.group), :])
        for r in range(d.count):
            base = fields[r, t * d.sources : (t + 1) * d.sources, :].astype(F32)
            out[t, :, r * w : (r + 1) * w] = (base - total[:, r * w : (r + 1) * w]).astype(BF)


def call(body, name, inputs, outs, scratch=(), flops=0):
    smem = pl.BlockSpec(memory_space=pltpu.SMEM)
    vmem = pl.BlockSpec(memory_space=pltpu.VMEM)
    moved = sum(x.size * x.dtype.itemsize for x in inputs) + sum(2 * functools.reduce(lambda a, b: a * b, s) for s in outs)
    return pl.pallas_call(
        body,
        name=name,
        out_shape=[jax.ShapeDtypeStruct(s, BF) for s in outs],
        in_specs=[smem] + [vmem] * (len(inputs) - 1),
        out_specs=[vmem] * len(outs),
        scratch_shapes=[pltpu.VMEM(s, BF) for s in scratch],
        compiler_params=pltpu.CompilerParams(vmem_limit_bytes=32 * 1024 * 1024),
        cost_estimate=pl.CostEstimate(flops=flops, bytes_accessed=moved, transcendentals=0),
    )(*inputs)


def on_device(rhs, inflow, diag_tiles, off_tiles, cols, inverse_tiles, coupling, iface):
    faces, slabs = lax.axis_size("face"), lax.axis_size("slab")
    ticks, _, sources, _ = rhs.shape
    _, count, neigh, width, _ = off_tiles.shape
    nq = coupling.shape[1]
    d = Dims(ticks, sources, count, neigh, width, nq, faces)
    diag, off, inv, couple = diag_tiles[0], off_tiles[0], inverse_tiles[0], coupling[0]
    face = lax.axis_index("face").astype(jnp.int32)
    local = cols[0].reshape(-1) - (face * count - HALO)
    meta = jnp.concatenate([local, iface, face[None]])
    tile = width * width

    pairing = [(i, i ^ 1) for i in range(faces) if i ^ 1 < faces]
    crossing = [(i, ((i + 1) ^ 1) - 1) for i in range(faces) if 0 <= ((i + 1) ^ 1) - 1 < faces]

    def exchange(pair, cross):
        got = lax.ppermute(cross, "face", crossing)
        return lax.ppermute(pair, "face", pairing), got

    def onward(block):
        got = []
        for hop in range(d.hops):
            route = []
            for s in range(1, slabs):
                for f in range(faces):
                    g = d.source_face(f, hop)
                    if 0 <= g < faces:
                        route.append(((s - 1) * faces + g, s * faces + f))
            got.append(lax.ppermute(block, ("slab", "face"), route))
        return got

    batch, group, ext, wide = d.batch, d.group, d.ext, d.slots * d.group
    right, field, grows, gfield, pair, cross = call(
        functools.partial(first_kernel, d),
        "first",
        [meta, rhs[:, 0], inflow[0], inv, couple],
        [(count, batch, width)] * 2 + [(nq, width, width)] * 2 + [(HALO, batch + group, width)] * 2,
        flops=2 * batch * count * tile,
    )
    pair0, cross0 = exchange(pair, cross)
    field, pair, cross = call(
        functools.partial(batch_kernel, d, False),
        "second",
        [meta, right, field, pair0, cross0, diag, off, inv],
        [(count, batch, width)] + [(HALO, batch, width)] * 2,
        [(ext, batch, width)],
        flops=2 * batch * count * tile * (neigh + 2),
    )
    pair1, cross1 = exchange(pair, cross)
    gfirst, gpair, gcross = call(
        functools.partial(coupling_first_kernel, d),
        "coupling_first",
        [meta, grows, gfield, pair0, cross0, diag, off, inv],
        [(count, wide, width)] + [(HALO, 3 * group, width)] * 2,
        [(ext, wide, width), (count, wide, width)],
        flops=2 * 3 * group * count * tile * (neigh + 2),
    )
    gpair, gcross = exchange(gpair, gcross)
    fields, faces_out, sent = call(
        functools.partial(batch_kernel, d, True),
        "third",
        [meta, right, field, pair1, cross1, diag, off, inv],
        [(count, batch, width), (ticks, nq, sources, width), (nq, sources, width)],
        [(ext, batch, width)],
        flops=2 * batch * count * tile * (neigh + 2),
    )
    arrived = onward(sent)
    coupled, chain = call(
        functools.partial(coupling_last_kernel, d),
        "coupling_last",
        [meta, grows, gfirst, gpair, gcross, diag, off, inv],
        [(wide, count * width), (wide, group)],
        [(ext, wide, width), (count, wide, width)],
        flops=2 * wide * count * tile * (neigh + 2),
    )
    everything = list(arrived)
    for tick in range(1, ticks - 1):
        (sent,) = call(
            functools.partial(chain_kernel, d, tick),
            "chain",
            [meta, chain, faces_out] + arrived,
            [(nq, sources, width)],
            flops=2 * sources * wide * group,
        )
        arrived = onward(sent)
        everything += arrived
    (out,) = call(
        functools.partial(final_kernel, d),
        "final",
        [meta, fields, coupled] + everything,
        [(ticks, sources, count * width)],
        flops=2 * (ticks - 1) * sources * wide * count * width,
    )
    return out[:, None]


def solution(mesh):
    placed = (
        P(None, "slab", None, "face"),
        P("slab", None, "face"),
        P("slab", "face", None, None),
        P("slab", "face", None, None, None),
        P("slab", "face", None),
        P("slab", "face", None, None),
        P("slab", "face", None, None),
        P("face"),
    )
    return jax.shard_map(
        on_device,
        mesh=mesh,
        in_specs=placed,
        out_specs=P(None, "slab", None, "face"),
        check_vma=False,
    )
```

```python
import functools
import math

import jax
import jax.numpy as jnp
from jax import lax
from jax.experimental import pallas as pl
from jax.experimental.pallas import tpu as pltpu
from jax.sharding import PartitionSpec as P

HALO = 2
BF = jnp.bfloat16
F32 = jnp.float32


def dot_nt(a, b):
    return lax.dot_general(a, b, (((1,), (1,)), ((), ())), preferred_element_type=F32)


def dot_nn(a, b):
    return lax.dot_general(a, b, (((1,), (0,)), ((), ())), preferred_element_type=F32)


class Dims:
    def __init__(self, ticks, sources, count, neigh, width, nq, faces):
        self.ticks, self.sources, self.count, self.neigh = ticks, sources, count, neigh
        self.width, self.nq, self.faces = width, nq, faces
        self.batch = ticks * sources
        self.group = nq * width
        self.ext = count + 2 * HALO
        self.depth = (1 + neigh) * width
        self.slots = 4 if faces <= 4 else 6
        self.wide = self.slots * self.group
        self.last = count - HALO
        self.up = count + HALO

    def start(self, face):
        return pl.multiple_of(lax.rem(face + 2 * self.slots, self.slots) * self.group, self.group)

    def first_col(self, face):
        return face * self.count - HALO


def edge_rows(d, parity):
    return d.last * (1 - parity), d.last * parity


def first_kernel(d, face_ref, iface, rhs, inflow, inv, coupling, field, gfield, pair, cross, right, flow, tiles, couple, sems):
    w = d.width
    copies = [
        pltpu.make_async_copy(inv, tiles, sems.at[0]),
        pltpu.make_async_copy(coupling, couple, sems.at[1]),
        pltpu.make_async_copy(inflow, flow, sems.at[2]),
    ]
    copies += [
        pltpu.make_async_copy(rhs.at[:, :, pl.ds(r * w, w)], right.at[r], sems.at[3 + r]) for r in range(d.count)
    ]
    for copy in copies:
        copy.start()
    parity = lax.rem(face_ref[0], 2)
    for copy in copies[:3]:
        copy.wait()
    coupled = []
    for q in range(d.nq):
        coupled.append(dot_nt(flow[:, q * w : (q + 1) * w], couple[q]))
        turned = couple[q].astype(F32).T.astype(BF)
        gfield[q] = dot_nt(turned, tiles[iface[q]]).astype(BF)
    for r in range(d.count):
        copies[3 + r].wait()
        field[r] = dot_nt(right[r].reshape(d.batch, w), tiles[r]).astype(BF)
    for q in range(d.nq):
        row = iface[q]
        corrected = (right[row, 0].astype(F32) - coupled[q]).astype(BF)
        field[row, 0 : d.sources, :] = dot_nt(corrected, tiles[row]).astype(BF)
    for start, buffer in zip(edge_rows(d, parity), (pair, cross)):
        for e in range(HALO):
            buffer[e, 0 : d.batch, :] = field[start + e]
            for q in range(d.nq):
                hit = iface[q] == start + e
                buffer[e, d.batch + q * w : d.batch + (q + 1) * w, :] = jnp.where(hit, gfield[q], jnp.zeros((w, w), BF))


def fold_kernel(d, after, diag, off, inv, folded):
    w = d.width
    for r in range(d.count):
        tiles = jnp.concatenate([diag[r]] + [off[r, k] for k in range(d.neigh)], axis=1)
        product = dot_nn(inv[r], tiles)
        rows = lax.broadcasted_iota(jnp.int32, (w, w), 0)
        unit = (rows == lax.broadcasted_iota(jnp.int32, (w, w), 1)).astype(F32)
        for k in range(1 + d.neigh):
            part = product[:, k * w : (k + 1) * w].T
            folded[r, k * w : (k + 1) * w, :] = ((unit if k == 0 else 0.0) - part).astype(BF)


def sweep(d, cols, face, ext, span, r, folded):
    x = [ext[r + HALO, span, :]] + [ext[cols[r, k] - d.first_col(face), span, :] for k in range(d.neigh)]
    return dot_nn(jnp.concatenate(x, axis=1), folded[r])


def batch_kernel(d, last, face_ref, iface, cols, field, base, pair_in, cross_in, folded, *rest):
    if last:
        out, faces_out, sent, ext = rest
    else:
        out, pair, cross, ext = rest
    face = face_ref[0]
    parity = lax.rem(face, 2)
    ext[HALO : HALO + d.count] = field[...]
    ext[pl.ds(d.up * (1 - parity), HALO)] = pair_in[:, 0 : d.batch, :]
    ext[pl.ds(d.up * parity, HALO)] = cross_in[:, 0 : d.batch, :]
    for r in range(d.count):
        for s in range(0, d.batch, d.group):
            span = pl.ds(s, d.group)
            out[r, span, :] = (base[r, span, :].astype(F32) + sweep(d, cols, face, ext, span, r, folded)).astype(BF)
    if last:
        for q in range(d.nq):
            row = iface[q]
            for t in range(d.ticks):
                faces_out[t, q] = out[row, t * d.sources : (t + 1) * d.sources, :]
            sent[q] = out[row, 0 : d.sources, :]
    else:
        for start, buffer in zip(edge_rows(d, parity), (pair, cross)):
            buffer[...] = out[pl.ds(start, HALO)]


def coupling_first_kernel(d, face_ref, iface, cols, gfield, pair_in, cross_in, folded, after, out, pair, cross, met):
    face = face_ref[0]
    parity = lax.rem(face, 2)
    w = d.width
    met[...] = jnp.zeros_like(met)
    for r in range(d.count):
        lanes = slice(r * w, (r + 1) * w)
        for q in range(d.nq):
            met[2 * HALO + q, :, lanes] = jnp.where(iface[q] == r, folded[r, 0:w, :], jnp.zeros((w, w), BF))
        for k in range(d.neigh):
            c = cols[r, k] - d.first_col(face)
            inside = jnp.logical_and(c >= HALO, c < d.up)
            at = jnp.where(c < HALO, c, c - d.count)
            hit = jnp.logical_not(inside)
            for q in range(d.nq):
                here = c == iface[q] + HALO
                at = jnp.where(here, 2 * HALO + q, at)
                hit = jnp.logical_or(hit, here)

            @pl.when(hit)
            def _():
                met[at, :, lanes] += folded[r, (1 + k) * w : (2 + k) * w, :]

    out[...] = jnp.zeros_like(out)

    def put(start, rows, value):
        for r in range(d.count):
            out[r, pl.ds(start, rows), :] = value[:, r * w : (r + 1) * w].astype(BF)

    pair_face, cross_face = face + 1 - 2 * parity, face - 1 + 2 * parity
    for at, other, block in ((HALO * (1 - parity), pair_face, pair_in), (HALO * parity, cross_face, cross_in)):
        x = jnp.concatenate([block[e, d.batch : d.batch + d.group, :] for e in range(HALO)], axis=1)
        tiles = jnp.concatenate([met[at + e] for e in range(HALO)], axis=0)
        put(d.start(other), d.group, dot_nn(x, tiles))
    for q in range(d.nq):
        start = d.start(face) + q * w
        put(start, w, dot_nn(gfield[q], met[2 * HALO + q]))
        row = iface[q]
        span = pl.ds(pl.multiple_of(start, w), w)
        out[row, span, :] = (out[row, span, :].astype(F32) + gfield[q].astype(F32)).astype(BF)
    for start, buffer in zip(edge_rows(d, parity), (pair, cross)):
        for i, shift in enumerate((-1, 0, 1)):
            buffer[:, i * d.group : (i + 1) * d.group, :] = out[pl.ds(start, HALO), pl.ds(d.start(face + shift), d.group), :]


def coupling_last_kernel(d, face_ref, iface, cols, gfield, gfirst, pair_in, cross_in, folded, out, chain, ext):
    face = face_ref[0]
    parity = lax.rem(face, 2)
    w = d.width
    ext[0:HALO] = jnp.zeros((HALO, d.wide, w), BF)
    ext[d.up : d.ext] = jnp.zeros((HALO, d.wide, w), BF)
    ext[HALO : HALO + d.count] = gfirst[...]
    neighbours = ((d.up * (1 - parity), face + 1 - 2 * parity, pair_in), (d.up * parity, face - 1 + 2 * parity, cross_in))
    for start, other, block in neighbours:
        for i, shift in enumerate((-1, 0, 1)):
            ext[pl.ds(start, HALO), pl.ds(d.start(other + shift), d.group), :] = block[:, i * d.group : (i + 1) * d.group, :]
    for r in range(d.count):
        for s in range(0, d.wide, d.group):
            span = pl.ds(s, d.group)
            out[span, r * w : (r + 1) * w] = sweep(d, cols, face, ext, span, r, folded).astype(BF)
    for q in range(d.nq):
        lane = pl.ds(pl.multiple_of(iface[q] * w, w), w)
        span = pl.ds(pl.multiple_of(d.start(face) + q * w, w), w)
        out[span, lane] = (out[span, lane].astype(F32) + gfield[q].astype(F32)).astype(BF)
        chain[:, q * w : (q + 1) * w] = out[:, lane]


def arrived_blocks(d, face, own, other):
    parity = lax.rem(face, 2)
    shifts = chip_shifts(d.faces)
    for k, shift in enumerate(shifts):
        there = face + 2 * shift if len(shifts) != 2 else face ^ (2 * shift)
        for block, source in ((own, there), (other, there + 1 - 2 * parity)):
            yield jnp.concatenate([block(k, q) for q in range(d.nq)], axis=1), d.start(source)


def chip_shifts(faces):
    return (0,) if faces <= 2 else (0, 1) if faces <= 4 else (0, -1, 1)


def chain_kernel(d, tick, face_ref, chain, faces_out, other, *rest):
    own, sent = rest[:-1], rest[-1]
    total = jnp.zeros((d.sources, d.group), F32)
    for x, start in arrived_blocks(d, face_ref[0], lambda k, q: own[k][q], lambda k, q: other[k, q]):
        total += dot_nn(x, chain[pl.ds(start, d.group), :])
    for q in range(d.nq):
        sent[q] = (faces_out[tick, q].astype(F32) - total[:, q * d.width : (q + 1) * d.width]).astype(BF)


def final_kernel(d, face_ref, fields, coupled, *rest):
    arrived, out = rest[:-1], rest[-1]
    w = d.width
    hops = len(chip_shifts(d.faces))
    for r in range(d.count):
        out[0, :, r * w : (r + 1) * w] = fields[r, 0 : d.sources, :]
    for t in range(1, d.ticks):
        other, *own = arrived[(t - 1) * (hops + 1) : t * (hops + 1)]
        total = jnp.zeros((d.sources, d.count * w), F32)
        for x, start in arrived_blocks(d, face_ref[0], lambda k, q: own[k][q], lambda k, q: other[k, q]):
            total += dot_nn(x, coupled[pl.ds(start, d.group), :])
        for r in range(d.count):
            base = fields[r, t * d.sources : (t + 1) * d.sources, :].astype(F32)
            out[t, :, r * w : (r + 1) * w] = (base - total[:, r * w : (r + 1) * w]).astype(BF)


def call(body, name, smem, inputs, outs, scratch=(), flops=0, anywhere=(), sems=0):
    vmem = pl.BlockSpec(memory_space=pltpu.VMEM)
    moved = sum(x.size * x.dtype.itemsize for x in inputs) + sum(2 * math.prod(s) for s in outs)
    specs = [pl.BlockSpec(memory_space=pl.ANY) if i in anywhere else vmem for i in range(len(inputs))]
    return pl.pallas_call(
        body,
        name=name,
        out_shape=[jax.ShapeDtypeStruct(s, BF) for s in outs],
        in_specs=[pl.BlockSpec(memory_space=pltpu.SMEM)] * len(smem) + specs,
        out_specs=[vmem] * len(outs),
        scratch_shapes=[pltpu.VMEM(s, BF) for s in scratch] + ([pltpu.SemaphoreType.DMA((sems,))] if sems else []),
        compiler_params=pltpu.CompilerParams(vmem_limit_bytes=32 * 1024 * 1024),
        cost_estimate=pl.CostEstimate(flops=flops, bytes_accessed=moved, transcendentals=0),
    )(*smem, *inputs)


def on_device(rhs, inflow, diag_tiles, off_tiles, cols, inverse_tiles, coupling, iface):
    faces, slabs = lax.axis_size("face"), lax.axis_size("slab")
    ticks, _, sources, _ = rhs.shape
    _, count, neigh, width, _ = off_tiles.shape
    nq = coupling.shape[1]
    d = Dims(ticks, sources, count, neigh, width, nq, faces)
    diag, off, inv, couple, cols = diag_tiles[0], off_tiles[0], inverse_tiles[0], coupling[0], cols[0]
    face = lax.axis_index("face").astype(jnp.int32)[None]
    face, iface, cols = (pltpu.with_memory_space_constraint(x, pltpu.SMEM) for x in (face, iface, cols))
    tile = width * width

    pairing = [(i, i ^ 1) for i in range(faces) if i ^ 1 < faces]
    crossing = [(i, ((i + 1) ^ 1) - 1) for i in range(faces) if 0 <= ((i + 1) ^ 1) - 1 < faces]

    def exchange(pair, cross):
        got = lax.ppermute(cross, "face", crossing)
        return lax.ppermute(pair, "face", pairing), got

    def onward(block):
        shifts = chip_shifts(faces)
        own = []
        for shift in shifts:
            route = []
            for s in range(1, slabs):
                for f in range(faces):
                    g = f ^ (2 * shift) if len(shifts) == 2 else f + 2 * shift
                    if 0 <= g < faces:
                        route.append(((s - 1) * faces + g, s * faces + f))
            own.append(lax.ppermute(block, ("slab", "face"), route))
        return [lax.ppermute(jnp.stack(own), "face", pairing)] + own

    batch, group, ext, wide = d.batch, d.group, d.ext, d.wide
    field, gfield, pair, cross = call(
        functools.partial(first_kernel, d),
        "first",
        [face, iface],
        [pltpu.with_memory_space_constraint(x, pltpu.HBM) for x in (rhs[:, 0], inflow[0], inv, couple)],
        [(count, batch, width), (nq, width, width)] + [(HALO, batch + group, width)] * 2,
        [(count, ticks, sources, width), (sources, group), (count, width, width), (nq, width, width)],
        flops=2 * batch * count * tile,
        anywhere=(0, 1, 2, 3),
        sems=3 + count,
    )
    (folded,) = call(
        functools.partial(fold_kernel, d),
        "fold",
        [],
        [gfield, diag, off, inv],
        [(count, d.depth, width)],
        flops=2 * width * count * tile * (neigh + 1),
        anywhere=(0,),
    )
    pair0, cross0 = exchange(pair, cross)
    once, pair, cross = call(
        functools.partial(batch_kernel, d, False),
        "second",
        [face, iface, cols],
        [field, field, pair0, cross0, folded],
        [(count, batch, width)] + [(HALO, batch, width)] * 2,
        [(ext, batch, width)],
        flops=2 * batch * count * tile * (neigh + 1),
    )
    pair1, cross1 = exchange(pair, cross)
    gfirst, gpair, gcross = call(
        functools.partial(coupling_first_kernel, d),
        "coupling_first",
        [face, iface, cols],
        [gfield, pair0, cross0, folded, once],
        [(count, wide, width)] + [(HALO, 3 * group, width)] * 2,
        [(2 * HALO + nq, width, count * width)],
        flops=2 * (2 * HALO + nq) * width * count * tile,
        anywhere=(4,),
    )
    gpair, gcross = exchange(gpair, gcross)
    fields, faces_out, sent = call(
        functools.partial(batch_kernel, d, True),
        "third",
        [face, iface, cols],
        [once, field, pair1, cross1, folded],
        [(count, batch, width), (ticks, nq, sources, width), (nq, sources, width)],
        [(ext, batch, width)],
        flops=2 * batch * count * tile * (neigh + 1),
    )
    arrived = onward(sent)
    coupled, chain = call(
        functools.partial(coupling_last_kernel, d),
        "coupling_last",
        [face, iface, cols],
        [gfield, gfirst, gpair, gcross, folded],
        [(wide, count * width), (wide, group)],
        [(ext, wide, width)],
        flops=2 * wide * count * tile * (neigh + 1),
    )
    everything = list(arrived)
    for tick in range(1, ticks - 1):
        (sent,) = call(
            functools.partial(chain_kernel, d, tick),
            "chain",
            [face],
            [chain, faces_out] + arrived,
            [(nq, sources, width)],
            flops=2 * sources * wide * group,
        )
        arrived = onward(sent)
        everything += arrived
    (out,) = call(
        functools.partial(final_kernel, d),
        "final",
        [face],
        [fields, coupled] + everything,
        [(ticks, sources, count * width)],
        flops=2 * (ticks - 1) * sources * wide * count * width,
    )
    return out[:, None]


def solution(mesh):
    placed = (
        P(None, "slab", None, "face"),
        P("slab", None, "face"),
        P("slab", "face", None, None),
        P("slab", "face", None, None, None),
        P("slab", "face", None),
        P("slab", "face", None, None),
        P("slab", "face", None, None),
        P("face"),
    )
    return jax.shard_map(
        on_device,
        mesh=mesh,
        in_specs=placed,
        out_specs=P(None, "slab", None, "face"),
        check_vma=False,
    )
```

```python
import functools
import math

import jax
import jax.numpy as jnp
from jax import lax
from jax.experimental import pallas as pl
from jax.experimental.pallas import tpu as pltpu
from jax.sharding import PartitionSpec as P

HALO = 2
BF = jnp.bfloat16
F32 = jnp.float32


def dot_nt(a, b):
    return lax.dot_general(a, b, (((1,), (1,)), ((), ())), preferred_element_type=F32)


def dot_nn(a, b):
    return lax.dot_general(a, b, (((1,), (0,)), ((), ())), preferred_element_type=F32)


class Dims:
    def __init__(self, ticks, sources, count, neigh, width, nq, faces):
        self.ticks, self.sources, self.count, self.neigh = ticks, sources, count, neigh
        self.width, self.nq, self.faces = width, nq, faces
        self.batch = ticks * sources
        self.group = nq * width
        self.ext = count + 2 * HALO
        self.depth = (1 + neigh) * width
        self.slots = 4 if faces <= 4 else 6
        self.wide = self.slots * self.group
        self.last = count - HALO
        self.up = count + HALO

    def start(self, face):
        return pl.multiple_of(lax.rem(face + 2 * self.slots, self.slots) * self.group, self.group)

    def first_col(self, face):
        return face * self.count - HALO


def edge_rows(d, parity):
    return d.last * (1 - parity), d.last * parity


def first_kernel(d, face_ref, iface_hbm, rhs, inflow, inv, coupling, field, gfield, pair, cross, iface, right, flow, tiles, couple, sems):
    w = d.width
    moves = [(inv, tiles)] + [(rhs.at[t], right.at[t]) for t in range(d.ticks)]
    moves += [(iface_hbm, iface), (coupling, couple), (inflow, flow)]
    copies = [pltpu.make_async_copy(a, b, sems.at[i]) for i, (a, b) in enumerate(moves)]
    for copy in copies:
        copy.start()
    for copy in copies:
        copy.wait()
    parity = lax.rem(face_ref[0], 2)
    for r in range(d.count):
        x = jnp.concatenate([right[t, :, r * w : (r + 1) * w] for t in range(d.ticks)], axis=0)
        field[r] = dot_nt(x, tiles[r]).astype(BF)
    for q in range(d.nq):
        row = iface[q]
        turned = couple[q].astype(F32).T.astype(BF)
        gfield[q] = dot_nt(turned, tiles[row]).astype(BF)
        coupled = dot_nn(flow[:, q * w : (q + 1) * w], turned)
        corrected = right[0, :, pl.ds(pl.multiple_of(row * w, w), w)].astype(F32) - coupled
        field[row, 0 : d.sources, :] = dot_nt(corrected.astype(BF), tiles[row]).astype(BF)
    for start, buffer in zip(edge_rows(d, parity), (pair, cross)):
        for e in range(HALO):
            buffer[e, 0 : d.batch, :] = field[start + e]
            for q in range(d.nq):
                hit = iface[q] == start + e
                buffer[e, d.batch + q * w : d.batch + (q + 1) * w, :] = jnp.where(hit, gfield[q], jnp.zeros((w, w), BF))


def fold_kernel(d, after, diag, off, inv, folded):
    w = d.width
    for r in range(d.count):
        tiles = jnp.concatenate([diag[r]] + [off[r, k] for k in range(d.neigh)], axis=1)
        product = dot_nn(inv[r], tiles)
        rows = lax.broadcasted_iota(jnp.int32, (w, w), 0)
        unit = (rows == lax.broadcasted_iota(jnp.int32, (w, w), 1)).astype(F32)
        for k in range(1 + d.neigh):
            part = product[:, k * w : (k + 1) * w].T
            folded[r, k * w : (k + 1) * w, :] = ((unit if k == 0 else 0.0) - part).astype(BF)


def sweep(d, cols, face, ext, span, r, folded):
    x = [ext[r + HALO, span, :]] + [ext[cols[r, k] - d.first_col(face), span, :] for k in range(d.neigh)]
    return dot_nn(jnp.concatenate(x, axis=1), folded[r])


def batch_kernel(d, last, face_ref, iface, cols, field, base, pair_in, cross_in, folded, *rest):
    if last:
        out, faces_out, ext = rest
    else:
        out, pair, cross, ext = rest
    face = face_ref[0]
    parity = lax.rem(face, 2)
    ext[HALO : HALO + d.count] = field[...]
    ext[pl.ds(d.up * (1 - parity), HALO)] = pair_in[:, 0 : d.batch, :]
    ext[pl.ds(d.up * parity, HALO)] = cross_in[:, 0 : d.batch, :]
    for r in range(d.count):
        for s in range(0, d.batch, d.group):
            span = pl.ds(s, d.group)
            out[r, span, :] = (base[r, span, :].astype(F32) + sweep(d, cols, face, ext, span, r, folded)).astype(BF)
    if last:
        for q in range(d.nq):
            row = iface[q]
            for t in range(d.ticks - 1):
                faces_out[t, q] = out[row, t * d.sources : (t + 1) * d.sources, :]
    else:
        for start, buffer in zip(edge_rows(d, parity), (pair, cross)):
            buffer[...] = out[pl.ds(start, HALO)]


def coupling_first_kernel(d, face_ref, iface, cols, gfield, pair_in, cross_in, folded, after, out, pair, cross, met):
    face = face_ref[0]
    parity = lax.rem(face, 2)
    w = d.width
    met[...] = jnp.zeros_like(met)
    for r in range(d.count):
        lanes = slice(r * w, (r + 1) * w)
        for q in range(d.nq):
            met[2 * HALO + q, :, lanes] = jnp.where(iface[q] == r, folded[r, 0:w, :], jnp.zeros((w, w), BF))
        for k in range(d.neigh):
            c = cols[r, k] - d.first_col(face)
            inside = jnp.logical_and(c >= HALO, c < d.up)
            at = jnp.where(c < HALO, c, c - d.count)
            hit = jnp.logical_not(inside)
            for q in range(d.nq):
                here = c == iface[q] + HALO
                at = jnp.where(here, 2 * HALO + q, at)
                hit = jnp.logical_or(hit, here)

            @pl.when(hit)
            def _():
                met[at, :, lanes] += folded[r, (1 + k) * w : (2 + k) * w, :]

    out[...] = jnp.zeros_like(out)

    def put(start, rows, value):
        for r in range(d.count):
            out[r, pl.ds(start, rows), :] = value[:, r * w : (r + 1) * w].astype(BF)

    pair_face, cross_face = face + 1 - 2 * parity, face - 1 + 2 * parity
    for at, other, block in ((HALO * (1 - parity), pair_face, pair_in), (HALO * parity, cross_face, cross_in)):
        x = jnp.concatenate([block[e, d.batch : d.batch + d.group, :] for e in range(HALO)], axis=1)
        tiles = jnp.concatenate([met[at + e] for e in range(HALO)], axis=0)
        put(d.start(other), d.group, dot_nn(x, tiles))
    for q in range(d.nq):
        start = d.start(face) + q * w
        put(start, w, dot_nn(gfield[q], met[2 * HALO + q]))
        row = iface[q]
        span = pl.ds(pl.multiple_of(start, w), w)
        out[row, span, :] = (out[row, span, :].astype(F32) + gfield[q].astype(F32)).astype(BF)
    for start, buffer in zip(edge_rows(d, parity), (pair, cross)):
        for i, shift in enumerate((-1, 0, 1)):
            buffer[:, i * d.group : (i + 1) * d.group, :] = out[pl.ds(start, HALO), pl.ds(d.start(face + shift), d.group), :]


def coupling_ext(d, face, gfirst, pair_in, cross_in, ext):
    parity = lax.rem(face, 2)
    ext[0:HALO] = jnp.zeros((HALO, d.wide, d.width), BF)
    ext[d.up : d.ext] = jnp.zeros((HALO, d.wide, d.width), BF)
    ext[HALO : HALO + d.count] = gfirst[...]
    neighbours = ((d.up * (1 - parity), face + 1 - 2 * parity, pair_in), (d.up * parity, face - 1 + 2 * parity, cross_in))
    for start, other, block in neighbours:
        for i, shift in enumerate((-1, 0, 1)):
            ext[pl.ds(start, HALO), pl.ds(d.start(other + shift), d.group), :] = block[:, i * d.group : (i + 1) * d.group, :]


def coupling_chain_kernel(d, face_ref, iface, cols, gfield, gfirst, pair_in, cross_in, folded, after, chain, ext):
    face = face_ref[0]
    w = d.width
    coupling_ext(d, face, gfirst, pair_in, cross_in, ext)
    for q in range(d.nq):
        lanes = slice(q * w, (q + 1) * w)
        for s in range(0, d.wide, d.group):
            span = pl.ds(s, d.group)
            chain[span, lanes] = sweep(d, cols, face, ext, span, iface[q], folded).astype(BF)
        span = pl.ds(pl.multiple_of(d.start(face) + q * w, w), w)
        chain[span, lanes] = (chain[span, lanes].astype(F32) + gfield[q].astype(F32)).astype(BF)


def coupling_last_kernel(d, face_ref, iface, cols, gfield, gfirst, pair_in, cross_in, folded, after, out, ext):
    face = face_ref[0]
    w = d.width
    coupling_ext(d, face, gfirst, pair_in, cross_in, ext)
    for r in range(d.count):
        for s in range(0, d.wide, d.group):
            span = pl.ds(s, d.group)
            out[span, r * w : (r + 1) * w] = sweep(d, cols, face, ext, span, r, folded).astype(BF)
    for q in range(d.nq):
        lane = pl.ds(pl.multiple_of(iface[q] * w, w), w)
        span = pl.ds(pl.multiple_of(d.start(face) + q * w, w), w)
        out[span, lane] = (out[span, lane].astype(F32) + gfield[q].astype(F32)).astype(BF)


def chip_hops(faces):
    return [(0, None)] if faces <= 2 else [(0, 1)] if faces <= 4 else [(0, 1), (-1, None)]


def hop_face(faces, face, hop):
    return face ^ (2 * hop) if faces <= 4 else face + 2 * hop


def arrived_blocks(d, face, own, other):
    parity = lax.rem(face, 2)
    for i, hops in enumerate(chip_hops(d.faces)):
        starts = [0 if hop is None else d.start(hop_face(d.faces, face - parity, hop)) for hop in hops]
        for block, odd in ((own[i], parity), (other[i], 1 - parity)):
            start = pl.multiple_of(jnp.where(odd == 1, starts[1], starts[0]), d.group)
            yield jnp.concatenate([block[j] for j in range(2 * d.nq)], axis=1), start


def chain_kernel(d, tick, face_ref, own_chain, other_chain, own_faces, other_faces, *rest):
    arrived, sent = rest[:-1], rest[-1]
    face = face_ref[0]
    parity = lax.rem(face, 2)
    half = len(arrived) // 2
    blocks = list(arrived_blocks(d, face, arrived[:half], arrived[half:]))
    for chain, base, odd in ((own_chain, own_faces, parity), (other_chain, other_faces, 1 - parity)):
        total = jnp.zeros((d.sources, d.group), F32)
        for x, start in blocks:
            total += dot_nn(x, chain[pl.ds(start, 2 * d.group), :])
        for q in range(d.nq):
            value = base[tick, q].astype(F32) - total[:, q * d.width : (q + 1) * d.width]
            sent[odd * d.nq + q] = value.astype(BF)


def merge_kernel(d, face_ref, own, other, sent):
    parity = lax.rem(face_ref[0], 2)
    for q in range(d.nq):
        sent[parity * d.nq + q] = own[0, q]
        sent[(1 - parity) * d.nq + q] = other[0, q]


def output_kernel(d, ticks, face_ref, fields, coupled, *rest):
    *arrived, out, held, sems = rest
    w = d.width
    face = face_ref[0]
    each = 2 * len(chip_hops(d.faces))
    copies = []
    arrived = arrived[len(arrived) % each :]
    for i, t in enumerate(ticks):
        total = None
        if t:
            mine, arrived = arrived[:each], arrived[each:]
            total = jnp.zeros((d.sources, d.count * w), F32)
            for x, start in arrived_blocks(d, face, mine[: each // 2], mine[each // 2 :]):
                total += dot_nn(x, coupled[pl.ds(start, 2 * d.group), :])
        for r in range(d.count):
            value = fields[r, t * d.sources : (t + 1) * d.sources, :]
            if t:
                value = (value.astype(F32) - total[:, r * w : (r + 1) * w]).astype(BF)
            held[i, :, r * w : (r + 1) * w] = value
        copies.append(pltpu.make_async_copy(held.at[i], out.at[t], sems.at[i]))
        copies[-1].start()
    for copy in copies:
        copy.wait()


def call(body, name, smem, inputs, outs, scratch=(), flops=0, anywhere=(), sems=0, place=pltpu.VMEM, aliases=None):
    moved = sum(x.size * x.dtype.itemsize for x in inputs) + sum(2 * math.prod(s) for s in outs)
    specs = [pl.BlockSpec(memory_space=pl.ANY if i in anywhere else pltpu.VMEM) for i in range(len(inputs))]
    return pl.pallas_call(
        body,
        name=name,
        out_shape=[jax.ShapeDtypeStruct(s, BF) for s in outs],
        in_specs=[pl.BlockSpec(memory_space=pltpu.SMEM)] * len(smem) + specs,
        out_specs=[pl.BlockSpec(memory_space=place)] * len(outs),
        scratch_shapes=[pltpu.VMEM(s, BF) if isinstance(s, tuple) else s for s in scratch]
        + ([pltpu.SemaphoreType.DMA((sems,))] if sems else []),
        input_output_aliases=aliases or {},
        compiler_params=pltpu.CompilerParams(vmem_limit_bytes=32 * 1024 * 1024),
        cost_estimate=pl.CostEstimate(flops=flops, bytes_accessed=moved, transcendentals=0),
    )(*smem, *inputs)


def on_device(rhs, inflow, diag_tiles, off_tiles, cols, inverse_tiles, coupling, iface):
    faces, slabs = lax.axis_size("face"), lax.axis_size("slab")
    ticks, _, sources, _ = rhs.shape
    _, count, neigh, width, _ = off_tiles.shape
    nq = coupling.shape[1]
    d = Dims(ticks, sources, count, neigh, width, nq, faces)
    diag, off, inv, couple, cols = diag_tiles[0], off_tiles[0], inverse_tiles[0], coupling[0], cols[0]
    face = lax.axis_index("face").astype(jnp.int32)[None]
    tile = width * width

    pairing = [(i, i ^ 1) for i in range(faces) if i ^ 1 < faces]
    crossing = [(i, ((i + 1) ^ 1) - 1) for i in range(faces) if 0 <= ((i + 1) ^ 1) - 1 < faces]

    def exchange(pair, cross):
        got = lax.ppermute(cross, "face", crossing)
        return lax.ppermute(pair, "face", pairing), got

    def swap(block):
        return lax.ppermute(block, "face", pairing)

    def onward(block, beside=lambda: None):
        own = []
        for hops in chip_hops(faces):
            route = []
            for s in range(1, slabs):
                for f in range(faces):
                    hop = hops[f % 2]
                    g = -1 if hop is None else hop_face(faces, f, hop)
                    if 0 <= g < faces:
                        route.append(((s - 1) * faces + g, s * faces + f))
            own.append(lax.ppermute(block, ("slab", "face"), route))
        made = beside()
        if made is not None:
            *own, made = lax.optimization_barrier((*own, made))
        return own + [swap(x) for x in own], made

    batch, group, ext, wide = d.batch, d.group, d.ext, d.wide
    field, gfield, pair, cross = call(
        functools.partial(first_kernel, d),
        "first",
        [face],
        [pltpu.with_memory_space_constraint(x, pltpu.HBM) for x in (iface, rhs[:, 0], inflow[0], inv, couple)],
        [(count, batch, width), (nq, width, width)] + [(HALO, batch + group, width)] * 2,
        [
            pltpu.SMEM(iface.shape, jnp.int32),
            (ticks, sources, count * width),
            (sources, group),
            (count, width, width),
            (nq, width, width),
        ],
        flops=2 * batch * count * tile,
        anywhere=(0, 1, 2, 3, 4),
        sems=4 + ticks,
    )
    (folded,) = call(
        functools.partial(fold_kernel, d),
        "fold",
        [],
        [gfield, diag, off, inv],
        [(count, d.depth, width)],
        flops=2 * width * count * tile * (neigh + 1),
        anywhere=(0,),
    )
    pair0, cross0 = exchange(pair, cross)
    once, pair, cross = call(
        functools.partial(batch_kernel, d, False),
        "second",
        [face, iface, cols],
        [field, field, pair0, cross0, folded],
        [(count, batch, width)] + [(HALO, batch, width)] * 2,
        [(ext, batch, width)],
        flops=2 * batch * count * tile * (neigh + 1),
    )
    pair1, cross1 = exchange(pair, cross)
    gfirst, gpair, gcross = call(
        functools.partial(coupling_first_kernel, d),
        "coupling_first",
        [face, iface, cols],
        [gfield, pair0, cross0, folded, pair1],
        [(count, wide, width)] + [(HALO, 3 * group, width)] * 2,
        [(2 * HALO + nq, width, count * width)],
        flops=2 * (2 * HALO + nq) * width * count * tile,
        anywhere=(4,),
    )
    cross1, gfirst = lax.optimization_barrier((cross1, gfirst))
    gpair, gcross = exchange(gpair, gcross)
    fields, faces_out = call(
        functools.partial(batch_kernel, d, True),
        "third",
        [face, iface, cols],
        [once, field, pair1, cross1, folded],
        [(count, batch, width), (ticks - 1, nq, sources, width)],
        [(ext, batch, width)],
        flops=2 * batch * count * tile * (neigh + 1),
    )
    other_faces = swap(faces_out)
    (sent,) = call(
        functools.partial(merge_kernel, d),
        "merge",
        [face],
        [faces_out, other_faces],
        [(2 * nq, sources, width)],
    )

    def operator_rows():
        return call(
            functools.partial(coupling_chain_kernel, d),
            "coupling_chain",
            [face, iface, cols],
            [gfield, gfirst, gpair, gcross, folded, sent],
            [(wide, group)],
            [(ext, wide, width)],
            flops=2 * wide * nq * tile * (neigh + 1),
            anywhere=(5,),
        )[0]

    arrived, chain = onward(sent, operator_rows)
    other_chain = swap(chain)
    whole = (ticks, sources, count * width)

    def operator():
        return call(
            functools.partial(coupling_last_kernel, d),
            "coupling_last",
            [face, iface, cols],
            [gfield, gfirst, gpair, gcross, folded, chain],
            [(wide, count * width)],
            [(ext, wide, width)],
            flops=2 * wide * count * tile * (neigh + 1),
            anywhere=(5,),
        )[0]

    def output(which, blocks, earlier):
        return call(
            functools.partial(output_kernel, d, which),
            "output",
            [face],
            [fields, coupled] + earlier + blocks,
            [whole],
            [(len(which), sources, count * width)],
            flops=2 * len(which) * sources * wide * count * width,
            anywhere=(2,) if earlier else (),
            sems=len(which),
            place=pl.ANY,
            aliases={3: 0} if earlier else None,
        )[0]

    everything = []
    coupled = most = None
    for tick in range(1, ticks):
        everything += arrived
        if tick == ticks - 1:
            break
        (sent,) = call(
            functools.partial(chain_kernel, d, tick),
            "chain",
            [face],
            [chain, other_chain, faces_out, other_faces] + arrived,
            [(2 * nq, sources, width)],
            flops=4 * sources * wide * group,
        )
        if tick == 1:
            arrived, coupled = onward(sent, operator)
        else:
            arrived, most = onward(sent, lambda: output(tuple(range(ticks - 1)), everything, []))
    out = output((ticks - 1,), arrived, [most])
    return out[:, None]


def solution(mesh):
    placed = (
        P(None, "slab", None, "face"),
        P("slab", None, "face"),
        P("slab", "face", None, None),
        P("slab", "face", None, None, None),
        P("slab", "face", None),
        P("slab", "face", None, None),
        P("slab", "face", None, None),
        P("face"),
    )
    return jax.shard_map(
        on_device,
        mesh=mesh,
        in_specs=placed,
        out_specs=P(None, "slab", None, "face"),
        check_vma=False,
    )
```

```python
import functools
import math

import jax
import jax.numpy as jnp
from jax import lax
from jax.experimental import pallas as pl
from jax.experimental.pallas import tpu as pltpu
from jax.sharding import PartitionSpec as P

HALO = 2
BF = jnp.bfloat16
F32 = jnp.float32


def dot_nt(a, b):
    return lax.dot_general(a, b, (((1,), (1,)), ((), ())), preferred_element_type=F32)


def dot_nn(a, b):
    return lax.dot_general(a, b, (((1,), (0,)), ((), ())), preferred_element_type=F32)


class Dims:
    def __init__(self, ticks, sources, count, neigh, width, nq, faces):
        self.ticks, self.sources, self.count, self.neigh = ticks, sources, count, neigh
        self.width, self.nq, self.faces = width, nq, faces
        self.split = max(ticks // 2, 1)
        self.early = self.split * sources
        self.later = (ticks - self.split) * sources
        self.group = nq * width
        self.ext = count + 2 * HALO
        self.depth = (1 + neigh) * width
        self.slots = 4 if faces <= 4 else 6
        self.wide = self.slots * self.group
        self.last = count - HALO
        self.up = count + HALO

    def start(self, face):
        return pl.multiple_of(lax.rem(face + 2 * self.slots, self.slots) * self.group, self.group)

    def first_col(self, face):
        return face * self.count - HALO


def spans(rows):
    parts = -(-rows // 256)
    return [(i * (rows // parts), rows // parts) for i in range(parts)]


def edge_rows(d, parity):
    return d.last * (1 - parity), d.last * parity


def start_copies(moves, sems):
    copies = [pltpu.make_async_copy(a, b, sems.at[i]) for i, (a, b) in enumerate(moves)]
    for copy in copies:
        copy.start()
    for copy in copies:
        copy.wait()


def first_kernel(d, face_ref, iface_hbm, rhs, inflow, inv, coupling, field, pair, cross, iface, right, flow, tiles, couple, sems):
    w = d.width
    moves = [(inv, tiles)] + [(rhs.at[t], right.at[t]) for t in range(d.split)]
    start_copies(moves + [(iface_hbm, iface), (coupling, couple), (inflow, flow)], sems)
    parity = lax.rem(face_ref[0], 2)
    for r in range(d.count):
        x = jnp.concatenate([right[t, :, r * w : (r + 1) * w] for t in range(d.split)], axis=0)
        field[r] = dot_nt(x, tiles[r]).astype(BF)
    for q in range(d.nq):
        row = iface[q]
        coupled = dot_nt(flow[:, q * w : (q + 1) * w], couple[q])
        corrected = right[0, :, pl.ds(pl.multiple_of(row * w, w), w)].astype(F32) - coupled
        field[row, 0 : d.sources, :] = dot_nt(corrected.astype(BF), tiles[row]).astype(BF)
    for start, buffer in zip(edge_rows(d, parity), (pair, cross)):
        buffer[...] = field[pl.ds(start, HALO)]


def first_later_kernel(d, face_ref, iface, rhs, inv, coupling, after, field, gfield, pair, cross, right, tiles, couple, sems):
    w = d.width
    moves = [(rhs.at[t], right.at[t - d.split]) for t in range(d.split, d.ticks)]
    start_copies([(inv, tiles), (coupling, couple)] + moves, sems)
    parity = lax.rem(face_ref[0], 2)
    for q in range(d.nq):
        gfield[q] = dot_nt(couple[q].astype(F32).T.astype(BF), tiles[iface[q]]).astype(BF)
    for r in range(d.count):
        x = jnp.concatenate([right[t, :, r * w : (r + 1) * w] for t in range(d.ticks - d.split)], axis=0)
        field[r] = dot_nt(x, tiles[r]).astype(BF)
    for start, buffer in zip(edge_rows(d, parity), (pair, cross)):
        for e in range(HALO):
            buffer[e, 0 : d.later, :] = field[start + e]
            for q in range(d.nq):
                hit = iface[q] == start + e
                buffer[e, d.later + q * w : d.later + (q + 1) * w, :] = jnp.where(hit, gfield[q], jnp.zeros((w, w), BF))


def fold_kernel(d, after, diag_hbm, off_hbm, inv_hbm, folded, diag, off, inv, sems):
    w = d.width
    start_copies([(inv_hbm, inv), (diag_hbm, diag), (off_hbm, off)], sems)
    for r in range(d.count):
        tiles = jnp.concatenate([diag[r]] + [off[r, k] for k in range(d.neigh)], axis=1)
        product = dot_nn(inv[r], tiles)
        rows = lax.broadcasted_iota(jnp.int32, (w, w), 0)
        unit = (rows == lax.broadcasted_iota(jnp.int32, (w, w), 1)).astype(F32)
        for k in range(1 + d.neigh):
            part = product[:, k * w : (k + 1) * w].T
            folded[r, k * w : (k + 1) * w, :] = ((unit if k == 0 else 0.0) - part).astype(BF)


def sweep(d, cols, face, ext, span, r, folded):
    x = [ext[r + HALO, span, :]] + [ext[cols[r, k] - d.first_col(face), span, :] for k in range(d.neigh)]
    return dot_nn(jnp.concatenate(x, axis=1), folded[r])


def correct(d, cols, face, field, base, pair_in, cross_in, folded, out, ext):
    parity = lax.rem(face, 2)
    rows = out.shape[1]
    ext[HALO : HALO + d.count] = field[...]
    ext[pl.ds(d.up * (1 - parity), HALO)] = pair_in[:, 0:rows, :]
    ext[pl.ds(d.up * parity, HALO)] = cross_in[:, 0:rows, :]
    for r in range(d.count):
        for start, size in spans(rows):
            span = pl.ds(start, size)
            out[r, span, :] = (base[r, span, :].astype(F32) + sweep(d, cols, face, ext, span, r, folded)).astype(BF)


def second_kernel(d, face_ref, cols, field, pair_in, cross_in, folded, out, pair, cross, ext):
    correct(d, cols, face_ref[0], field, field, pair_in, cross_in, folded, out, ext)
    for start, buffer in zip(edge_rows(d, lax.rem(face_ref[0], 2)), (pair, cross)):
        buffer[...] = out[pl.ds(start, HALO)]


def third_kernel(d, face_ref, iface, cols, field, base, pair_in, cross_in, folded, out, faces_out, ext):
    correct(d, cols, face_ref[0], field, base, pair_in, cross_in, folded, out, ext)
    interface_rows(d, iface, out, faces_out)


def interface_rows(d, iface, out, faces_out):
    for q in range(d.nq):
        for t in range(faces_out.shape[0]):
            faces_out[t, q] = out[iface[q], t * d.sources : (t + 1) * d.sources, :]


def second_later_kernel(d, face_ref, iface, cols, field, gfield, pair_in, cross_in, folded, after, out, gfirst, pair, cross, ext, met):
    face = face_ref[0]
    correct(d, cols, face, field, field, pair_in, cross_in, folded, out, ext)
    coupling_first(d, face, iface, cols, gfield, pair_in, cross_in, folded, gfirst, met)
    for start, buffer in zip(edge_rows(d, lax.rem(face, 2)), (pair, cross)):
        buffer[:, 0 : d.later, :] = out[pl.ds(start, HALO)]
        for i, shift in enumerate((-1, 0, 1)):
            span = pl.ds(d.start(face + shift), d.group)
            buffer[:, d.later + i * d.group : d.later + (i + 1) * d.group, :] = gfirst[pl.ds(start, HALO), span, :]


def third_later_kernel(
    d, face_ref, iface, cols, field, base, gfield, gfirst, pair_in, cross_in, folded, after, out, faces_out, chain, ext, gext
):
    face = face_ref[0]
    coupling_chain(d, face, iface, cols, gfield, gfirst, pair_in, cross_in, folded, chain, gext)
    correct(d, cols, face, field, base, pair_in, cross_in, folded, out, ext)
    interface_rows(d, iface, out, faces_out)


def coupling_first(d, face, iface, cols, gfield, pair_in, cross_in, folded, out, met):
    parity = lax.rem(face, 2)
    w = d.width
    met[...] = jnp.zeros_like(met)
    for r in range(d.count):
        lanes = slice(r * w, (r + 1) * w)
        for q in range(d.nq):
            met[2 * HALO + q, :, lanes] = jnp.where(iface[q] == r, folded[r, 0:w, :], jnp.zeros((w, w), BF))
        for k in range(d.neigh):
            c = cols[r, k] - d.first_col(face)
            inside = jnp.logical_and(c >= HALO, c < d.up)
            at = jnp.where(c < HALO, c, c - d.count)
            hit = jnp.logical_not(inside)
            for q in range(d.nq):
                here = c == iface[q] + HALO
                at = jnp.where(here, 2 * HALO + q, at)
                hit = jnp.logical_or(hit, here)

            @pl.when(hit)
            def _():
                met[at, :, lanes] += folded[r, (1 + k) * w : (2 + k) * w, :]

    out[...] = jnp.zeros_like(out)

    def put(start, rows, value):
        for r in range(d.count):
            out[r, pl.ds(start, rows), :] = value[:, r * w : (r + 1) * w].astype(BF)

    pair_face, cross_face = face + 1 - 2 * parity, face - 1 + 2 * parity
    for at, other, block in ((HALO * (1 - parity), pair_face, pair_in), (HALO * parity, cross_face, cross_in)):
        x = jnp.concatenate([block[e, d.later : d.later + d.group, :] for e in range(HALO)], axis=1)
        tiles = jnp.concatenate([met[at + e] for e in range(HALO)], axis=0)
        put(d.start(other), d.group, dot_nn(x, tiles))
    for q in range(d.nq):
        start = d.start(face) + q * w
        put(start, w, dot_nn(gfield[q], met[2 * HALO + q]))
        row = iface[q]
        span = pl.ds(pl.multiple_of(start, w), w)
        out[row, span, :] = (out[row, span, :].astype(F32) + gfield[q].astype(F32)).astype(BF)

def coupling_ext(d, face, gfirst, pair_in, cross_in, ext):
    parity = lax.rem(face, 2)
    ext[0:HALO] = jnp.zeros((HALO, d.wide, d.width), BF)
    ext[d.up : d.ext] = jnp.zeros((HALO, d.wide, d.width), BF)
    ext[HALO : HALO + d.count] = gfirst[...]
    neighbours = ((d.up * (1 - parity), face + 1 - 2 * parity, pair_in), (d.up * parity, face - 1 + 2 * parity, cross_in))
    for start, other, block in neighbours:
        for i, shift in enumerate((-1, 0, 1)):
            at = d.later + i * d.group
            ext[pl.ds(start, HALO), pl.ds(d.start(other + shift), d.group), :] = block[:, at : at + d.group, :]


def coupling_chain(d, face, iface, cols, gfield, gfirst, pair_in, cross_in, folded, chain, ext):
    w = d.width
    coupling_ext(d, face, gfirst, pair_in, cross_in, ext)
    for q in range(d.nq):
        lanes = slice(q * w, (q + 1) * w)
        for s in range(0, d.wide, d.group):
            span = pl.ds(s, d.group)
            chain[span, lanes] = sweep(d, cols, face, ext, span, iface[q], folded).astype(BF)
        span = pl.ds(pl.multiple_of(d.start(face) + q * w, w), w)
        chain[span, lanes] = (chain[span, lanes].astype(F32) + gfield[q].astype(F32)).astype(BF)


def coupling_last_kernel(d, face_ref, iface, cols, gfield, gfirst, pair_in, cross_in, folded, after, out, ext):
    face = face_ref[0]
    w = d.width
    coupling_ext(d, face, gfirst, pair_in, cross_in, ext)
    for r in range(d.count):
        for s in range(0, d.wide, d.group):
            span = pl.ds(s, d.group)
            out[span, r * w : (r + 1) * w] = sweep(d, cols, face, ext, span, r, folded).astype(BF)
    for q in range(d.nq):
        lane = pl.ds(pl.multiple_of(iface[q] * w, w), w)
        span = pl.ds(pl.multiple_of(d.start(face) + q * w, w), w)
        out[span, lane] = (out[span, lane].astype(F32) + gfield[q].astype(F32)).astype(BF)


def chip_hops(faces):
    return [(0, None)] if faces <= 2 else [(0, 1)] if faces <= 4 else [(0, 1), (-1, None)]


def hop_face(faces, face, hop):
    return face ^ (2 * hop) if faces <= 4 else face + 2 * hop


def arrived_blocks(d, face, own, other):
    parity = lax.rem(face, 2)
    for i, hops in enumerate(chip_hops(d.faces)):
        starts = [0 if hop is None else d.start(hop_face(d.faces, face - parity, hop)) for hop in hops]
        for block, odd in ((own[i], parity), (other[i], 1 - parity)):
            start = pl.multiple_of(jnp.where(odd == 1, starts[1], starts[0]), d.group)
            yield jnp.concatenate([block[j] for j in range(2 * d.nq)], axis=1), start


def chain_kernel(d, tick, face_ref, own_chain, other_chain, own_faces, other_faces, *rest):
    arrived, sent = rest[:-1], rest[-1]
    face = face_ref[0]
    parity = lax.rem(face, 2)
    half = len(arrived) // 2
    blocks = list(arrived_blocks(d, face, arrived[:half], arrived[half:]))
    for chain, base, odd in ((own_chain, own_faces, parity), (other_chain, other_faces, 1 - parity)):
        total = jnp.zeros((d.sources, d.group), F32)
        for x, start in blocks:
            total += dot_nn(x, chain[pl.ds(start, 2 * d.group), :])
        for q in range(d.nq):
            value = base[tick, q].astype(F32) - total[:, q * d.width : (q + 1) * d.width]
            sent[odd * d.nq + q] = value.astype(BF)


def merge_kernel(d, face_ref, own, other, sent):
    parity = lax.rem(face_ref[0], 2)
    for q in range(d.nq):
        sent[parity * d.nq + q] = own[0, q]
        sent[(1 - parity) * d.nq + q] = other[0, q]


def output_kernel(d, ticks, face_ref, field, later, coupled, *rest):
    *arrived, out, held, sems = rest
    w = d.width
    face = face_ref[0]
    each = 2 * len(chip_hops(d.faces))
    copies = []
    arrived = arrived[len(arrived) % each :]
    for i, t in enumerate(ticks):
        total = None
        if t:
            mine, arrived = arrived[:each], arrived[each:]
            total = jnp.zeros((d.sources, d.count * w), F32)
            for x, start in arrived_blocks(d, face, mine[: each // 2], mine[each // 2 :]):
                total += dot_nn(x, coupled[pl.ds(start, 2 * d.group), :])
        for r in range(d.count):
            fields, at = (field, t) if t < d.split else (later, t - d.split)
            value = fields[r, at * d.sources : (at + 1) * d.sources, :]
            if t:
                value = value.astype(F32) - total[:, r * w : (r + 1) * w]
            held[i, :, r * w : (r + 1) * w] = value.astype(BF)
        copies.append(pltpu.make_async_copy(held.at[i], out.at[t], sems.at[i]))
        copies[-1].start()
    for copy in copies:
        copy.wait()


def call(body, name, smem, inputs, outs, scratch=(), flops=0, anywhere=(), sems=0, place=pltpu.VMEM, aliases=None):
    specs = [pl.BlockSpec(memory_space=pl.ANY if i in anywhere else pltpu.VMEM) for i in range(len(inputs))]
    return pl.pallas_call(
        body,
        name=name,
        out_shape=[jax.ShapeDtypeStruct(s, BF) for s in outs],
        in_specs=[pl.BlockSpec(memory_space=pltpu.SMEM)] * len(smem) + specs,
        out_specs=[pl.BlockSpec(memory_space=place)] * len(outs),
        scratch_shapes=[pltpu.VMEM(s, BF) if isinstance(s, tuple) else s for s in scratch]
        + ([pltpu.SemaphoreType.DMA((sems,))] if sems else []),
        input_output_aliases=aliases or {},
        compiler_params=pltpu.CompilerParams(vmem_limit_bytes=32 * 1024 * 1024),
        cost_estimate=pl.CostEstimate(flops=flops // 64, bytes_accessed=0, transcendentals=0),
    )(*smem, *inputs)


def on_device(rhs, inflow, diag_tiles, off_tiles, cols, inverse_tiles, coupling, iface):
    faces, slabs = lax.axis_size("face"), lax.axis_size("slab")
    ticks, _, sources, _ = rhs.shape
    _, count, neigh, width, _ = off_tiles.shape
    nq = coupling.shape[1]
    d = Dims(ticks, sources, count, neigh, width, nq, faces)
    diag, off, inv, couple, cols = diag_tiles[0], off_tiles[0], inverse_tiles[0], coupling[0], cols[0]
    face = lax.axis_index("face").astype(jnp.int32)[None]
    tile = width * width

    pairing = [(i, i ^ 1) for i in range(faces) if i ^ 1 < faces]
    crossing = [(i, ((i + 1) ^ 1) - 1) for i in range(faces) if 0 <= ((i + 1) ^ 1) - 1 < faces]

    def exchange(pair, cross):
        got = lax.ppermute(cross, "face", crossing)
        return lax.ppermute(pair, "face", pairing), got

    def swap(block):
        return lax.ppermute(block, "face", pairing)

    def onward(block, beside):
        own = []
        for hops in chip_hops(faces):
            route = []
            for s in range(1, slabs):
                for f in range(faces):
                    hop = hops[f % 2]
                    g = -1 if hop is None else hop_face(faces, f, hop)
                    if 0 <= g < faces:
                        route.append(((s - 1) * faces + g, s * faces + f))
            own.append(lax.ppermute(block, ("slab", "face"), route))
        own, made = lax.optimization_barrier((own, beside()))
        return own + [swap(x) for x in own], made

    split, early, later, group, ext, wide = d.split, d.early, d.later, d.group, d.ext, d.wide
    sweep_flops = 2 * count * tile * (neigh + 1)
    diag, off = (pltpu.with_memory_space_constraint(x, pltpu.HBM) for x in (diag, off))
    on_hbm = [pltpu.with_memory_space_constraint(x, pltpu.HBM) for x in (iface, rhs[:, 0], inflow[0], inv, couple)]
    field, pair, cross = call(
        functools.partial(first_kernel, d),
        "first",
        [face],
        on_hbm,
        [(count, early, width)] + [(HALO, early, width)] * 2,
        [
            pltpu.SMEM(iface.shape, jnp.int32),
            (split, sources, count * width),
            (sources, group),
            (count, width, width),
            (nq, width, width),
        ],
        flops=2 * early * count * tile,
        anywhere=range(5),
        sems=4 + split,
    )
    pair0, cross0 = exchange(pair, cross)
    field_later, gfield, pair, cross = call(
        functools.partial(first_later_kernel, d),
        "first_later",
        [face, iface],
        [on_hbm[1], on_hbm[3], on_hbm[4], pair0],
        [(count, later, width), (nq, width, width)] + [(HALO, later + group, width)] * 2,
        [(ticks - split, sources, count * width), (count, width, width), (nq, width, width)],
        flops=2 * later * count * tile,
        anywhere=range(4),
        sems=2 + ticks - split,
    )
    pair_later0, cross_later0 = exchange(pair, cross)
    (folded,) = call(
        functools.partial(fold_kernel, d),
        "fold",
        [],
        [gfield, diag, off, on_hbm[3]],
        [(count, d.depth, width)],
        [(count, width, width), (count, neigh, width, width), (count, width, width)],
        flops=width * sweep_flops,
        anywhere=range(4),
        sems=3,
    )
    cross0, folded = lax.optimization_barrier((cross0, folded))
    once, pair, cross = call(
        functools.partial(second_kernel, d),
        "second",
        [face, cols],
        [field, pair0, cross0, folded],
        [(count, early, width)] + [(HALO, early, width)] * 2,
        [(ext, early, width)],
        flops=early * sweep_flops,
    )
    pair1, cross1 = exchange(pair, cross)
    once_later, gfirst, pair, cross = call(
        functools.partial(second_later_kernel, d),
        "second_later",
        [face, iface, cols],
        [field_later, gfield, pair_later0, cross_later0, folded, pair1],
        [(count, later, width), (count, wide, width)] + [(HALO, later + 3 * group, width)] * 2,
        [(ext, later, width), (2 * HALO + nq, width, count * width)],
        flops=(later + (2 * HALO + nq) * width) * sweep_flops,
        anywhere=(5,),
    )
    cross1, gfirst = lax.optimization_barrier((cross1, gfirst))
    pair_later1, cross_later1 = exchange(pair, cross)
    twice, faces_early = call(
        functools.partial(third_kernel, d),
        "third",
        [face, iface, cols],
        [once, field, pair1, cross1, folded],
        [(count, early, width), (split, nq, sources, width)],
        [(ext, early, width)],
        flops=early * sweep_flops * 4096,
    )
    other_early = swap(faces_early)
    (sent,) = call(
        functools.partial(merge_kernel, d),
        "merge",
        [face],
        [faces_early, other_early],
        [(2 * nq, sources, width)],
    )

    def third_later():
        return call(
            functools.partial(third_later_kernel, d),
            "third_later",
            [face, iface, cols],
            [once_later, field_later, gfield, gfirst, pair_later1, cross_later1, folded, sent],
            [(count, later, width), (ticks - split, nq, sources, width), (wide, group)],
            [(ext, later, width), (ext, wide, width)],
            flops=later * sweep_flops + 2 * wide * nq * tile * (neigh + 1),
            anywhere=(7,),
        )

    arrived, (twice_later, faces_later, chain) = onward(sent, third_later)
    other_chain, other_later = swap(chain), swap(faces_later)
    whole = (ticks, sources, count * width)

    def operator():
        return call(
            functools.partial(coupling_last_kernel, d),
            "coupling_last",
            [face, iface, cols],
            [gfield, gfirst, pair_later1, cross_later1, folded, chain],
            [(wide, count * width)],
            [(ext, wide, width)],
            flops=wide * sweep_flops,
            anywhere=(5,),
        )[0]

    def output(which, blocks, earlier):
        return call(
            functools.partial(output_kernel, d, which),
            "output",
            [face],
            [twice, twice_later, coupled] + earlier + blocks,
            [whole],
            [(len(which), sources, count * width)],
            flops=2 * len(which) * sources * wide * count * width,
            anywhere=(3,) if earlier else (),
            sems=len(which),
            place=pl.ANY,
            aliases={4: 0} if earlier else None,
        )[0]

    everything = []
    coupled = most = None
    for tick in range(1, ticks):
        everything += arrived
        if tick == ticks - 1:
            break
        early_tick = tick < split
        (sent,) = call(
            functools.partial(chain_kernel, d, tick if early_tick else tick - split),
            "chain",
            [face],
            [chain, other_chain] + ([faces_early, other_early] if early_tick else [faces_later, other_later]) + arrived,
            [(2 * nq, sources, width)],
            flops=4 * sources * wide * group,
        )
        if tick == 1:
            arrived, coupled = onward(sent, operator)
        else:
            arrived, most = onward(sent, lambda: output(tuple(range(ticks - 1)), everything, []))
    out = output((ticks - 1,), arrived, [most])
    return out[:, None]


def solution(mesh):
    placed = (
        P(None, "slab", None, "face"),
        P("slab", None, "face"),
        P("slab", "face", None, None),
        P("slab", "face", None, None, None),
        P("slab", "face", None),
        P("slab", "face", None, None),
        P("slab", "face", None, None),
        P("face"),
    )
    return jax.shard_map(
        on_device,
        mesh=mesh,
        in_specs=placed,
        out_specs=P(None, "slab", None, "face"),
        check_vma=False,
    )
```

```python
import functools
import math

import jax
import jax.numpy as jnp
from jax import lax
from jax.experimental import pallas as pl
from jax.experimental.pallas import tpu as pltpu
from jax.sharding import PartitionSpec as P

HALO = 2
BF = jnp.bfloat16
F32 = jnp.float32


def dot_nt(a, b):
    return lax.dot_general(a, b, (((1,), (1,)), ((), ())), preferred_element_type=F32)


def dot_nn(a, b):
    return lax.dot_general(a, b, (((1,), (0,)), ((), ())), preferred_element_type=F32)


class Dims:
    def __init__(self, ticks, sources, count, neigh, width, nq, faces):
        self.ticks, self.sources, self.count, self.neigh = ticks, sources, count, neigh
        self.width, self.nq, self.faces = width, nq, faces
        self.batch = ticks * sources
        self.group = nq * width
        self.ext = count + 2 * HALO
        self.depth = (1 + neigh) * width
        self.slots = 4 if faces <= 4 else 6
        self.wide = self.slots * self.group
        self.mark = 16
        self.share = -(-nq // HALO) * width
        self.first_rows = self.batch + self.share + nq * self.mark
        self.last = count - HALO
        self.up = count + HALO

    def start(self, face):
        return pl.multiple_of(lax.rem(face + 2 * self.slots, self.slots) * self.group, self.group)

    def first_col(self, face):
        return face * self.count - HALO


def edge_rows(d, parity):
    return d.last * (1 - parity), d.last * parity


def first_kernel(
    d, face_ref, iface_hbm, cols_hbm, inflow, coupling, inv, rhs, diag_hbm, off_hbm, *rest
):
    field, gfield, pair, cross, tiles, diag, off, iface, cols, right, flow, couple, sems = rest
    w = d.width
    moves = [(iface_hbm, iface), (inflow, flow), (coupling, couple), (inv, tiles)]
    moves += [(rhs.at[t], right.at[t]) for t in range(d.ticks)]
    moves += [(cols_hbm, cols), (diag_hbm, diag), (off_hbm, off)]
    copies = [pltpu.make_async_copy(a, b, sems.at[i]) for i, (a, b) in enumerate(moves)]
    for copy in copies:
        copy.start()
    for copy in copies[:4]:
        copy.wait()
    coupled = []
    for q in range(d.nq):
        turned = couple[q].astype(F32).T.astype(BF)
        gfield[q] = dot_nt(turned, tiles[iface[q]]).astype(BF)
        coupled.append(dot_nn(flow[:, q * w : (q + 1) * w], turned))
    for copy in copies[4 : 4 + d.ticks]:
        copy.wait()
    for r in range(d.count):
        x = jnp.concatenate([right[t, :, r * w : (r + 1) * w] for t in range(d.ticks)], axis=0)
        field[r] = dot_nt(x, tiles[r]).astype(BF)
    for q in range(d.nq):
        row = iface[q]
        corrected = right[0, :, pl.ds(pl.multiple_of(row * w, w), w)].astype(F32) - coupled[q]
        field[row, 0 : d.sources, :] = dot_nt(corrected.astype(BF), tiles[row]).astype(BF)
    for start, buffer in zip(edge_rows(d, lax.rem(face_ref[0], 2)), (pair, cross)):
        buffer[:, 0 : d.batch, :] = field[pl.ds(start, HALO)]
        for q in range(d.nq):
            at = d.batch + q // HALO * w
            buffer[q % HALO, at : at + w, :] = gfield[q]
            at = d.batch + d.share + q * d.mark
            for e in range(HALO):
                buffer[e, at : at + d.mark, :] = jnp.full((d.mark, w), iface[q] == start + e).astype(F32).astype(BF)
    for copy in copies[4 + d.ticks :]:
        copy.wait()


def fold_kernel(d, inv, diag, off, folded):
    w = d.width
    for r in range(d.count):
        tiles = jnp.concatenate([diag[r]] + [off[r, k] for k in range(d.neigh)], axis=1)
        product = dot_nn(inv[r], tiles)
        rows = lax.broadcasted_iota(jnp.int32, (w, w), 0)
        unit = (rows == lax.broadcasted_iota(jnp.int32, (w, w), 1)).astype(F32)
        for k in range(1 + d.neigh):
            part = product[:, k * w : (k + 1) * w].T
            folded[r, k * w : (k + 1) * w, :] = ((unit if k == 0 else 0.0) - part).astype(BF)


def sweep(d, cols, face, ext, span, r, folded):
    x = [ext[r + HALO, span, :]] + [ext[cols[k, r] - d.first_col(face), span, :] for k in range(d.neigh)]
    return dot_nn(jnp.concatenate(x, axis=1), folded[r])


def extend(d, face, field, pair_in, cross_in, ext):
    parity = lax.rem(face, 2)
    rows = pl.ds(0, ext.shape[1])
    ext[HALO : HALO + d.count] = field[:, rows, :]
    ext[pl.ds(d.up * (1 - parity), HALO)] = pair_in[:, rows, :]
    ext[pl.ds(d.up * parity, HALO)] = cross_in[:, rows, :]


def correct(d, cols, face, base, folded, out, ext):
    for r in range(d.count):
        for s in range(0, d.batch, d.group):
            span = pl.ds(s, d.group)
            out[r, span, :] = (base[r, span, :].astype(F32) + sweep(d, cols, face, ext, span, r, folded)).astype(BF)


def second_kernel(d, face_ref, cols, field, pair_in, cross_in, folded, out, pair, cross, ext):
    face = face_ref[0]
    extend(d, face, field, pair_in, cross_in, ext)
    correct(d, cols, face, field, folded, out, ext)
    for start, buffer in zip(edge_rows(d, lax.rem(face, 2)), (pair, cross)):
        buffer[...] = out[pl.ds(start, HALO)]


def third_rows_kernel(d, face_ref, iface, cols, once, field, pair_in, cross_in, folded, faces_out, ext):
    face = face_ref[0]
    extend(d, face, once, pair_in, cross_in, ext)
    for q in range(d.nq):
        row = iface[q]
        span = pl.ds(0, (d.ticks - 1) * d.sources)
        value = (field[row, span, :].astype(F32) + sweep(d, cols, face, ext, span, row, folded)).astype(BF)
        for t in range(d.ticks - 1):
            faces_out[t, q] = value[t * d.sources : (t + 1) * d.sources, :]


def third_kernel(d, face_ref, cols, once, field, pair_in, cross_in, folded, after, out, ext):
    face = face_ref[0]
    extend(d, face, once, pair_in, cross_in, ext)
    correct(d, cols, face, field, folded, out, ext)


def marked(d, block, e):
    parts = []
    for q in range(d.nq):
        at = d.batch + q // HALO * d.width
        mark = d.batch + d.share + q * d.mark
        mark = block[e, mark : mark + d.mark, :]
        parts.append(block[q % HALO, at : at + d.width, :] * jnp.concatenate([mark] * (d.width // d.mark), axis=0))
    return jnp.concatenate(parts, axis=0)


def coupling_first_kernel(d, face_ref, iface, cols, gfield, pair_in, cross_in, folded, after, out, pair, cross, met):
    face = face_ref[0]
    parity = lax.rem(face, 2)
    w = d.width
    met[...] = jnp.zeros_like(met)
    for r in range(d.count):
        lanes = slice(r * w, (r + 1) * w)
        for q in range(d.nq):
            met[2 * HALO + q, :, lanes] = jnp.where(iface[q] == r, folded[r, 0:w, :], jnp.zeros((w, w), BF))
        for k in range(d.neigh):
            c = cols[k, r] - d.first_col(face)
            inside = jnp.logical_and(c >= HALO, c < d.up)
            at = jnp.where(c < HALO, c, c - d.count)
            hit = jnp.logical_not(inside)
            for q in range(d.nq):
                here = c == iface[q] + HALO
                at = jnp.where(here, 2 * HALO + q, at)
                hit = jnp.logical_or(hit, here)

            @pl.when(hit)
            def _():
                met[at, :, lanes] += folded[r, (1 + k) * w : (2 + k) * w, :]

    out[...] = jnp.zeros_like(out)

    def put(start, rows, value):
        for r in range(d.count):
            out[r, pl.ds(start, rows), :] = value[:, r * w : (r + 1) * w].astype(BF)

    pair_face, cross_face = face + 1 - 2 * parity, face - 1 + 2 * parity
    for at, other, block in ((HALO * (1 - parity), pair_face, pair_in), (HALO * parity, cross_face, cross_in)):
        x = jnp.concatenate([marked(d, block, e) for e in range(HALO)], axis=1)
        tiles = jnp.concatenate([met[at + e] for e in range(HALO)], axis=0)
        put(d.start(other), d.group, dot_nn(x, tiles))
    for q in range(d.nq):
        start = d.start(face) + q * w
        put(start, w, dot_nn(gfield[q], met[2 * HALO + q]))
        row = iface[q]
        span = pl.ds(pl.multiple_of(start, w), w)
        out[row, span, :] = (out[row, span, :].astype(F32) + gfield[q].astype(F32)).astype(BF)
    for start, buffer in zip(edge_rows(d, parity), (pair, cross)):
        for i, shift in enumerate((-1, 0, 1)):
            buffer[:, i * d.group : (i + 1) * d.group, :] = out[pl.ds(start, HALO), pl.ds(d.start(face + shift), d.group), :]


def coupling_ext(d, face, gfirst, pair_in, cross_in, ext):
    parity = lax.rem(face, 2)
    ext[0:HALO] = jnp.zeros((HALO, d.wide, d.width), BF)
    ext[d.up : d.ext] = jnp.zeros((HALO, d.wide, d.width), BF)
    ext[HALO : HALO + d.count] = gfirst[...]
    neighbours = ((d.up * (1 - parity), face + 1 - 2 * parity, pair_in), (d.up * parity, face - 1 + 2 * parity, cross_in))
    for start, other, block in neighbours:
        for i, shift in enumerate((-1, 0, 1)):
            ext[pl.ds(start, HALO), pl.ds(d.start(other + shift), d.group), :] = block[:, i * d.group : (i + 1) * d.group, :]


def coupling_chain_kernel(d, face_ref, iface, cols, gfield, gfirst, pair_in, cross_in, folded, after, chain, ext):
    face = face_ref[0]
    w = d.width
    coupling_ext(d, face, gfirst, pair_in, cross_in, ext)
    for q in range(d.nq):
        lanes = slice(q * w, (q + 1) * w)
        for s in range(0, d.wide, d.group):
            span = pl.ds(s, d.group)
            chain[span, lanes] = sweep(d, cols, face, ext, span, iface[q], folded).astype(BF)
        span = pl.ds(pl.multiple_of(d.start(face) + q * w, w), w)
        chain[span, lanes] = (chain[span, lanes].astype(F32) + gfield[q].astype(F32)).astype(BF)


def coupling_last_kernel(d, face_ref, iface, cols, gfield, gfirst, pair_in, cross_in, folded, after, out, ext):
    face = face_ref[0]
    w = d.width
    coupling_ext(d, face, gfirst, pair_in, cross_in, ext)
    for r in range(d.count):
        for s in range(0, d.wide, d.group):
            span = pl.ds(s, d.group)
            out[span, r * w : (r + 1) * w] = sweep(d, cols, face, ext, span, r, folded).astype(BF)
    for q in range(d.nq):
        lane = pl.ds(pl.multiple_of(iface[q] * w, w), w)
        span = pl.ds(pl.multiple_of(d.start(face) + q * w, w), w)
        out[span, lane] = (out[span, lane].astype(F32) + gfield[q].astype(F32)).astype(BF)


def chip_hops(faces):
    return [(0, None)] if faces <= 2 else [(0, 1)] if faces <= 4 else [(0, 1), (-1, None)]


def hop_face(faces, face, hop):
    return face ^ (2 * hop) if faces <= 4 else face + 2 * hop


def arrived_blocks(d, face, own, other):
    parity = lax.rem(face, 2)
    for i, hops in enumerate(chip_hops(d.faces)):
        starts = [0 if hop is None else d.start(hop_face(d.faces, face - parity, hop)) for hop in hops]
        for block, odd in ((own[i], parity), (other[i], 1 - parity)):
            start = pl.multiple_of(jnp.where(odd == 1, starts[1], starts[0]), d.group)
            yield jnp.concatenate([block[j] for j in range(2 * d.nq)], axis=1), start


def chain_kernel(d, tick, face_ref, own_chain, other_chain, own_faces, other_faces, *rest):
    arrived, sent = rest[:-1], rest[-1]
    face = face_ref[0]
    parity = lax.rem(face, 2)
    half = len(arrived) // 2
    blocks = list(arrived_blocks(d, face, arrived[:half], arrived[half:]))
    for chain, base, odd in ((own_chain, own_faces, parity), (other_chain, other_faces, 1 - parity)):
        total = jnp.zeros((d.sources, d.group), F32)
        for x, start in blocks:
            total += dot_nn(x, chain[pl.ds(start, 2 * d.group), :])
        for q in range(d.nq):
            value = base[tick, q].astype(F32) - total[:, q * d.width : (q + 1) * d.width]
            sent[odd * d.nq + q] = value.astype(BF)


def merge_kernel(d, face_ref, own, other, sent):
    parity = lax.rem(face_ref[0], 2)
    for q in range(d.nq):
        sent[parity * d.nq + q] = own[0, q]
        sent[(1 - parity) * d.nq + q] = other[0, q]


def output_kernel(d, ticks, face_ref, fields, coupled, *rest):
    *arrived, out, held, sems = rest
    w = d.width
    face = face_ref[0]
    each = 2 * len(chip_hops(d.faces))
    copies = []
    arrived = arrived[len(arrived) % each :]
    for i, t in enumerate(ticks):
        total = None
        if t:
            mine, arrived = arrived[:each], arrived[each:]
            total = jnp.zeros((d.sources, d.count * w), F32)
            for x, start in arrived_blocks(d, face, mine[: each // 2], mine[each // 2 :]):
                total += dot_nn(x, coupled[pl.ds(start, 2 * d.group), :])
        for r in range(d.count):
            value = fields[r, t * d.sources : (t + 1) * d.sources, :]
            if t:
                value = (value.astype(F32) - total[:, r * w : (r + 1) * w]).astype(BF)
            held[i, :, r * w : (r + 1) * w] = value
        copies.append(pltpu.make_async_copy(held.at[i], out.at[t], sems.at[i]))
        copies[-1].start()
    for copy in copies:
        copy.wait()


def call(body, name, smem, inputs, outs, scratch=(), flops=0, anywhere=(), sems=0, place=pltpu.VMEM, aliases=None):
    outs = [x if isinstance(x, jax.ShapeDtypeStruct) else jax.ShapeDtypeStruct(x, BF) for x in outs]
    specs = [pl.BlockSpec(memory_space=pl.ANY if i in anywhere else pltpu.VMEM) for i in range(len(inputs))]
    return pl.pallas_call(
        body,
        name=name,
        out_shape=outs,
        in_specs=[pl.BlockSpec(memory_space=pltpu.SMEM)] * len(smem) + specs,
        out_specs=[pl.BlockSpec(memory_space=place if x.dtype == BF else pltpu.SMEM) for x in outs],
        scratch_shapes=[pltpu.VMEM(s, BF) for s in scratch] + ([pltpu.SemaphoreType.DMA((sems,))] if sems else []),
        input_output_aliases=aliases or {},
        compiler_params=pltpu.CompilerParams(vmem_limit_bytes=32 * 1024 * 1024),
        cost_estimate=pl.CostEstimate(flops=flops, bytes_accessed=0, transcendentals=0),
    )(*smem, *inputs)


def on_device(rhs, inflow, diag_tiles, off_tiles, cols, inverse_tiles, coupling, iface):
    faces, slabs = lax.axis_size("face"), lax.axis_size("slab")
    ticks, _, sources, _ = rhs.shape
    _, count, neigh, width, _ = off_tiles.shape
    nq = coupling.shape[1]
    d = Dims(ticks, sources, count, neigh, width, nq, faces)
    diag, off, inv, couple, cols = diag_tiles[0], off_tiles[0], inverse_tiles[0], coupling[0], cols[0].T
    face = lax.axis_index("face").astype(jnp.int32)[None]
    tile = width * width

    pairing = [(i, i ^ 1) for i in range(faces) if i ^ 1 < faces]
    crossing = [(i, ((i + 1) ^ 1) - 1) for i in range(faces) if 0 <= ((i + 1) ^ 1) - 1 < faces]

    def exchange(pair, cross):
        got = lax.ppermute(cross, "face", crossing)
        return lax.ppermute(pair, "face", pairing), got

    def swap(block):
        return lax.ppermute(block, "face", pairing)

    def onward(block, beside=lambda: None):
        own = []
        for hops in chip_hops(faces):
            route = []
            for s in range(1, slabs):
                for f in range(faces):
                    hop = hops[f % 2]
                    g = -1 if hop is None else hop_face(faces, f, hop)
                    if 0 <= g < faces:
                        route.append(((s - 1) * faces + g, s * faces + f))
            own.append(lax.ppermute(block, ("slab", "face"), route))
        made = beside()
        if made is not None:
            *own, made = lax.optimization_barrier((*own, made))
        return own + [swap(x) for x in own], made

    batch, group, ext, wide = d.batch, d.group, d.ext, d.wide
    sweep_flops = 2 * count * tile * (neigh + 1)
    ints = [jax.ShapeDtypeStruct(x.shape, x.dtype) for x in (iface, cols)]
    on_hbm = (iface, cols, inflow[0], couple, inv, rhs[:, 0], diag, off)
    field, gfield, pair, cross, inv, diag, off, iface, cols = call(
        functools.partial(first_kernel, d),
        "first",
        [face],
        [pltpu.with_memory_space_constraint(x, pltpu.HBM) for x in on_hbm],
        [(count, batch, width), (nq, width, width)] + [(HALO, d.first_rows, width)] * 2 + [x.shape for x in (inv, diag, off)] + ints,
        [(ticks, sources, count * width), (sources, group), (nq, width, width)],
        flops=2 * batch * count * tile,
        anywhere=range(8),
        sems=7 + ticks,
    )
    pair0, cross0 = exchange(pair, cross)
    (folded,) = call(
        functools.partial(fold_kernel, d),
        "fold",
        [],
        [inv, diag, off],
        [(count, d.depth, width)],
        flops=width * sweep_flops // 64,
    )
    once, pair, cross = call(
        functools.partial(second_kernel, d),
        "second",
        [face, cols],
        [field, pair0, cross0, folded],
        [(count, batch, width)] + [(HALO, batch, width)] * 2,
        [(ext, batch, width)],
        flops=batch * sweep_flops // 64,
    )
    pair1, cross1 = exchange(pair, cross)
    gfirst, gpair, gcross = call(
        functools.partial(coupling_first_kernel, d),
        "coupling_first",
        [face, iface, cols],
        [gfield, pair0, cross0, folded, pair1],
        [(count, wide, width)] + [(HALO, 3 * group, width)] * 2,
        [(2 * HALO + nq, width, count * width)],
        flops=2 * (2 * HALO + nq) * width * count * tile,
        anywhere=(4,),
    )
    cross1, gfirst = lax.optimization_barrier((cross1, gfirst))
    gpair, gcross = exchange(gpair, gcross)
    (faces_out,) = call(
        functools.partial(third_rows_kernel, d),
        "third_rows",
        [face, iface, cols],
        [once, field, pair1, cross1, folded],
        [(ticks - 1, nq, sources, width)],
        [(ext, (ticks - 1) * sources, width)],
        flops=batch * sweep_flops,
    )
    other_faces = swap(faces_out)
    (sent,) = call(
        functools.partial(merge_kernel, d),
        "merge",
        [face],
        [faces_out, other_faces],
        [(2 * nq, sources, width)],
    )
    def operator_rows():
        return call(
            functools.partial(coupling_chain_kernel, d),
            "coupling_chain",
            [face, iface, cols],
            [gfield, gfirst, gpair, gcross, folded, sent],
            [(wide, group)],
            [(ext, wide, width)],
            flops=2 * wide * nq * tile * (neigh + 1),
            anywhere=(5,),
        )[0]

    def fields():
        return call(
            functools.partial(third_kernel, d),
            "third",
            [face, cols],
            [once, field, pair1, cross1, folded, sent],
            [(count, batch, width)],
            [(ext, batch, width)],
            flops=batch * sweep_flops,
            anywhere=(5,),
        )[0]

    arrived, chain = onward(sent, operator_rows)
    other_chain = swap(chain)
    whole = (ticks, sources, count * width)

    def operator():
        return call(
            functools.partial(coupling_last_kernel, d),
            "coupling_last",
            [face, iface, cols],
            [gfield, gfirst, gpair, gcross, folded, chain],
            [(wide, count * width)],
            [(ext, wide, width)],
            flops=wide * sweep_flops,
            anywhere=(5,),
        )[0]

    def output(which, blocks, earlier):
        return call(
            functools.partial(output_kernel, d, which),
            "output",
            [face],
            [twice, coupled] + earlier + blocks,
            [whole],
            [(len(which), sources, count * width)],
            flops=2 * len(which) * sources * wide * count * width,
            anywhere=(2,) if earlier else (),
            sems=len(which),
            place=pl.ANY,
            aliases={3: 0} if earlier else None,
        )[0]

    everything = []
    coupled = most = None
    for tick in range(1, ticks):
        everything += arrived
        if tick == ticks - 1:
            break
        (sent,) = call(
            functools.partial(chain_kernel, d, tick),
            "chain",
            [face],
            [chain, other_chain, faces_out, other_faces] + arrived,
            [(2 * nq, sources, width)],
            flops=4 * sources * wide * group,
        )
        if tick == 1:
            arrived, coupled = onward(sent, operator)
        else:
            twice = fields()
            arrived, most = onward(sent, lambda: output(tuple(range(ticks - 1)), everything, []))
    out = output((ticks - 1,), arrived, [most])
    return out[:, None]


def solution(mesh):
    placed = (
        P(None, "slab", None, "face"),
        P("slab", None, "face"),
        P("slab", "face", None, None),
        P("slab", "face", None, None, None),
        P("slab", "face", None),
        P("slab", "face", None, None),
        P("slab", "face", None, None),
        P("face"),
    )
    return jax.shard_map(
        on_device,
        mesh=mesh,
        in_specs=placed,
        out_specs=P(None, "slab", None, "face"),
        check_vma=False,
    )
```

```python
import functools
import math

import jax
import jax.numpy as jnp
from jax import lax
from jax.experimental import pallas as pl
from jax.experimental.pallas import tpu as pltpu
from jax.sharding import PartitionSpec as P

HALO = 2
BF = jnp.bfloat16
F32 = jnp.float32


def dot_nt(a, b):
    return lax.dot_general(a, b, (((1,), (1,)), ((), ())), preferred_element_type=F32)


def dot_nn(a, b):
    return lax.dot_general(a, b, (((1,), (0,)), ((), ())), preferred_element_type=F32)


class Dims:
    def __init__(self, ticks, sources, count, neigh, width, nq, faces):
        self.ticks, self.sources, self.count, self.neigh = ticks, sources, count, neigh
        self.width, self.nq, self.faces = width, nq, faces
        self.batch = ticks * sources
        self.group = nq * width
        self.ext = count + 2 * HALO
        self.depth = (1 + neigh) * width
        self.slots = 4 if faces <= 4 else 6
        self.wide = self.slots * self.group
        self.mark = 16
        self.share = -(-nq // HALO) * width
        self.first_rows = self.batch + self.share + nq * self.mark
        self.last = count - HALO
        self.up = count + HALO

    def start(self, face):
        return pl.multiple_of(lax.rem(face + 2 * self.slots, self.slots) * self.group, self.group)

    def first_col(self, face):
        return face * self.count - HALO


def edge_rows(d, parity):
    return d.last * (1 - parity), d.last * parity


def first_kernel(
    d, face_ref, iface_hbm, cols_hbm, inflow, coupling, inv, rhs, diag_hbm, off_hbm, *rest
):
    field, gfield, pair, cross, tiles, diag, off, iface, cols, right, flow, couple, sems = rest
    w = d.width
    moves = [(iface_hbm, iface), (inflow, flow), (coupling, couple), (inv, tiles)]
    moves += [(rhs.at[t], right.at[t]) for t in range(d.ticks)]
    moves += [(cols_hbm, cols), (diag_hbm, diag), (off_hbm, off)]
    copies = [pltpu.make_async_copy(a, b, sems.at[i]) for i, (a, b) in enumerate(moves)]
    for copy in copies:
        copy.start()
    for copy in copies[:4]:
        copy.wait()
    coupled = []
    for q in range(d.nq):
        turned = couple[q].astype(F32).T.astype(BF)
        gfield[q] = dot_nt(turned, tiles[iface[q]]).astype(BF)
        coupled.append(dot_nn(flow[:, q * w : (q + 1) * w], turned))
    for copy in copies[4 : 4 + d.ticks]:
        copy.wait()
    for r in range(d.count):
        x = jnp.concatenate([right[t, :, r * w : (r + 1) * w] for t in range(d.ticks)], axis=0)
        field[r] = dot_nt(x, tiles[r]).astype(BF)
    for q in range(d.nq):
        row = iface[q]
        corrected = right[0, :, pl.ds(pl.multiple_of(row * w, w), w)].astype(F32) - coupled[q]
        field[row, 0 : d.sources, :] = dot_nt(corrected.astype(BF), tiles[row]).astype(BF)
    for start, buffer in zip(edge_rows(d, lax.rem(face_ref[0], 2)), (pair, cross)):
        buffer[:, 0 : d.batch, :] = field[pl.ds(start, HALO)]
        for q in range(d.nq):
            at = d.batch + q // HALO * w
            buffer[q % HALO, at : at + w, :] = gfield[q]
            at = d.batch + d.share + q * d.mark
            for e in range(HALO):
                buffer[e, at : at + d.mark, :] = jnp.full((d.mark, w), iface[q] == start + e).astype(F32).astype(BF)
    for copy in copies[4 + d.ticks :]:
        copy.wait()


def fold_kernel(d, face_ref, iface, cols, inv, diag, off, folded, met):
    w = d.width
    for r in range(d.count):
        tiles = jnp.concatenate([diag[r]] + [off[r, k] for k in range(d.neigh)], axis=1)
        product = dot_nn(inv[r], tiles)
        rows = lax.broadcasted_iota(jnp.int32, (w, w), 0)
        unit = (rows == lax.broadcasted_iota(jnp.int32, (w, w), 1)).astype(F32)
        for k in range(1 + d.neigh):
            part = product[:, k * w : (k + 1) * w].T
            folded[r, k * w : (k + 1) * w, :] = ((unit if k == 0 else 0.0) - part).astype(BF)
    met[...] = jnp.zeros_like(met)
    for r in range(d.count):
        lanes = slice(r * w, (r + 1) * w)
        for q in range(d.nq):
            met[2 * HALO + q, :, lanes] = jnp.where(iface[q] == r, folded[r, 0:w, :], jnp.zeros((w, w), BF))
        for k in range(d.neigh):
            c = cols[k, r] - d.first_col(face_ref[0])
            inside = jnp.logical_and(c >= HALO, c < d.up)
            at = jnp.where(c < HALO, c, c - d.count)
            hit = jnp.logical_not(inside)
            for q in range(d.nq):
                here = c == iface[q] + HALO
                at = jnp.where(here, 2 * HALO + q, at)
                hit = jnp.logical_or(hit, here)

            @pl.when(hit)
            def _():
                met[at, :, lanes] += folded[r, (1 + k) * w : (2 + k) * w, :]


def sweep(d, cols, face, ext, span, r, folded):
    x = [ext[r + HALO, span, :]] + [ext[cols[k, r] - d.first_col(face), span, :] for k in range(d.neigh)]
    return dot_nn(jnp.concatenate(x, axis=1), folded[r])


def place_halo(d, face, pair_in, cross_in, ext):
    parity = lax.rem(face, 2)
    rows = pl.ds(0, ext.shape[1])
    ext[pl.ds(d.up * (1 - parity), HALO)] = pair_in[:, rows, :]
    ext[pl.ds(d.up * parity, HALO)] = cross_in[:, rows, :]


def extend(d, face, edges, inner, pair_in, cross_in, ext):
    rows = pl.ds(0, ext.shape[1])
    ext[HALO : 2 * HALO] = edges[0:HALO, rows, :]
    ext[2 * HALO : d.count] = inner[:, rows, :]
    ext[d.count : d.up] = edges[HALO : 2 * HALO, rows, :]
    place_halo(d, face, pair_in, cross_in, ext)


def correct(d, cols, face, base, folded, out, ext, rows, first=0):
    for i, r in enumerate(rows):
        for s in range(0, d.batch, d.group):
            span = pl.ds(s, d.group)
            value = base[r, span, :].astype(F32) + sweep(d, cols, face, ext, span, r, folded)
            out[first + i, span, :] = value.astype(BF)


def second_edges_kernel(d, face_ref, cols, field, pair_in, cross_in, folded, edges, pair, cross, ext):
    face = face_ref[0]
    ext[HALO : HALO + d.count] = field[...]
    place_halo(d, face, pair_in, cross_in, ext)
    correct(d, cols, face, field, folded, edges, ext, list(range(HALO)) + list(range(d.last, d.count)))
    parity = lax.rem(face, 2)
    pair[...] = edges[pl.ds(HALO * (1 - parity), HALO)]
    cross[...] = edges[pl.ds(HALO * parity, HALO)]


def second_inner_kernel(d, face_ref, cols, field, ext, folded, after, out):
    correct(d, cols, face_ref[0], field, folded, out, ext, range(HALO, d.last))


def third_rows_kernel(d, face_ref, iface, cols, edges, inner, field, pair_in, cross_in, folded, sent, ext):
    face = face_ref[0]
    extend(d, face, edges, inner, pair_in, cross_in, ext)
    span = pl.ds(0, d.sources)
    for q in range(d.nq):
        row = iface[q]
        sent[q] = (field[row, span, :].astype(F32) + sweep(d, cols, face, ext, span, row, folded)).astype(BF)


def third_kernel(d, face_ref, iface, cols, edges, inner, field, pair_in, cross_in, folded, after, out, faces_out, ext):
    face = face_ref[0]
    extend(d, face, edges, inner, pair_in, cross_in, ext)
    correct(d, cols, face, field, folded, out, ext, range(d.count))
    for q in range(d.nq):
        for t in range(1, d.ticks - 1):
            faces_out[t - 1, q] = out[iface[q], t * d.sources : (t + 1) * d.sources, :]


def marked(d, block, e):
    parts = []
    for q in range(d.nq):
        at = d.batch + q // HALO * d.width
        mark = d.batch + d.share + q * d.mark
        mark = block[e, mark : mark + d.mark, :]
        parts.append(block[q % HALO, at : at + d.width, :] * jnp.concatenate([mark] * (d.width // d.mark), axis=0))
    return jnp.concatenate(parts, axis=0)


def coupling_first_kernel(d, face_ref, iface, gfield, pair_in, cross_in, met, after, out, pair, cross):
    face = face_ref[0]
    parity = lax.rem(face, 2)
    w = d.width
    for shift in range(2, d.slots - 1):
        out[:, pl.ds(d.start(face + shift), d.group), :] = jnp.zeros((d.count, d.group, w), BF)

    def put(start, rows, value):
        for r in range(d.count):
            out[r, pl.ds(start, rows), :] = value[:, r * w : (r + 1) * w].astype(BF)

    pair_face, cross_face = face + 1 - 2 * parity, face - 1 + 2 * parity
    for at, other, block in ((HALO * (1 - parity), pair_face, pair_in), (HALO * parity, cross_face, cross_in)):
        x = jnp.concatenate([marked(d, block, e) for e in range(HALO)], axis=1)
        tiles = jnp.concatenate([met[at + e] for e in range(HALO)], axis=0)
        put(d.start(other), d.group, dot_nn(x, tiles))
    for q in range(d.nq):
        start = d.start(face) + q * w
        put(start, w, dot_nn(gfield[q], met[2 * HALO + q]))
        row = iface[q]
        span = pl.ds(pl.multiple_of(start, w), w)
        out[row, span, :] = (out[row, span, :].astype(F32) + gfield[q].astype(F32)).astype(BF)
    for start, buffer in zip(edge_rows(d, parity), (pair, cross)):
        for i, shift in enumerate((-1, 0, 1)):
            buffer[:, i * d.group : (i + 1) * d.group, :] = out[pl.ds(start, HALO), pl.ds(d.start(face + shift), d.group), :]


def coupling_ext(d, face, gfirst, pair_in, cross_in, ext):
    parity = lax.rem(face, 2)
    ext[0:HALO] = jnp.zeros((HALO, d.wide, d.width), BF)
    ext[d.up : d.ext] = jnp.zeros((HALO, d.wide, d.width), BF)
    ext[HALO : HALO + d.count] = gfirst[...]
    neighbours = ((d.up * (1 - parity), face + 1 - 2 * parity, pair_in), (d.up * parity, face - 1 + 2 * parity, cross_in))
    for start, other, block in neighbours:
        for i, shift in enumerate((-1, 0, 1)):
            ext[pl.ds(start, HALO), pl.ds(d.start(other + shift), d.group), :] = block[:, i * d.group : (i + 1) * d.group, :]


def coupling_chain_kernel(d, face_ref, iface, cols, gfield, gfirst, pair_in, cross_in, folded, after, chain, ext):
    face = face_ref[0]
    w = d.width
    coupling_ext(d, face, gfirst, pair_in, cross_in, ext)
    for q in range(d.nq):
        lanes = slice(q * w, (q + 1) * w)
        for s in range(0, d.wide, d.group):
            span = pl.ds(s, d.group)
            chain[span, lanes] = sweep(d, cols, face, ext, span, iface[q], folded).astype(BF)
        span = pl.ds(pl.multiple_of(d.start(face) + q * w, w), w)
        chain[span, lanes] = (chain[span, lanes].astype(F32) + gfield[q].astype(F32)).astype(BF)


def coupling_last_kernel(d, face_ref, iface, cols, gfield, gfirst, pair_in, cross_in, folded, after, out, ext):
    face = face_ref[0]
    w = d.width
    coupling_ext(d, face, gfirst, pair_in, cross_in, ext)
    for r in range(d.count):
        for s in range(0, d.wide, d.group):
            span = pl.ds(s, d.group)
            out[span, r * w : (r + 1) * w] = sweep(d, cols, face, ext, span, r, folded).astype(BF)
    for q in range(d.nq):
        lane = pl.ds(pl.multiple_of(iface[q] * w, w), w)
        span = pl.ds(pl.multiple_of(d.start(face) + q * w, w), w)
        out[span, lane] = (out[span, lane].astype(F32) + gfield[q].astype(F32)).astype(BF)


def chip_hops(faces):
    return [(0, None)] if faces <= 2 else [(0, 1)] if faces <= 4 else [(0, 1), (-1, None)]


def hop_face(faces, face, hop):
    return face ^ (2 * hop) if faces <= 4 else face + 2 * hop


def arrived_blocks(d, face, own, other):
    parity = lax.rem(face, 2)
    for i, hops in enumerate(chip_hops(d.faces)):
        starts = [0 if hop is None else d.start(hop_face(d.faces, face - parity, hop)) for hop in hops]
        for block, odd in ((own[i], parity), (other[i], 1 - parity)):
            start = pl.multiple_of(jnp.where(odd == 1, starts[1], starts[0]), d.group)
            yield jnp.concatenate([block[j] for j in range(2 * d.nq)], axis=1), start


def chain_kernel(d, tick, face_ref, own_chain, other_chain, own_faces, other_faces, *rest):
    arrived, sent = rest[:-1], rest[-1]
    face = face_ref[0]
    parity = lax.rem(face, 2)
    half = len(arrived) // 2
    blocks = list(arrived_blocks(d, face, arrived[:half], arrived[half:]))
    for chain, base, odd in ((own_chain, own_faces, parity), (other_chain, other_faces, 1 - parity)):
        total = jnp.zeros((d.sources, d.group), F32)
        for x, start in blocks:
            total += dot_nn(x, chain[pl.ds(start, 2 * d.group), :])
        for q in range(d.nq):
            value = base[tick - 1, q].astype(F32) - total[:, q * d.width : (q + 1) * d.width]
            sent[odd * d.nq + q] = value.astype(BF)


def merge_kernel(d, face_ref, own, other, sent):
    parity = lax.rem(face_ref[0], 2)
    for q in range(d.nq):
        sent[parity * d.nq + q] = own[q]
        sent[(1 - parity) * d.nq + q] = other[q]


def output_kernel(d, ticks, face_ref, fields, coupled, *rest):
    *arrived, out, held, sems = rest
    w = d.width
    face = face_ref[0]
    each = 2 * len(chip_hops(d.faces))
    copies = []
    arrived = arrived[len(arrived) % each :]
    part = 2 * w
    for i, t in enumerate(ticks):
        blocks = []
        if t:
            mine, arrived = arrived[:each], arrived[each:]
            blocks = list(arrived_blocks(d, face, mine[: each // 2], mine[each // 2 :]))
        for c in range(0, d.count * w, part):
            total = jnp.zeros((d.sources, part), F32)
            for x, start in blocks:
                total += dot_nn(x, coupled[pl.ds(start, 2 * d.group), c : c + part])
            for j in range(0, part, w):
                value = fields[(c + j) // w, t * d.sources : (t + 1) * d.sources, :].astype(F32)
                held[i, :, c + j : c + j + w] = (value - total[:, j : j + w]).astype(BF)
            here = held.at[i, :, c : c + part]
            copies.append(pltpu.make_async_copy(here, out.at[t, :, c : c + part], sems.at[len(copies)]))
            copies[-1].start()
    for copy in copies:
        copy.wait()


def call(body, name, smem, inputs, outs, scratch=(), flops=0, anywhere=(), sems=0, place=pltpu.VMEM, aliases=None):
    outs = [x if isinstance(x, jax.ShapeDtypeStruct) else jax.ShapeDtypeStruct(x, BF) for x in outs]
    specs = [pl.BlockSpec(memory_space=pl.ANY if i in anywhere else pltpu.VMEM) for i in range(len(inputs))]
    return pl.pallas_call(
        body,
        name=name,
        out_shape=outs,
        in_specs=[pl.BlockSpec(memory_space=pltpu.SMEM)] * len(smem) + specs,
        out_specs=[pl.BlockSpec(memory_space=place if x.dtype == BF else pltpu.SMEM) for x in outs],
        scratch_shapes=[pltpu.VMEM(s, BF) for s in scratch] + ([pltpu.SemaphoreType.DMA((sems,))] if sems else []),
        input_output_aliases=aliases or {},
        compiler_params=pltpu.CompilerParams(vmem_limit_bytes=32 * 1024 * 1024),
        cost_estimate=pl.CostEstimate(flops=flops, bytes_accessed=0, transcendentals=0),
    )(*smem, *inputs)


def on_device(rhs, inflow, diag_tiles, off_tiles, cols, inverse_tiles, coupling, iface):
    faces, slabs = lax.axis_size("face"), lax.axis_size("slab")
    ticks, _, sources, _ = rhs.shape
    _, count, neigh, width, _ = off_tiles.shape
    nq = coupling.shape[1]
    d = Dims(ticks, sources, count, neigh, width, nq, faces)
    diag, off, inv, couple, cols = diag_tiles[0], off_tiles[0], inverse_tiles[0], coupling[0], cols[0].T
    face = lax.axis_index("face").astype(jnp.int32)[None]
    tile = width * width

    pairing = [(i, i ^ 1) for i in range(faces) if i ^ 1 < faces]
    crossing = [(i, ((i + 1) ^ 1) - 1) for i in range(faces) if 0 <= ((i + 1) ^ 1) - 1 < faces]

    def exchange(pair, cross):
        got = lax.ppermute(cross, "face", crossing)
        return lax.ppermute(pair, "face", pairing), got

    def swap(block):
        return lax.ppermute(block, "face", pairing)

    def onward(block, beside=lambda: None):
        own = []
        for hops in chip_hops(faces):
            route = []
            for s in range(1, slabs):
                for f in range(faces):
                    hop = hops[f % 2]
                    g = -1 if hop is None else hop_face(faces, f, hop)
                    if 0 <= g < faces:
                        route.append(((s - 1) * faces + g, s * faces + f))
            own.append(lax.ppermute(block, ("slab", "face"), route))
        made = beside()
        if made is not None:
            *own, made = lax.optimization_barrier((*own, made))
        return own + [swap(x) for x in own], made

    batch, group, ext, wide = d.batch, d.group, d.ext, d.wide
    sweep_flops = 2 * count * tile * (neigh + 1)
    ints = [jax.ShapeDtypeStruct(x.shape, x.dtype) for x in (iface, cols)]
    on_hbm = (iface, cols, inflow[0], couple, inv, rhs[:, 0], diag, off)
    field, gfield, pair, cross, inv, diag, off, iface, cols = call(
        functools.partial(first_kernel, d),
        "first",
        [face],
        [pltpu.with_memory_space_constraint(x, pltpu.HBM) for x in on_hbm],
        [(count, batch, width), (nq, width, width)] + [(HALO, d.first_rows, width)] * 2 + [x.shape for x in (inv, diag, off)] + ints,
        [(ticks, sources, count * width), (sources, group), (nq, width, width)],
        flops=2 * batch * count * tile,
        anywhere=range(8),
        sems=7 + ticks,
    )
    pair0, cross0 = exchange(pair, cross)
    folded, met = call(
        functools.partial(fold_kernel, d),
        "fold",
        [face, iface, cols],
        [inv, diag, off],
        [(count, d.depth, width), (2 * HALO + nq, width, count * width)],
        flops=width * sweep_flops // 64,
    )
    edges, pair, cross, ext0 = call(
        functools.partial(second_edges_kernel, d),
        "second_edges",
        [face, cols],
        [field, pair0, cross0, folded],
        [(2 * HALO, batch, width)] + [(HALO, batch, width)] * 2 + [(ext, batch, width)],
        flops=batch * sweep_flops // 64,
    )
    pair1, cross1 = exchange(pair, cross)
    gfirst, gpair, gcross = call(
        functools.partial(coupling_first_kernel, d),
        "coupling_first",
        [face, iface],
        [gfield, pair0, cross0, met, pair1],
        [(count, wide, width)] + [(HALO, 3 * group, width)] * 2,
        flops=2 * (2 * HALO + nq) * width * count * tile,
        anywhere=(4,),
    )
    gpair1, gcross1 = exchange(gpair, gcross)
    (inner,) = call(
        functools.partial(second_inner_kernel, d),
        "second_inner",
        [face, cols],
        [field, ext0, folded, gfirst],
        [(count - 2 * HALO, batch, width)],
        flops=0,
        anywhere=(3,),
    )
    cross1, inner = lax.optimization_barrier((cross1, inner))
    (own_first,) = call(
        functools.partial(third_rows_kernel, d),
        "third_rows",
        [face, iface, cols],
        [edges, inner, field, pair1, cross1, folded],
        [(nq, sources, width)],
        [(ext, sources, width)],
        flops=batch * sweep_flops * 5 // 2,
    )
    (sent,) = call(
        functools.partial(merge_kernel, d),
        "merge",
        [face],
        [own_first, swap(own_first)],
        [(2 * nq, sources, width)],
    )

    def operator_rows():
        (chain,) = call(
            functools.partial(coupling_chain_kernel, d),
            "coupling_chain",
            [face, iface, cols],
            [gfield, gfirst, gpair1, gcross1, folded, sent],
            [(wide, group)],
            [(ext, wide, width)],
            flops=0,
            anywhere=(5,),
        )
        return chain, *call(
            functools.partial(third_kernel, d),
            "third",
            [face, iface, cols],
            [edges, inner, field, pair1, cross1, folded, chain],
            [(count, batch, width), (ticks - 2, nq, sources, width)],
            [(ext, batch, width)],
            flops=0,
            anywhere=(6,),
        )

    arrived, (chain, twice, faces_out) = onward(sent, operator_rows)
    other_chain, other_faces = swap(chain), swap(faces_out)
    whole = (ticks, sources, count * width)

    def operator():
        return call(
            functools.partial(coupling_last_kernel, d),
            "coupling_last",
            [face, iface, cols],
            [gfield, gfirst, gpair1, gcross1, folded, chain],
            [(wide, count * width)],
            [(ext, wide, width)],
            flops=wide * sweep_flops,
            anywhere=(5,),
        )[0]

    def output(which, blocks, earlier):
        return call(
            functools.partial(output_kernel, d, which),
            "output",
            [face],
            [twice, coupled] + earlier + blocks,
            [whole],
            [(len(which), sources, count * width)],
            flops=2 * len(which) * sources * wide * count * width,
            anywhere=(2,) if earlier else (),
            sems=len(which) * count,
            place=pl.ANY,
            aliases={3: 0} if earlier else None,
        )[0]

    everything = []
    coupled = most = None
    for tick in range(1, ticks):
        everything += arrived
        if tick == ticks - 1:
            break
        (sent,) = call(
            functools.partial(chain_kernel, d, tick),
            "chain",
            [face],
            [chain, other_chain, faces_out, other_faces] + arrived,
            [(2 * nq, sources, width)],
            flops=4 * sources * wide * group,
        )
        if tick == 1:
            arrived, coupled = onward(sent, operator)
        else:
            arrived, most = onward(sent, lambda: output(tuple(range(ticks - 1)), everything, []))
    out = output((ticks - 1,), arrived, [most])
    return out[:, None]


def solution(mesh):
    placed = (
        P(None, "slab", None, "face"),
        P("slab", None, "face"),
        P("slab", "face", None, None),
        P("slab", "face", None, None, None),
        P("slab", "face", None),
        P("slab", "face", None, None),
        P("slab", "face", None, None),
        P("face"),
    )
    return jax.shard_map(
        on_device,
        mesh=mesh,
        in_specs=placed,
        out_specs=P(None, "slab", None, "face"),
        check_vma=False,
    )
```

```python
import functools
import math

import jax
import jax.numpy as jnp
from jax import lax
from jax.experimental import pallas as pl
from jax.experimental.pallas import tpu as pltpu
from jax.sharding import PartitionSpec as P

HALO = 2
BF = jnp.bfloat16
F32 = jnp.float32


def dot_nt(a, b):
    return lax.dot_general(a, b, (((1,), (1,)), ((), ())), preferred_element_type=F32)


def dot_nn(a, b):
    return lax.dot_general(a, b, (((1,), (0,)), ((), ())), preferred_element_type=F32)


class Dims:
    def __init__(self, ticks, sources, count, neigh, width, nq, faces):
        self.ticks, self.sources, self.count, self.neigh = ticks, sources, count, neigh
        self.width, self.nq, self.faces = width, nq, faces
        self.batch = ticks * sources
        self.group = nq * width
        self.ext = count + 2 * HALO
        self.depth = (1 + neigh) * width
        self.slots = 4 if faces <= 4 else 6
        self.wide = self.slots * self.group
        self.parts = 4 if self.slots % 4 == 0 else 3
        self.part = self.wide // self.parts
        self.mark = 16
        self.share = -(-nq // HALO) * width
        self.first_rows = self.batch + self.share + nq * self.mark
        self.last = count - HALO
        self.up = count + HALO

    def start(self, face):
        return pl.multiple_of(lax.rem(face + 2 * self.slots, self.slots) * self.group, self.group)

    def first_col(self, face):
        return face * self.count - HALO


def edge_rows(d, parity):
    return d.last * (1 - parity), d.last * parity


def first_kernel(
    d, face_ref, iface_hbm, cols_hbm, inflow, coupling, inv, rhs, diag_hbm, off_hbm, *rest
):
    field, gfield, pair, cross, tiles, diag, off, iface, cols, right, flow, couple, sems = rest
    w = d.width
    moves = [(iface_hbm, iface), (inflow, flow), (coupling, couple), (inv, tiles)]
    moves += [(rhs.at[t], right.at[t]) for t in range(d.ticks)]
    moves += [(cols_hbm, cols), (diag_hbm, diag), (off_hbm, off)]
    copies = [pltpu.make_async_copy(a, b, sems.at[i]) for i, (a, b) in enumerate(moves)]
    for copy in copies:
        copy.start()
    for copy in copies[:4]:
        copy.wait()
    coupled = []
    for q in range(d.nq):
        turned = couple[q].astype(F32).T.astype(BF)
        gfield[q] = dot_nt(turned, tiles[iface[q]]).astype(BF)
        coupled.append(dot_nn(flow[:, q * w : (q + 1) * w], turned))
    for copy in copies[4 : 4 + d.ticks]:
        copy.wait()
    for r in range(d.count):
        x = jnp.concatenate([right[t, :, r * w : (r + 1) * w] for t in range(d.ticks)], axis=0)
        field[r] = dot_nt(x, tiles[r]).astype(BF)
    for q in range(d.nq):
        row = iface[q]
        corrected = right[0, :, pl.ds(pl.multiple_of(row * w, w), w)].astype(F32) - coupled[q]
        field[row, 0 : d.sources, :] = dot_nt(corrected.astype(BF), tiles[row]).astype(BF)
    for start, buffer in zip(edge_rows(d, lax.rem(face_ref[0], 2)), (pair, cross)):
        buffer[:, 0 : d.batch, :] = field[pl.ds(start, HALO)]
        for q in range(d.nq):
            at = d.batch + q // HALO * w
            buffer[q % HALO, at : at + w, :] = gfield[q]
            at = d.batch + d.share + q * d.mark
            for e in range(HALO):
                buffer[e, at : at + d.mark, :] = jnp.full((d.mark, w), iface[q] == start + e).astype(F32).astype(BF)
    for copy in copies[4 + d.ticks :]:
        copy.wait()


def fold_kernel(d, face_ref, iface, cols, inv, diag, off, folded, met):
    w = d.width
    for r in range(d.count):
        tiles = jnp.concatenate([diag[r]] + [off[r, k] for k in range(d.neigh)], axis=1)
        product = dot_nn(inv[r], tiles)
        rows = lax.broadcasted_iota(jnp.int32, (w, w), 0)
        unit = (rows == lax.broadcasted_iota(jnp.int32, (w, w), 1)).astype(F32)
        for k in range(1 + d.neigh):
            part = product[:, k * w : (k + 1) * w].T
            folded[r, k * w : (k + 1) * w, :] = ((unit if k == 0 else 0.0) - part).astype(BF)
    met[...] = jnp.zeros_like(met)
    for r in range(d.count):
        lanes = slice(r * w, (r + 1) * w)
        for q in range(d.nq):
            met[2 * HALO + q, :, lanes] = jnp.where(iface[q] == r, folded[r, 0:w, :], jnp.zeros((w, w), BF))
        for k in range(d.neigh):
            c = cols[k, r] - d.first_col(face_ref[0])
            inside = jnp.logical_and(c >= HALO, c < d.up)
            at = jnp.where(c < HALO, c, c - d.count)
            hit = jnp.logical_not(inside)
            for q in range(d.nq):
                here = c == iface[q] + HALO
                at = jnp.where(here, 2 * HALO + q, at)
                hit = jnp.logical_or(hit, here)

            @pl.when(hit)
            def _():
                met[at, :, lanes] += folded[r, (1 + k) * w : (2 + k) * w, :]


def sweep(d, cols, face, ext, span, r, folded):
    x = [ext[r + HALO, span, :]] + [ext[cols[k, r] - d.first_col(face), span, :] for k in range(d.neigh)]
    return dot_nn(jnp.concatenate(x, axis=1), folded[r])


def place_halo(d, face, pair_in, cross_in, ext, rows):
    parity = lax.rem(face, 2)
    ext[pl.ds(d.up * (1 - parity), HALO)] = pair_in[:, rows, :]
    ext[pl.ds(d.up * parity, HALO)] = cross_in[:, rows, :]


def extend(d, face, edges, inner, pair_in, cross_in, ext, rows):
    ext[HALO : 2 * HALO] = edges[0:HALO, rows, :]
    ext[2 * HALO : d.count] = inner[:, rows, :]
    ext[d.count : d.up] = edges[HALO : 2 * HALO, rows, :]
    place_halo(d, face, pair_in, cross_in, ext, rows)


def correct(d, cols, face, base, folded, out, ext, rows, first=0):
    for i, r in enumerate(rows):
        for s in range(0, d.batch, d.group):
            span = pl.ds(s, d.group)
            value = base[r, span, :].astype(F32) + sweep(d, cols, face, ext, span, r, folded)
            out[first + i, span, :] = value.astype(BF)


def second_edges_kernel(d, face_ref, cols, field, pair_in, cross_in, folded, edges, pair, cross, ext):
    face = face_ref[0]
    ext[HALO : HALO + d.count] = field[...]
    place_halo(d, face, pair_in, cross_in, ext, pl.ds(0, d.batch))
    correct(d, cols, face, field, folded, edges, ext, list(range(HALO)) + list(range(d.last, d.count)))
    parity = lax.rem(face, 2)
    pair[...] = edges[pl.ds(HALO * (1 - parity), HALO)]
    cross[...] = edges[pl.ds(HALO * parity, HALO)]


def second_inner_kernel(d, face_ref, cols, field, ext, folded, after, out):
    correct(d, cols, face_ref[0], field, folded, out, ext, range(HALO, d.last))


def interface_rows(d, face, iface, cols, edges, inner, field, pair_in, cross_in, folded, first, outs, ext):
    ticks = pl.ds(first * d.sources, len(outs) * d.sources)
    extend(d, face, edges, inner, pair_in, cross_in, ext, ticks)
    for q in range(d.nq):
        row = iface[q]
        value = sweep(d, cols, face, ext, pl.ds(0, len(outs) * d.sources), row, folded)
        value = (field[row, ticks, :].astype(F32) + value).astype(BF)
        for t, out in enumerate(outs):
            out[q] = value[t * d.sources : (t + 1) * d.sources]


def third_rows_kernel(d, face_ref, iface, cols, edges, inner, field, pair_in, cross_in, folded, sent, ext):
    interface_rows(d, face_ref[0], iface, cols, edges, inner, field, pair_in, cross_in, folded, 0, [sent], ext)


def third_kernel(d, face_ref, cols, edges, inner, field, pair_in, cross_in, folded, after, out, ext):
    face = face_ref[0]
    extend(d, face, edges, inner, pair_in, cross_in, ext, pl.ds(0, d.batch))
    correct(d, cols, face, field, folded, out, ext, range(d.count))


def marked(d, block, e):
    parts = []
    for q in range(d.nq):
        at = d.batch + q // HALO * d.width
        mark = d.batch + d.share + q * d.mark
        mark = block[e, mark : mark + d.mark, :]
        parts.append(block[q % HALO, at : at + d.width, :] * jnp.concatenate([mark] * (d.width // d.mark), axis=0))
    return jnp.concatenate(parts, axis=0)


def coupling_first_kernel(d, face_ref, iface, gfield, pair_in, cross_in, met, after, out, pair, cross):
    face = face_ref[0]
    parity = lax.rem(face, 2)
    w = d.width
    for shift in range(2, d.slots - 1):
        out[:, pl.ds(d.start(face + shift), d.group), :] = jnp.zeros((d.count, d.group, w), BF)

    def put(start, rows, value):
        for r in range(d.count):
            out[r, pl.ds(start, rows), :] = value[:, r * w : (r + 1) * w].astype(BF)

    pair_face, cross_face = face + 1 - 2 * parity, face - 1 + 2 * parity
    for at, other, block in ((HALO * (1 - parity), pair_face, pair_in), (HALO * parity, cross_face, cross_in)):
        x = jnp.concatenate([marked(d, block, e) for e in range(HALO)], axis=1)
        tiles = jnp.concatenate([met[at + e] for e in range(HALO)], axis=0)
        put(d.start(other), d.group, dot_nn(x, tiles))
    for q in range(d.nq):
        start = d.start(face) + q * w
        put(start, w, dot_nn(gfield[q], met[2 * HALO + q]))
        row = iface[q]
        span = pl.ds(pl.multiple_of(start, w), w)
        out[row, span, :] = (out[row, span, :].astype(F32) + gfield[q].astype(F32)).astype(BF)
    for start, buffer in zip(edge_rows(d, parity), (pair, cross)):
        for i, shift in enumerate((-1, 0, 1)):
            buffer[:, i * d.group : (i + 1) * d.group, :] = out[pl.ds(start, HALO), pl.ds(d.start(face + shift), d.group), :]


def coupling_ext(d, face, gfirst, pair_in, cross_in, ext):
    parity = lax.rem(face, 2)
    ext[0:HALO] = jnp.zeros((HALO, d.wide, d.width), BF)
    ext[d.up : d.ext] = jnp.zeros((HALO, d.wide, d.width), BF)
    ext[HALO : HALO + d.count] = gfirst[...]
    neighbours = ((d.up * (1 - parity), face + 1 - 2 * parity, pair_in), (d.up * parity, face - 1 + 2 * parity, cross_in))
    for start, other, block in neighbours:
        for i, shift in enumerate((-1, 0, 1)):
            ext[pl.ds(start, HALO), pl.ds(d.start(other + shift), d.group), :] = block[:, i * d.group : (i + 1) * d.group, :]


def interface_kernel(d, face_ref, iface, cols, *rest):
    edges, inner, field, pair_in, cross_in, folded, gfield, gfirst, gpair_in, gcross_in, after = rest[:11]
    chain, (faces_out, ext, small) = rest[11 : 11 + d.parts], rest[11 + d.parts :]
    face = face_ref[0]
    w = d.width
    interface_rows(d, face, iface, cols, edges, inner, field, pair_in, cross_in, folded, 1, [faces_out.at[t] for t in range(d.ticks - 2)], small)
    pair_in, cross_in = gpair_in, gcross_in
    coupling_ext(d, face, gfirst, pair_in, cross_in, ext)
    for i in range(d.slots):
        start = i * d.group % d.part
        part = chain[i * d.group // d.part]
        for q in range(d.nq):
            value = sweep(d, cols, face, ext, pl.ds(i * d.group, d.group), iface[q], folded)
            part[start : start + d.group, q * w : (q + 1) * w] = value.astype(BF)

        @pl.when(lax.rem(face, d.slots) == i)
        def _():
            for q in range(d.nq):
                block = (slice(start + q * w, start + (q + 1) * w), slice(q * w, (q + 1) * w))
                part[block] = (part[block].astype(F32) + gfield[q].astype(F32)).astype(BF)


def coupling_last_kernel(d, face_ref, iface, cols, gfield, gfirst, pair_in, cross_in, folded, after, out, ext):
    face = face_ref[0]
    w = d.width
    coupling_ext(d, face, gfirst, pair_in, cross_in, ext)
    for r in range(d.count):
        for s in range(0, d.wide, d.group):
            span = pl.ds(s, d.group)
            out[span, r * w : (r + 1) * w] = sweep(d, cols, face, ext, span, r, folded).astype(BF)
    for q in range(d.nq):
        lane = pl.ds(pl.multiple_of(iface[q] * w, w), w)
        span = pl.ds(pl.multiple_of(d.start(face) + q * w, w), w)
        out[span, lane] = (out[span, lane].astype(F32) + gfield[q].astype(F32)).astype(BF)


def chip_hops(faces):
    return [(0, None)] if faces <= 2 else [(0, 1)] if faces <= 4 else [(0, 1), (-1, None)]


def hop_face(faces, face, hop):
    return face ^ (2 * hop) if faces <= 4 else face + 2 * hop


def arrived_blocks(d, face, own, other):
    parity = lax.rem(face, 2)
    for i, hops in enumerate(chip_hops(d.faces)):
        starts = [0 if hop is None else d.start(hop_face(d.faces, face - parity, hop)) for hop in hops]
        for block, odd in ((own[i], parity), (other[i], 1 - parity)):
            start = pl.multiple_of(jnp.where(odd == 1, starts[1], starts[0]), d.group)
            yield jnp.concatenate([block[j] for j in range(2 * d.nq)], axis=1), start


def chain_kernel(d, tick, face_ref, *rest):
    own_chain, other_chain, rest = rest[: d.parts], rest[d.parts : 2 * d.parts], rest[2 * d.parts :]
    own_faces, other_faces, *arrived, sent, chain = rest
    face = face_ref[0]
    parity = lax.rem(face, 2)
    for i in range(d.parts):
        for j, part in enumerate((own_chain[i], other_chain[i])):
            chain[i * d.part : (i + 1) * d.part, j * d.group : (j + 1) * d.group] = part[...]
    half = len(arrived) // 2
    total = jnp.zeros((d.sources, 2 * d.group), F32)
    for x, start in arrived_blocks(d, face, arrived[:half], arrived[half:]):
        total += dot_nn(x, chain[pl.ds(start, 2 * d.group), :])
    for j, (base, odd) in enumerate(((own_faces, parity), (other_faces, 1 - parity))):
        for q in range(d.nq):
            at = j * d.group + q * d.width
            sent[odd * d.nq + q] = (base[tick - 1, q].astype(F32) - total[:, at : at + d.width]).astype(BF)


def merge_kernel(d, face_ref, own, other, sent):
    parity = lax.rem(face_ref[0], 2)
    for q in range(d.nq):
        sent[parity * d.nq + q] = own[q]
        sent[(1 - parity) * d.nq + q] = other[q]


def output_kernel(d, ticks, face_ref, fields, coupled, *rest):
    *arrived, out, held, sems = rest
    w = d.width
    face = face_ref[0]
    each = 2 * len(chip_hops(d.faces))
    copies = []
    arrived = arrived[len(arrived) % each :]
    part = 2 * w
    for i, t in enumerate(ticks):
        blocks = []
        if t:
            mine, arrived = arrived[:each], arrived[each:]
            blocks = list(arrived_blocks(d, face, mine[: each // 2], mine[each // 2 :]))
        for c in range(0, d.count * w, part):
            total = jnp.zeros((d.sources, part), F32)
            for x, start in blocks:
                total += dot_nn(x, coupled[pl.ds(start, 2 * d.group), c : c + part])
            for j in range(0, part, w):
                value = fields[(c + j) // w, t * d.sources : (t + 1) * d.sources, :].astype(F32)
                held[i, :, c + j : c + j + w] = (value - total[:, j : j + w]).astype(BF)
            here = held.at[i, :, c : c + part]
            copies.append(pltpu.make_async_copy(here, out.at[t, :, c : c + part], sems.at[len(copies)]))
            copies[-1].start()
    for copy in copies:
        copy.wait()


def call(body, name, smem, inputs, outs, scratch=(), flops=0, anywhere=(), sems=0, place=pltpu.VMEM, aliases=None):
    outs = [x if isinstance(x, jax.ShapeDtypeStruct) else jax.ShapeDtypeStruct(x, BF) for x in outs]
    specs = [pl.BlockSpec(memory_space=pl.ANY if i in anywhere else pltpu.VMEM) for i in range(len(inputs))]
    return pl.pallas_call(
        body,
        name=name,
        out_shape=outs,
        in_specs=[pl.BlockSpec(memory_space=pltpu.SMEM)] * len(smem) + specs,
        out_specs=[pl.BlockSpec(memory_space=place if x.dtype != jnp.int32 else pltpu.SMEM) for x in outs],
        scratch_shapes=[pltpu.VMEM(s, BF) for s in scratch] + ([pltpu.SemaphoreType.DMA((sems,))] if sems else []),
        input_output_aliases=aliases or {},
        compiler_params=pltpu.CompilerParams(vmem_limit_bytes=32 * 1024 * 1024),
        cost_estimate=pl.CostEstimate(flops=flops, bytes_accessed=0, transcendentals=0),
    )(*smem, *inputs)


def on_device(rhs, inflow, diag_tiles, off_tiles, cols, inverse_tiles, coupling, iface):
    faces, slabs = lax.axis_size("face"), lax.axis_size("slab")
    ticks, _, sources, _ = rhs.shape
    _, count, neigh, width, _ = off_tiles.shape
    nq = coupling.shape[1]
    d = Dims(ticks, sources, count, neigh, width, nq, faces)
    diag, off, inv, couple, cols = diag_tiles[0], off_tiles[0], inverse_tiles[0], coupling[0], cols[0].T
    face = lax.axis_index("face").astype(jnp.int32)[None]
    tile = width * width

    pairing = [(i, i ^ 1) for i in range(faces) if i ^ 1 < faces]
    crossing = [(i, ((i + 1) ^ 1) - 1) for i in range(faces) if 0 <= ((i + 1) ^ 1) - 1 < faces]

    def exchange(pair, cross):
        got = lax.ppermute(cross, "face", crossing)
        return lax.ppermute(pair, "face", pairing), got

    def swap(block):
        return lax.ppermute(block, "face", pairing)

    def onward(block, beside=lambda: None):
        own = []
        for hops in chip_hops(faces):
            route = []
            for s in range(1, slabs):
                for f in range(faces):
                    hop = hops[f % 2]
                    g = -1 if hop is None else hop_face(faces, f, hop)
                    if 0 <= g < faces:
                        route.append(((s - 1) * faces + g, s * faces + f))
            own.append(lax.ppermute(block, ("slab", "face"), route))
        made = beside()
        if made is not None:
            *own, made = lax.optimization_barrier((*own, made))
        return own + [swap(x) for x in own], made

    batch, group, ext, wide = d.batch, d.group, d.ext, d.wide
    sweep_flops = 2 * count * tile * (neigh + 1)
    ints = [jax.ShapeDtypeStruct(x.shape, x.dtype) for x in (iface, cols)]
    on_hbm = (iface, cols, inflow[0], couple, inv, rhs[:, 0], diag, off)
    field, gfield, pair, cross, inv, diag, off, iface, cols = call(
        functools.partial(first_kernel, d),
        "first",
        [face],
        [pltpu.with_memory_space_constraint(x, pltpu.HBM) for x in on_hbm],
        [(count, batch, width), (nq, width, width)] + [(HALO, d.first_rows, width)] * 2 + [x.shape for x in (inv, diag, off)] + ints,
        [(ticks, sources, count * width), (sources, group), (nq, width, width)],
        flops=2 * batch * count * tile,
        anywhere=range(8),
        sems=7 + ticks,
    )
    pair0, cross0 = exchange(pair, cross)
    folded, met = call(
        functools.partial(fold_kernel, d),
        "fold",
        [face, iface, cols],
        [inv, diag, off],
        [(count, d.depth, width), (2 * HALO + nq, width, count * width)],
        flops=width * sweep_flops // 64,
    )
    edges, pair, cross, ext0 = call(
        functools.partial(second_edges_kernel, d),
        "second_edges",
        [face, cols],
        [field, pair0, cross0, folded],
        [(2 * HALO, batch, width)] + [(HALO, batch, width)] * 2 + [(ext, batch, width)],
        flops=batch * sweep_flops // 64,
    )
    pair1, cross1 = exchange(pair, cross)
    gfirst, gpair, gcross = call(
        functools.partial(coupling_first_kernel, d),
        "coupling_first",
        [face, iface],
        [gfield, pair0, cross0, met, pair1],
        [(count, wide, width)] + [(HALO, 3 * group, width)] * 2,
        flops=2 * (2 * HALO + nq) * width * count * tile,
        anywhere=(4,),
    )
    gpair1, gcross1 = exchange(gpair, gcross)
    (inner,) = call(
        functools.partial(second_inner_kernel, d),
        "second_inner",
        [face, cols],
        [field, ext0, folded, gfirst],
        [(count - 2 * HALO, batch, width)],
        flops=0,
        anywhere=(3,),
    )
    cross1, inner = lax.optimization_barrier((cross1, inner))
    (own_first,) = call(
        functools.partial(third_rows_kernel, d),
        "third_rows",
        [face, iface, cols],
        [edges, inner, field, pair1, cross1, folded],
        [(nq, sources, width)],
        [(ext, sources, width)],
        flops=batch * sweep_flops * 5 // 2,
    )
    (sent,) = call(
        functools.partial(merge_kernel, d),
        "merge",
        [face],
        [own_first, swap(own_first)],
        [(2 * nq, sources, width)],
    )

    def beside_first():
        rows = call(
            functools.partial(interface_kernel, d),
            "interface",
            [face, iface, cols],
            [edges, inner, field, pair1, cross1, folded, gfield, gfirst, gpair1, gcross1, sent],
            [(d.part, group)] * d.parts + [(ticks - 2, nq, sources, width)],
            [(ext, wide, width), (ext, (ticks - 2) * sources, width)],
            anywhere=(10,),
        )
        other_rows = [swap(x) for x in rows[: d.parts]]
        (twice,) = call(
            functools.partial(third_kernel, d),
            "third",
            [face, cols],
            [edges, inner, field, pair1, cross1, folded, rows[0]],
            [(count, batch, width)],
            [(ext, batch, width)],
            anywhere=(6,),
        )
        return rows, other_rows, twice

    arrived, (rows, other_chain, twice) = onward(sent, beside_first)
    *chain, faces_out = rows
    other_faces = swap(faces_out)
    whole = (ticks, sources, count * width)

    def operator():
        return call(
            functools.partial(coupling_last_kernel, d),
            "coupling_last",
            [face, iface, cols],
            [gfield, gfirst, gpair1, gcross1, folded, chain[0]],
            [(wide, count * width)],
            [(ext, wide, width)],
            flops=wide * sweep_flops,
            anywhere=(5,),
        )[0]

    def output(which, blocks, earlier):
        return call(
            functools.partial(output_kernel, d, which),
            "output",
            [face],
            [twice, coupled] + earlier + blocks,
            [whole],
            [(len(which), sources, count * width)],
            flops=2 * len(which) * sources * wide * count * width,
            anywhere=(2,) if earlier else (),
            sems=len(which) * count,
            place=pl.ANY,
            aliases={3: 0} if earlier else None,
        )[0]

    everything = []
    coupled = most = None
    for tick in range(1, ticks):
        everything += arrived
        if tick == ticks - 1:
            break
        (sent,) = call(
            functools.partial(chain_kernel, d, tick),
            "chain",
            [face],
            [*chain, *other_chain, faces_out, other_faces] + arrived,
            [(2 * nq, sources, width)],
            [(wide, 2 * group)],
            flops=4 * sources * wide * group,
        )
        if tick == 1:
            arrived, coupled = onward(sent, operator)
        else:
            arrived, most = onward(sent, lambda: output(tuple(range(ticks - 1)), everything, []))
    out = output((ticks - 1,), arrived, [most])
    return out[:, None]


def solution(mesh):
    placed = (
        P(None, "slab", None, "face"),
        P("slab", None, "face"),
        P("slab", "face", None, None),
        P("slab", "face", None, None, None),
        P("slab", "face", None),
        P("slab", "face", None, None),
        P("slab", "face", None, None),
        P("face"),
    )
    return jax.shard_map(
        on_device,
        mesh=mesh,
        in_specs=placed,
        out_specs=P(None, "slab", None, "face"),
        check_vma=False,
    )
```

```python
import functools
import math

import jax
import jax.numpy as jnp
from jax import lax
from jax.experimental import pallas as pl
from jax.experimental.pallas import tpu as pltpu
from jax.sharding import PartitionSpec as P

HALO = 2
BF = jnp.bfloat16
F32 = jnp.float32


def dot_nt(a, b):
    return lax.dot_general(a, b, (((1,), (1,)), ((), ())), preferred_element_type=F32)


def dot_nn(a, b):
    return lax.dot_general(a, b, (((1,), (0,)), ((), ())), preferred_element_type=F32)


class Dims:
    def __init__(self, ticks, sources, count, neigh, width, nq, faces):
        self.ticks, self.sources, self.count, self.neigh = ticks, sources, count, neigh
        self.width, self.nq, self.faces = width, nq, faces
        self.split = max(ticks // 2, 1)
        self.early, self.later = self.split * sources, (ticks - self.split) * sources
        self.group = nq * width
        self.ext = count + 2 * HALO
        self.depth = (1 + neigh) * width
        self.slots = 4 if faces <= 4 else 6
        self.wide = self.slots * self.group
        self.parts = 4 if self.slots % 4 == 0 else 3
        self.part = self.wide // self.parts
        self.mark = 16
        self.share = -(-nq // HALO) * width
        self.first_rows = self.later + self.share + nq * self.mark
        self.last = count - HALO
        self.up = count + HALO

    def start(self, face):
        return pl.multiple_of(lax.rem(face + 2 * self.slots, self.slots) * self.group, self.group)

    def first_col(self, face):
        return face * self.count - HALO


def spans(rows):
    parts = -(-rows // 256)
    return [pl.ds(i * (rows // parts), rows // parts) for i in range(parts)]


def edge_rows(d, parity):
    return d.last * (1 - parity), d.last * parity


def first_kernel(
    d, face_ref, iface_hbm, cols_hbm, inflow, coupling, inv, rhs, diag_hbm, off_hbm, *rest
):
    early, later, gfield, *buffers, tiles, diag, off, iface, cols, right, flow, couple, sems = rest
    w = d.width
    moves = [(iface_hbm, iface), (inflow, flow), (coupling, couple), (inv, tiles)]
    moves += [(rhs.at[t], right.at[t]) for t in range(d.ticks)]
    moves += [(cols_hbm, cols), (diag_hbm, diag), (off_hbm, off)]
    copies = [pltpu.make_async_copy(a, b, sems.at[i]) for i, (a, b) in enumerate(moves)]
    for copy in copies:
        copy.start()
    for copy in copies[:4]:
        copy.wait()
    coupled = []
    for q in range(d.nq):
        turned = couple[q].astype(F32).T.astype(BF)
        gfield[q] = dot_nt(turned, tiles[iface[q]]).astype(BF)
        coupled.append(dot_nn(flow[:, q * w : (q + 1) * w], turned))
    for copy in copies[4 : 4 + d.ticks]:
        copy.wait()
    for r in range(d.count):
        x = jnp.concatenate([right[t, :, r * w : (r + 1) * w] for t in range(d.ticks)], axis=0)
        value = dot_nt(x, tiles[r]).astype(BF)
        early[r] = value[: d.early]
        later[r] = value[d.early :]
    for q in range(d.nq):
        row = iface[q]
        corrected = right[0, :, pl.ds(pl.multiple_of(row * w, w), w)].astype(F32) - coupled[q]
        early[row, 0 : d.sources, :] = dot_nt(corrected.astype(BF), tiles[row]).astype(BF)
    for i, start in enumerate(edge_rows(d, lax.rem(face_ref[0], 2))):
        buffers[i][...] = early[pl.ds(start, HALO)]
        buffer = buffers[2 + i]
        buffer[:, 0 : d.later, :] = later[pl.ds(start, HALO)]
        for q in range(d.nq):
            at = d.later + q // HALO * w
            buffer[q % HALO, at : at + w, :] = gfield[q]
            at = d.later + d.share + q * d.mark
            for e in range(HALO):
                buffer[e, at : at + d.mark, :] = jnp.full((d.mark, w), iface[q] == start + e).astype(F32).astype(BF)
    for copy in copies[4 + d.ticks :]:
        copy.wait()


def fold_kernel(d, face_ref, iface, cols, inv, diag, off, folded, met):
    w = d.width
    for r in range(d.count):
        tiles = jnp.concatenate([diag[r]] + [off[r, k] for k in range(d.neigh)], axis=1)
        product = dot_nn(inv[r], tiles)
        rows = lax.broadcasted_iota(jnp.int32, (w, w), 0)
        unit = (rows == lax.broadcasted_iota(jnp.int32, (w, w), 1)).astype(F32)
        for k in range(1 + d.neigh):
            part = product[:, k * w : (k + 1) * w].T
            folded[r, k * w : (k + 1) * w, :] = ((unit if k == 0 else 0.0) - part).astype(BF)
    met[...] = jnp.zeros_like(met)
    for r in range(d.count):
        lanes = slice(r * w, (r + 1) * w)
        for q in range(d.nq):
            met[2 * HALO + q, :, lanes] = jnp.where(iface[q] == r, folded[r, 0:w, :], jnp.zeros((w, w), BF))
        for k in range(d.neigh):
            c = cols[k, r] - d.first_col(face_ref[0])
            inside = jnp.logical_and(c >= HALO, c < d.up)
            at = jnp.where(c < HALO, c, c - d.count)
            hit = jnp.logical_not(inside)
            for q in range(d.nq):
                here = c == iface[q] + HALO
                at = jnp.where(here, 2 * HALO + q, at)
                hit = jnp.logical_or(hit, here)

            @pl.when(hit)
            def _():
                met[at, :, lanes] += folded[r, (1 + k) * w : (2 + k) * w, :]


def sweep(d, cols, face, ext, span, r, folded):
    x = [ext[r + HALO, span, :]] + [ext[cols[k, r] - d.first_col(face), span, :] for k in range(d.neigh)]
    return dot_nn(jnp.concatenate(x, axis=1), folded[r])


def place_halo(d, face, pair_in, cross_in, ext, rows):
    parity = lax.rem(face, 2)
    ext[pl.ds(d.up * (1 - parity), HALO)] = pair_in[:, rows, :]
    ext[pl.ds(d.up * parity, HALO)] = cross_in[:, rows, :]


def extend(d, face, edges, inner, pair_in, cross_in, ext, rows):
    ext[HALO : 2 * HALO] = edges[0:HALO, rows, :]
    ext[2 * HALO : d.count] = inner[:, rows, :]
    ext[d.count : d.up] = edges[HALO : 2 * HALO, rows, :]
    place_halo(d, face, pair_in, cross_in, ext, rows)


def correct(d, cols, face, base, folded, out, ext, rows):
    for i, r in enumerate(rows):
        for span in spans(out.shape[1]):
            value = base[r, span, :].astype(F32) + sweep(d, cols, face, ext, span, r, folded)
            out[i, span, :] = value.astype(BF)


def correct_edges(d, cols, face, field, pair_in, cross_in, folded, edges, ext):
    ext[HALO : HALO + d.count] = field[...]
    place_halo(d, face, pair_in, cross_in, ext, pl.ds(0, field.shape[1]))
    correct(d, cols, face, field, folded, edges, ext, list(range(HALO)) + list(range(d.last, d.count)))


def second_edges_kernel(d, face_ref, cols, field, pair_in, cross_in, folded, edges, pair, cross, ext):
    face = face_ref[0]
    parity = lax.rem(face, 2)
    correct_edges(d, cols, face, field, pair_in, cross_in, folded, edges, ext)
    pair[...] = edges[pl.ds(HALO * (1 - parity), HALO)]
    cross[...] = edges[pl.ds(HALO * parity, HALO)]


def second_inner_kernel(d, face_ref, cols, field, ext, folded, after, out):
    correct(d, cols, face_ref[0], field, folded, out, ext, range(HALO, d.last))


def interface_rows(d, face, iface, cols, edges, inner, field, pair_in, cross_in, folded, first, outs, ext):
    ticks = pl.ds(first * d.sources, len(outs) * d.sources)
    extend(d, face, edges, inner, pair_in, cross_in, ext, ticks)
    for q in range(d.nq):
        row = iface[q]
        value = sweep(d, cols, face, ext, pl.ds(0, len(outs) * d.sources), row, folded)
        value = (field[row, ticks, :].astype(F32) + value).astype(BF)
        for t, out in enumerate(outs):
            out[q] = value[t * d.sources : (t + 1) * d.sources]


def third_rows_kernel(d, face_ref, iface, cols, edges, inner, field, pair_in, cross_in, folded, sent, ext):
    interface_rows(d, face_ref[0], iface, cols, edges, inner, field, pair_in, cross_in, folded, 0, [sent], ext)


def third_kernel(d, face_ref, cols, *rest):
    *inputs, folded, after, early, later, early_ext, later_ext = rest
    face = face_ref[0]
    for i, (out, ext) in enumerate(((early, early_ext), (later, later_ext))):
        edges, inner, field, pair_in, cross_in = inputs[5 * i : 5 * i + 5]
        extend(d, face, edges, inner, pair_in, cross_in, ext, pl.ds(0, out.shape[1]))
        correct(d, cols, face, field, folded, out, ext, range(d.count))


def marked(d, block, e):
    parts = []
    for q in range(d.nq):
        at = d.later + q // HALO * d.width
        mark = d.later + d.share + q * d.mark
        mark = block[e, mark : mark + d.mark, :]
        parts.append(block[q % HALO, at : at + d.width, :] * jnp.concatenate([mark] * (d.width // d.mark), axis=0))
    return jnp.concatenate(parts, axis=0)


def behind_kernel(
    d, face_ref, iface, cols, field, gfield, pair_in, cross_in, met, folded, after, edges, out, pair, cross, field_ext
):
    face = face_ref[0]
    parity = lax.rem(face, 2)
    correct_edges(d, cols, face, field, pair_in, cross_in, folded, edges, field_ext)
    pair[:, 0 : d.later, :] = edges[pl.ds(HALO * (1 - parity), HALO)]
    cross[:, 0 : d.later, :] = edges[pl.ds(HALO * parity, HALO)]
    w = d.width
    for shift in range(2, d.slots - 1):
        out[:, pl.ds(d.start(face + shift), d.group), :] = jnp.zeros((d.count, d.group, w), BF)

    def put(start, rows, value):
        for r in range(d.count):
            out[r, pl.ds(start, rows), :] = value[:, r * w : (r + 1) * w].astype(BF)

    pair_face, cross_face = face + 1 - 2 * parity, face - 1 + 2 * parity
    for at, other, block in ((HALO * (1 - parity), pair_face, pair_in), (HALO * parity, cross_face, cross_in)):
        x = jnp.concatenate([marked(d, block, e) for e in range(HALO)], axis=1)
        tiles = jnp.concatenate([met[at + e] for e in range(HALO)], axis=0)
        put(d.start(other), d.group, dot_nn(x, tiles))
    for q in range(d.nq):
        start = d.start(face) + q * w
        put(start, w, dot_nn(gfield[q], met[2 * HALO + q]))
        row = iface[q]
        span = pl.ds(pl.multiple_of(start, w), w)
        out[row, span, :] = (out[row, span, :].astype(F32) + gfield[q].astype(F32)).astype(BF)
    for start, buffer in zip(edge_rows(d, parity), (pair, cross)):
        for i, shift in enumerate((-1, 0, 1)):
            at = d.later + i * d.group
            buffer[:, at : at + d.group, :] = out[pl.ds(start, HALO), pl.ds(d.start(face + shift), d.group), :]


def coupling_ext(d, face, gfirst, pair_in, cross_in, ext):
    parity = lax.rem(face, 2)
    ext[0:HALO] = jnp.zeros((HALO, d.wide, d.width), BF)
    ext[d.up : d.ext] = jnp.zeros((HALO, d.wide, d.width), BF)
    ext[HALO : HALO + d.count] = gfirst[...]
    neighbours = ((d.up * (1 - parity), face + 1 - 2 * parity, pair_in), (d.up * parity, face - 1 + 2 * parity, cross_in))
    for start, other, block in neighbours:
        for i, shift in enumerate((-1, 0, 1)):
            at = d.later + i * d.group
            ext[pl.ds(start, HALO), pl.ds(d.start(other + shift), d.group), :] = block[:, at : at + d.group, :]


def interface_kernel(d, face_ref, iface, cols, *rest):
    early, (edges, field, field_ext, pair_in, cross_in, folded, gfield, gfirst, after) = rest[:5], rest[5:14]
    chain, (faces_out, inner, ext, small) = rest[14 : 14 + d.parts], rest[14 + d.parts :]
    face = face_ref[0]
    w = d.width
    correct(d, cols, face, field, folded, inner, field_ext, range(HALO, d.last))
    later = (edges, inner, field, pair_in, cross_in)
    for group, first, last, shift in ((early, 1, d.split, 0), (later, d.split, d.ticks - 1, d.split)):
        outs = [faces_out.at[t - 1] for t in range(first, last)]
        if outs:
            held = small.at[:, pl.ds(0, len(outs) * d.sources), :]
            interface_rows(d, face, iface, cols, *group, folded, first - shift, outs, held)
    coupling_ext(d, face, gfirst, pair_in, cross_in, ext)
    for i in range(d.slots):
        start = i * d.group % d.part
        part = chain[i * d.group // d.part]
        for q in range(d.nq):
            value = sweep(d, cols, face, ext, pl.ds(i * d.group, d.group), iface[q], folded)
            part[start : start + d.group, q * w : (q + 1) * w] = value.astype(BF)

        @pl.when(lax.rem(face, d.slots) == i)
        def _():
            for q in range(d.nq):
                block = (slice(start + q * w, start + (q + 1) * w), slice(q * w, (q + 1) * w))
                part[block] = (part[block].astype(F32) + gfield[q].astype(F32)).astype(BF)


def coupling_last_kernel(d, face_ref, iface, cols, gfield, gfirst, pair_in, cross_in, folded, after, out, ext):
    face = face_ref[0]
    w = d.width
    coupling_ext(d, face, gfirst, pair_in, cross_in, ext)
    for r in range(d.count):
        for s in range(0, d.wide, d.group):
            span = pl.ds(s, d.group)
            out[span, r * w : (r + 1) * w] = sweep(d, cols, face, ext, span, r, folded).astype(BF)
    for q in range(d.nq):
        lane = pl.ds(pl.multiple_of(iface[q] * w, w), w)
        span = pl.ds(pl.multiple_of(d.start(face) + q * w, w), w)
        out[span, lane] = (out[span, lane].astype(F32) + gfield[q].astype(F32)).astype(BF)


def chip_hops(faces):
    return [(0, None)] if faces <= 2 else [(0, 1)] if faces <= 4 else [(0, 1), (-1, None)]


def hop_face(faces, face, hop):
    return face ^ (2 * hop) if faces <= 4 else face + 2 * hop


def arrived_blocks(d, face, own, other):
    parity = lax.rem(face, 2)
    for i, hops in enumerate(chip_hops(d.faces)):
        starts = [0 if hop is None else d.start(hop_face(d.faces, face - parity, hop)) for hop in hops]
        for block, odd in ((own[i], parity), (other[i], 1 - parity)):
            start = pl.multiple_of(jnp.where(odd == 1, starts[1], starts[0]), d.group)
            yield jnp.concatenate([block[j] for j in range(2 * d.nq)], axis=1), start


def chain_kernel(d, tick, face_ref, *rest):
    own_chain, other_chain, rest = rest[: d.parts], rest[d.parts : 2 * d.parts], rest[2 * d.parts :]
    own_faces, other_faces, *arrived, sent, chain = rest
    face = face_ref[0]
    parity = lax.rem(face, 2)
    for i in range(d.parts):
        for j, part in enumerate((own_chain[i], other_chain[i])):
            chain[i * d.part : (i + 1) * d.part, j * d.group : (j + 1) * d.group] = part[...]
    half = len(arrived) // 2
    total = jnp.zeros((d.sources, 2 * d.group), F32)
    for x, start in arrived_blocks(d, face, arrived[:half], arrived[half:]):
        total += dot_nn(x, chain[pl.ds(start, 2 * d.group), :])
    for j, (base, odd) in enumerate(((own_faces, parity), (other_faces, 1 - parity))):
        for q in range(d.nq):
            at = j * d.group + q * d.width
            sent[odd * d.nq + q] = (base[tick - 1, q].astype(F32) - total[:, at : at + d.width]).astype(BF)


def merge_kernel(d, face_ref, own, other, sent):
    parity = lax.rem(face_ref[0], 2)
    for q in range(d.nq):
        sent[parity * d.nq + q] = own[q]
        sent[(1 - parity) * d.nq + q] = other[q]


def output_kernel(d, ticks, face_ref, early, later, coupled, *rest):
    *arrived, out, held, sems = rest
    w = d.width
    face = face_ref[0]
    each = 2 * len(chip_hops(d.faces))
    copies = []
    arrived = arrived[len(arrived) % each :]
    part = 2 * w
    for i, t in enumerate(ticks):
        blocks = []
        if t:
            mine, arrived = arrived[:each], arrived[each:]
            blocks = list(arrived_blocks(d, face, mine[: each // 2], mine[each // 2 :]))
        for c in range(0, d.count * w, part):
            total = jnp.zeros((d.sources, part), F32)
            for x, start in blocks:
                total += dot_nn(x, coupled[pl.ds(start, 2 * d.group), c : c + part])
            for j in range(0, part, w):
                fields, at = (early, t) if t < d.split else (later, t - d.split)
                value = fields[(c + j) // w, at * d.sources : (at + 1) * d.sources, :].astype(F32)
                held[i, :, c + j : c + j + w] = (value - total[:, j : j + w]).astype(BF)
            here = held.at[i, :, c : c + part]
            copies.append(pltpu.make_async_copy(here, out.at[t, :, c : c + part], sems.at[len(copies)]))
            copies[-1].start()
    for copy in copies:
        copy.wait()


def call(body, name, smem, inputs, outs, scratch=(), flops=0, anywhere=(), sems=0, place=pltpu.VMEM, aliases=None):
    outs = [x if isinstance(x, jax.ShapeDtypeStruct) else jax.ShapeDtypeStruct(x, BF) for x in outs]
    specs = [pl.BlockSpec(memory_space=pl.ANY if i in anywhere else pltpu.VMEM) for i in range(len(inputs))]
    return pl.pallas_call(
        body,
        name=name,
        out_shape=outs,
        in_specs=[pl.BlockSpec(memory_space=pltpu.SMEM)] * len(smem) + specs,
        out_specs=[pl.BlockSpec(memory_space=place if x.dtype != jnp.int32 else pltpu.SMEM) for x in outs],
        scratch_shapes=[pltpu.VMEM(s, BF) for s in scratch] + ([pltpu.SemaphoreType.DMA((sems,))] if sems else []),
        input_output_aliases=aliases or {},
        compiler_params=pltpu.CompilerParams(vmem_limit_bytes=32 * 1024 * 1024),
        cost_estimate=pl.CostEstimate(flops=flops, bytes_accessed=0, transcendentals=0),
    )(*smem, *inputs)


def on_device(rhs, inflow, diag_tiles, off_tiles, cols, inverse_tiles, coupling, iface):
    faces, slabs = lax.axis_size("face"), lax.axis_size("slab")
    ticks, _, sources, _ = rhs.shape
    _, count, neigh, width, _ = off_tiles.shape
    nq = coupling.shape[1]
    d = Dims(ticks, sources, count, neigh, width, nq, faces)
    diag, off, inv, couple, cols = diag_tiles[0], off_tiles[0], inverse_tiles[0], coupling[0], cols[0].T
    face = lax.axis_index("face").astype(jnp.int32)[None]
    tile = width * width

    pairing = [(i, i ^ 1) for i in range(faces) if i ^ 1 < faces]
    crossing = [(i, ((i + 1) ^ 1) - 1) for i in range(faces) if 0 <= ((i + 1) ^ 1) - 1 < faces]

    def exchange(pair, cross):
        got = lax.ppermute(cross, "face", crossing)
        return lax.ppermute(pair, "face", pairing), got

    def swap(block):
        return lax.ppermute(block, "face", pairing)

    def onward(block, beside=lambda: None):
        own = []
        for hops in chip_hops(faces):
            route = []
            for s in range(1, slabs):
                for f in range(faces):
                    hop = hops[f % 2]
                    g = -1 if hop is None else hop_face(faces, f, hop)
                    if 0 <= g < faces:
                        route.append(((s - 1) * faces + g, s * faces + f))
            own.append(lax.ppermute(block, ("slab", "face"), route))
        made = beside()
        if made is not None:
            *own, made = lax.optimization_barrier((*own, made))
        return own + [swap(x) for x in own], made

    early, later, group, ext, wide = d.early, d.later, d.group, d.ext, d.wide
    sweep_flops = 2 * count * tile * (neigh + 1)
    ints = [jax.ShapeDtypeStruct(x.shape, x.dtype) for x in (iface, cols)]
    on_hbm = (iface, cols, inflow[0], couple, inv, rhs[:, 0], diag, off)
    field, field_later, gfield, pair, cross, pair_later, cross_later, inv, diag, off, iface, cols = call(
        functools.partial(first_kernel, d),
        "first",
        [face],
        [pltpu.with_memory_space_constraint(x, pltpu.HBM) for x in on_hbm],
        [(count, early, width), (count, later, width), (nq, width, width)]
        + [(HALO, early, width)] * 2
        + [(HALO, d.first_rows, width)] * 2
        + [x.shape for x in (inv, diag, off)]
        + ints,
        [(ticks, sources, count * width), (sources, group), (nq, width, width)],
        anywhere=range(8),
        sems=7 + ticks,
    )
    pair0, cross0 = exchange(pair, cross)
    pair_later0, cross_later0 = exchange(pair_later, cross_later)
    folded, met = call(
        functools.partial(fold_kernel, d),
        "fold",
        [face, iface, cols],
        [inv, diag, off],
        [(count, d.depth, width), (2 * HALO + nq, width, count * width)],
    )
    edges, pair, cross, ext0 = call(
        functools.partial(second_edges_kernel, d),
        "second_edges",
        [face, cols],
        [field, pair0, cross0, folded],
        [(2 * HALO, early, width)] + [(HALO, early, width)] * 2 + [(ext, early, width)],
    )
    pair1, cross1 = exchange(pair, cross)
    edges_later, gfirst, pair, cross, ext_later0 = call(
        functools.partial(behind_kernel, d),
        "behind",
        [face, iface, cols],
        [field_later, gfield, pair_later0, cross_later0, met, folded, pair1],
        [(2 * HALO, later, width), (count, wide, width)] + [(HALO, later + 3 * group, width)] * 2 + [(ext, later, width)],
        anywhere=(6,),
    )
    pair_later1, cross_later1 = exchange(pair, cross)
    (inner,) = call(
        functools.partial(second_inner_kernel, d),
        "second_inner",
        [face, cols],
        [field, ext0, folded, gfirst],
        [(count - 2 * HALO, early, width)],
        anywhere=(3,),
    )
    cross1, inner = lax.optimization_barrier((cross1, inner))
    early_parts = (edges, inner, field, pair1, cross1)
    (own_first,) = call(
        functools.partial(third_rows_kernel, d),
        "third_rows",
        [face, iface, cols],
        [*early_parts, folded],
        [(nq, sources, width)],
        [(ext, sources, width)],
        flops=12 * early * sweep_flops,
    )
    (sent,) = call(
        functools.partial(merge_kernel, d),
        "merge",
        [face],
        [own_first, swap(own_first)],
        [(2 * nq, sources, width)],
    )

    def beside_first():
        *rows, faces_out, inner_later = call(
            functools.partial(interface_kernel, d),
            "interface",
            [face, iface, cols],
            [*early_parts, edges_later, field_later, ext_later0, pair_later1, cross_later1, folded, gfield, gfirst, sent],
            [(d.part, group)] * d.parts + [(ticks - 2, nq, sources, width), (count - 2 * HALO, later, width)],
            [(ext, wide, width), (ext, max(early, later), width)],
            anywhere=(13,),
        )
        return rows, [swap(x) for x in rows], faces_out, inner_later

    arrived, (chain, other_chain, faces_out, inner_later) = onward(sent, beside_first)
    other_faces = swap(faces_out)

    def fields(after):
        return call(
            functools.partial(third_kernel, d),
            "third",
            [face, cols],
            [*early_parts, edges_later, inner_later, field_later, pair_later1, cross_later1, folded, after],
            [(count, early, width), (count, later, width)],
            [(ext, early, width), (ext, later, width)],
            anywhere=(11,),
        )

    whole = (ticks, sources, count * width)

    def operator():
        return call(
            functools.partial(coupling_last_kernel, d),
            "coupling_last",
            [face, iface, cols],
            [gfield, gfirst, pair_later1, cross_later1, folded, chain[0]],
            [(wide, count * width)],
            [(ext, wide, width)],
            flops=wide * sweep_flops,
            anywhere=(5,),
        )[0]

    def output(which, blocks, earlier):
        return call(
            functools.partial(output_kernel, d, which),
            "output",
            [face],
            [*twice, coupled] + earlier + blocks,
            [whole],
            [(len(which), sources, count * width)],
            flops=2 * len(which) * sources * wide * count * width,
            anywhere=(3,) if earlier else (),
            sems=len(which) * count,
            place=pl.ANY,
            aliases={4: 0} if earlier else None,
        )[0]

    everything = []
    coupled = most = None
    for tick in range(1, ticks):
        everything += arrived
        if tick == ticks - 1:
            break
        (sent,) = call(
            functools.partial(chain_kernel, d, tick),
            "chain",
            [face],
            [*chain, *other_chain, faces_out, other_faces] + arrived,
            [(2 * nq, sources, width)],
            [(wide, 2 * group)],
            flops=4 * sources * wide * group,
        )
        if tick == 1:
            arrived, coupled = onward(sent, operator)
        else:
            twice = fields(sent)
            arrived, most = onward(sent, lambda: output(tuple(range(ticks - 1)), everything, []))
    out = output((ticks - 1,), arrived, [most])
    return out[:, None]


def solution(mesh):
    placed = (
        P(None, "slab", None, "face"),
        P("slab", None, "face"),
        P("slab", "face", None, None),
        P("slab", "face", None, None, None),
        P("slab", "face", None),
        P("slab", "face", None, None),
        P("slab", "face", None, None),
        P("face"),
    )
    return jax.shard_map(
        on_device,
        mesh=mesh,
        in_specs=placed,
        out_specs=P(None, "slab", None, "face"),
        check_vma=False,
    )
```

```python
import functools
import math

import jax
import jax.numpy as jnp
from jax import lax
from jax.experimental import pallas as pl
from jax.experimental.pallas import tpu as pltpu
from jax.sharding import PartitionSpec as P

HALO = 2
BF = jnp.bfloat16
F32 = jnp.float32


def dot_nt(a, b):
    return lax.dot_general(a, b, (((1,), (1,)), ((), ())), preferred_element_type=F32)


def dot_nn(a, b):
    return lax.dot_general(a, b, (((1,), (0,)), ((), ())), preferred_element_type=F32)


class Dims:
    def __init__(self, ticks, sources, count, neigh, width, nq, faces):
        self.ticks, self.sources, self.count, self.neigh = ticks, sources, count, neigh
        self.width, self.nq, self.faces = width, nq, faces
        self.split = max(ticks // 2, 1)
        self.early, self.later = self.split * sources, (ticks - self.split) * sources
        self.group = nq * width
        self.ext = count + 2 * HALO
        self.depth = (1 + neigh) * width
        self.slots = 4 if faces <= 4 else 6
        self.wide = self.slots * self.group
        self.parts = 4 if self.slots % 4 == 0 else 3
        self.part = self.wide // self.parts
        self.mark = 16
        self.share = -(-nq // HALO) * width
        self.first_rows = self.later + self.share + nq * self.mark
        self.last = count - HALO
        self.up = count + HALO

    def start(self, face):
        return pl.multiple_of(lax.rem(face + 2 * self.slots, self.slots) * self.group, self.group)

    def first_col(self, face):
        return face * self.count - HALO


def spans(rows):
    parts = -(-rows // 256)
    return [pl.ds(i * (rows // parts), rows // parts) for i in range(parts)]


def edge_rows(d, parity):
    return d.last * (1 - parity), d.last * parity


def first_kernel(
    d, face_ref, iface_hbm, cols_hbm, inflow, coupling, inv, rhs, diag_hbm, off_hbm, *rest
):
    early, later, gfield, *buffers, tiles, diag, off, iface, cols, right, flow, couple, sems = rest
    w = d.width
    moves = [(iface_hbm, iface), (inflow, flow), (coupling, couple), (inv, tiles)]
    moves += [(rhs.at[t], right.at[t]) for t in range(d.ticks)]
    moves += [(cols_hbm, cols), (diag_hbm, diag), (off_hbm, off)]
    copies = [pltpu.make_async_copy(a, b, sems.at[i]) for i, (a, b) in enumerate(moves)]
    for copy in copies:
        copy.start()
    for copy in copies[:4]:
        copy.wait()
    coupled = []
    for q in range(d.nq):
        turned = couple[q].astype(F32).T.astype(BF)
        gfield[q] = dot_nt(turned, tiles[iface[q]]).astype(BF)
        coupled.append(dot_nn(flow[:, q * w : (q + 1) * w], turned))
    for copy in copies[4 : 4 + d.ticks]:
        copy.wait()
    for r in range(d.count):
        x = jnp.concatenate([right[t, :, r * w : (r + 1) * w] for t in range(d.ticks)], axis=0)
        value = dot_nt(x, tiles[r]).astype(BF)
        early[r] = value[: d.early]
        later[r] = value[d.early :]
    for q in range(d.nq):
        row = iface[q]
        corrected = right[0, :, pl.ds(pl.multiple_of(row * w, w), w)].astype(F32) - coupled[q]
        early[row, 0 : d.sources, :] = dot_nt(corrected.astype(BF), tiles[row]).astype(BF)
    for i, start in enumerate(edge_rows(d, lax.rem(face_ref[0], 2))):
        buffers[i][...] = early[pl.ds(start, HALO)]
        buffer = buffers[2 + i]
        buffer[:, 0 : d.later, :] = later[pl.ds(start, HALO)]
        for q in range(d.nq):
            at = d.later + q // HALO * w
            buffer[q % HALO, at : at + w, :] = gfield[q]
            at = d.later + d.share + q * d.mark
            for e in range(HALO):
                buffer[e, at : at + d.mark, :] = jnp.full((d.mark, w), iface[q] == start + e).astype(F32).astype(BF)
    for copy in copies[4 + d.ticks :]:
        copy.wait()


def fold_kernel(d, face_ref, iface, cols, inv, diag, off, folded, met):
    w = d.width
    for r in range(d.count):
        tiles = jnp.concatenate([diag[r]] + [off[r, k] for k in range(d.neigh)], axis=1)
        product = dot_nn(inv[r], tiles)
        rows = lax.broadcasted_iota(jnp.int32, (w, w), 0)
        unit = (rows == lax.broadcasted_iota(jnp.int32, (w, w), 1)).astype(F32)
        for k in range(1 + d.neigh):
            part = product[:, k * w : (k + 1) * w].T
            folded[r, k * w : (k + 1) * w, :] = ((unit if k == 0 else 0.0) - part).astype(BF)
    met[...] = jnp.zeros_like(met)
    for r in range(d.count):
        lanes = slice(r * w, (r + 1) * w)
        for q in range(d.nq):
            met[2 * HALO + q, :, lanes] = jnp.where(iface[q] == r, folded[r, 0:w, :], jnp.zeros((w, w), BF))
        for k in range(d.neigh):
            c = cols[k, r] - d.first_col(face_ref[0])
            inside = jnp.logical_and(c >= HALO, c < d.up)
            at = jnp.where(c < HALO, c, c - d.count)
            hit = jnp.logical_not(inside)
            for q in range(d.nq):
                here = c == iface[q] + HALO
                at = jnp.where(here, 2 * HALO + q, at)
                hit = jnp.logical_or(hit, here)

            @pl.when(hit)
            def _():
                met[at, :, lanes] += folded[r, (1 + k) * w : (2 + k) * w, :]


def sweep(d, cols, face, ext, span, r, folded):
    x = [ext[r + HALO, span, :]] + [ext[cols[k, r] - d.first_col(face), span, :] for k in range(d.neigh)]
    return dot_nn(jnp.concatenate(x, axis=1), folded[r])


def place_halo(d, face, pair_in, cross_in, ext, rows):
    parity = lax.rem(face, 2)
    ext[pl.ds(d.up * (1 - parity), HALO)] = pair_in[:, rows, :]
    ext[pl.ds(d.up * parity, HALO)] = cross_in[:, rows, :]


def extend(d, face, edges, inner, pair_in, cross_in, ext, rows):
    ext[HALO : 2 * HALO] = edges[0:HALO, rows, :]
    ext[2 * HALO : d.count] = inner[:, rows, :]
    ext[d.count : d.up] = edges[HALO : 2 * HALO, rows, :]
    place_halo(d, face, pair_in, cross_in, ext, rows)


def correct(d, cols, face, base, folded, out, ext, rows):
    for i, r in enumerate(rows):
        for span in spans(out.shape[1]):
            value = base[r, span, :].astype(F32) + sweep(d, cols, face, ext, span, r, folded)
            out[i, span, :] = value.astype(BF)


def correct_edges(d, cols, face, field, pair_in, cross_in, folded, edges, ext):
    ext[HALO : HALO + d.count] = field[...]
    place_halo(d, face, pair_in, cross_in, ext, pl.ds(0, field.shape[1]))
    correct(d, cols, face, field, folded, edges, ext, list(range(HALO)) + list(range(d.last, d.count)))


def second_edges_kernel(d, face_ref, cols, field, pair_in, cross_in, folded, edges, pair, cross, ext):
    face = face_ref[0]
    parity = lax.rem(face, 2)
    correct_edges(d, cols, face, field, pair_in, cross_in, folded, edges, ext)
    pair[...] = edges[pl.ds(HALO * (1 - parity), HALO)]
    cross[...] = edges[pl.ds(HALO * parity, HALO)]


def second_inner_kernel(d, face_ref, cols, field, ext, folded, after, out):
    correct(d, cols, face_ref[0], field, folded, out, ext, range(HALO, d.last))


def interface_rows(d, face, iface, cols, edges, inner, field, pair_in, cross_in, folded, first, outs, ext):
    ticks = pl.ds(first * d.sources, len(outs) * d.sources)
    extend(d, face, edges, inner, pair_in, cross_in, ext, ticks)
    for q in range(d.nq):
        row = iface[q]
        value = sweep(d, cols, face, ext, pl.ds(0, len(outs) * d.sources), row, folded)
        value = (field[row, ticks, :].astype(F32) + value).astype(BF)
        for t, out in enumerate(outs):
            out[q] = value[t * d.sources : (t + 1) * d.sources]


def third_rows_kernel(d, face_ref, iface, cols, edges, inner, field, pair_in, cross_in, folded, sent, ext):
    interface_rows(d, face_ref[0], iface, cols, edges, inner, field, pair_in, cross_in, folded, 0, [sent], ext)


def third_kernel(d, face_ref, cols, *rest):
    *inputs, folded, after, early, later, early_ext, later_ext = rest
    face = face_ref[0]
    for i, (out, ext) in enumerate(((early, early_ext), (later, later_ext))):
        edges, inner, field, pair_in, cross_in = inputs[5 * i : 5 * i + 5]
        extend(d, face, edges, inner, pair_in, cross_in, ext, pl.ds(0, out.shape[1]))
        correct(d, cols, face, field, folded, out, ext, range(d.count))


def marked(d, block, e):
    parts = []
    for q in range(d.nq):
        at = d.later + q // HALO * d.width
        mark = d.later + d.share + q * d.mark
        mark = block[e, mark : mark + d.mark, :]
        parts.append(block[q % HALO, at : at + d.width, :] * jnp.concatenate([mark] * (d.width // d.mark), axis=0))
    return jnp.concatenate(parts, axis=0)


def behind_kernel(
    d, face_ref, iface, cols, field, gfield, pair_in, cross_in, met, folded, after, edges, out, pair, cross, field_ext
):
    face = face_ref[0]
    parity = lax.rem(face, 2)
    correct_edges(d, cols, face, field, pair_in, cross_in, folded, edges, field_ext)
    pair[:, 0 : d.later, :] = edges[pl.ds(HALO * (1 - parity), HALO)]
    cross[:, 0 : d.later, :] = edges[pl.ds(HALO * parity, HALO)]
    w = d.width
    for shift in range(2, d.slots - 1):
        out[:, pl.ds(d.start(face + shift), d.group), :] = jnp.zeros((d.count, d.group, w), BF)

    def put(start, rows, value):
        for r in range(d.count):
            out[r, pl.ds(start, rows), :] = value[:, r * w : (r + 1) * w].astype(BF)

    pair_face, cross_face = face + 1 - 2 * parity, face - 1 + 2 * parity
    for at, other, block in ((HALO * (1 - parity), pair_face, pair_in), (HALO * parity, cross_face, cross_in)):
        x = jnp.concatenate([marked(d, block, e) for e in range(HALO)], axis=1)
        tiles = jnp.concatenate([met[at + e] for e in range(HALO)], axis=0)
        put(d.start(other), d.group, dot_nn(x, tiles))
    for q in range(d.nq):
        start = d.start(face) + q * w
        put(start, w, dot_nn(gfield[q], met[2 * HALO + q]))
        row = iface[q]
        span = pl.ds(pl.multiple_of(start, w), w)
        out[row, span, :] = (out[row, span, :].astype(F32) + gfield[q].astype(F32)).astype(BF)
    for start, buffer in zip(edge_rows(d, parity), (pair, cross)):
        for i, shift in enumerate((-1, 0, 1)):
            at = d.later + i * d.group
            buffer[:, at : at + d.group, :] = out[pl.ds(start, HALO), pl.ds(d.start(face + shift), d.group), :]


def coupling_ext(d, face, gfirst, pair_in, cross_in, ext):
    parity = lax.rem(face, 2)
    ext[0:HALO] = jnp.zeros((HALO, d.wide, d.width), BF)
    ext[d.up : d.ext] = jnp.zeros((HALO, d.wide, d.width), BF)
    ext[HALO : HALO + d.count] = gfirst[...]
    neighbours = ((d.up * (1 - parity), face + 1 - 2 * parity, pair_in), (d.up * parity, face - 1 + 2 * parity, cross_in))
    for start, other, block in neighbours:
        for i, shift in enumerate((-1, 0, 1)):
            at = d.later + i * d.group
            ext[pl.ds(start, HALO), pl.ds(d.start(other + shift), d.group), :] = block[:, at : at + d.group, :]


def interface_kernel(d, face_ref, iface, cols, *rest):
    early, (edges, field, field_ext, pair_in, cross_in, folded, gfield, gfirst, after) = rest[:5], rest[5:14]
    chain, (faces_out, inner, ext, small) = rest[14 : 14 + d.parts], rest[14 + d.parts :]
    face = face_ref[0]
    w = d.width
    correct(d, cols, face, field, folded, inner, field_ext, range(HALO, d.last))
    later = (edges, inner, field, pair_in, cross_in)
    for group, first, last, shift in ((early, 1, d.split, 0), (later, d.split, d.ticks - 1, d.split)):
        outs = [faces_out.at[t - 1] for t in range(first, last)]
        if outs:
            held = small.at[:, pl.ds(0, len(outs) * d.sources), :]
            interface_rows(d, face, iface, cols, *group, folded, first - shift, outs, held)
    coupling_ext(d, face, gfirst, pair_in, cross_in, ext)
    for i in range(d.slots):
        start = i * d.group % d.part
        part = chain[i * d.group // d.part]
        for q in range(d.nq):
            value = sweep(d, cols, face, ext, pl.ds(i * d.group, d.group), iface[q], folded)
            part[start : start + d.group, q * w : (q + 1) * w] = value.astype(BF)

        @pl.when(lax.rem(face, d.slots) == i)
        def _():
            for q in range(d.nq):
                block = (slice(start + q * w, start + (q + 1) * w), slice(q * w, (q + 1) * w))
                part[block] = (part[block].astype(F32) + gfield[q].astype(F32)).astype(BF)


def coupling_last_kernel(d, face_ref, iface, cols, gfield, gfirst, pair_in, cross_in, folded, after, out, ext):
    face = face_ref[0]
    w = d.width
    coupling_ext(d, face, gfirst, pair_in, cross_in, ext)
    for r in range(d.count):
        for s in range(0, d.wide, d.group):
            span = pl.ds(s, d.group)
            out[span, r * w : (r + 1) * w] = sweep(d, cols, face, ext, span, r, folded).astype(BF)
    for q in range(d.nq):
        lane = pl.ds(pl.multiple_of(iface[q] * w, w), w)
        span = pl.ds(pl.multiple_of(d.start(face) + q * w, w), w)
        out[span, lane] = (out[span, lane].astype(F32) + gfield[q].astype(F32)).astype(BF)


def chip_hops(faces):
    return [(0, None)] if faces <= 2 else [(0, 1)] if faces <= 4 else [(0, 1), (-1, None)]


def hop_face(faces, face, hop):
    return face ^ (2 * hop) if faces <= 4 else face + 2 * hop


def arrived_blocks(d, face, own, other):
    parity = lax.rem(face, 2)
    for i, hops in enumerate(chip_hops(d.faces)):
        starts = [0 if hop is None else d.start(hop_face(d.faces, face - parity, hop)) for hop in hops]
        for block, odd in ((own[i], parity), (other[i], 1 - parity)):
            start = pl.multiple_of(jnp.where(odd == 1, starts[1], starts[0]), d.group)
            yield jnp.concatenate([block[j] for j in range(2 * d.nq)], axis=1), start


def chain_kernel(d, tick, face_ref, *rest):
    own_chain, other_chain, rest = rest[: d.parts], rest[d.parts : 2 * d.parts], rest[2 * d.parts :]
    own_faces, other_faces, *arrived, sent, chain = rest
    face = face_ref[0]
    parity = lax.rem(face, 2)
    for i in range(d.parts):
        for j, part in enumerate((own_chain[i], other_chain[i])):
            chain[i * d.part : (i + 1) * d.part, j * d.group : (j + 1) * d.group] = part[...]
    half = len(arrived) // 2
    total = jnp.zeros((d.sources, 2 * d.group), F32)
    for x, start in arrived_blocks(d, face, arrived[:half], arrived[half:]):
        total += dot_nn(x, chain[pl.ds(start, 2 * d.group), :])
    for j, (base, odd) in enumerate(((own_faces, parity), (other_faces, 1 - parity))):
        for q in range(d.nq):
            at = j * d.group + q * d.width
            sent[odd * d.nq + q] = (base[tick - 1, q].astype(F32) - total[:, at : at + d.width]).astype(BF)


def merge_kernel(d, face_ref, own, other, sent):
    parity = lax.rem(face_ref[0], 2)
    for q in range(d.nq):
        sent[parity * d.nq + q] = own[q]
        sent[(1 - parity) * d.nq + q] = other[q]


def tick_rows(d, early, later, tick, row):
    fields, at = (early, tick) if tick < d.split else (later, tick - d.split)
    return fields[row, at * d.sources : (at + 1) * d.sources, :].astype(F32)


def output_kernel(d, face_ref, early, later, coupled, *rest):
    *arrived, out, held, sems = rest
    w = d.width
    each = 2 * len(chip_hops(d.faces))
    copies = []
    part = 2 * w
    for t in range(d.ticks - 1):
        blocks = []
        if t:
            mine, arrived = arrived[:each], arrived[each:]
            blocks = list(arrived_blocks(d, face_ref[0], mine[: each // 2], mine[each // 2 :]))
        for c in range(0, d.count * w, part):
            total = jnp.zeros((d.sources, part), F32)
            for x, start in blocks:
                total += dot_nn(x, coupled[pl.ds(start, 2 * d.group), c : c + part])
            for j in range(0, part, w):
                value = tick_rows(d, early, later, t, (c + j) // w) - total[:, j : j + w]
                held[t, :, c + j : c + j + w] = value.astype(BF)
        copies.append(pltpu.make_async_copy(held.at[t], out.at[t], sems.at[t]))
        copies[-1].start()
    for copy in copies:
        copy.wait()


def last_own_kernel(d, face_ref, early, later, coupled, *rest):
    own, out = rest[:-1], rest[-1]
    w = d.width
    total = jnp.zeros((d.sources, d.count * w), F32)
    for x, start in list(arrived_blocks(d, face_ref[0], own, own))[0::2]:
        total += dot_nn(x, coupled[pl.ds(start, 2 * d.group), :])
    for r in range(d.count):
        out[:, r * w : (r + 1) * w] = tick_rows(d, early, later, d.ticks - 1, r) - total[:, r * w : (r + 1) * w]


def last_other_kernel(d, face_ref, own_part, coupled, earlier, *rest):
    other, (out, held, sems) = rest[:-3], rest[-3:]
    blocks = list(arrived_blocks(d, face_ref[0], other, other))[1::2]
    part = 2 * d.width
    copies = []
    for i, c in enumerate(range(0, d.count * d.width, part)):
        total = own_part[:, c : c + part]
        for x, start in blocks:
            total -= dot_nn(x, coupled[pl.ds(start, 2 * d.group), c : c + part])
        held[:, c : c + part] = total.astype(BF)
        here = held.at[:, c : c + part]
        copies.append(pltpu.make_async_copy(here, out.at[d.ticks - 1, :, c : c + part], sems.at[i]))
        copies[-1].start()
    for copy in copies:
        copy.wait()


def call(body, name, smem, inputs, outs, scratch=(), flops=0, anywhere=(), sems=0, place=pltpu.VMEM, aliases=None):
    outs = [x if isinstance(x, jax.ShapeDtypeStruct) else jax.ShapeDtypeStruct(x, BF) for x in outs]
    specs = [pl.BlockSpec(memory_space=pl.ANY if i in anywhere else pltpu.VMEM) for i in range(len(inputs))]
    return pl.pallas_call(
        body,
        name=name,
        out_shape=outs,
        in_specs=[pl.BlockSpec(memory_space=pltpu.SMEM)] * len(smem) + specs,
        out_specs=[pl.BlockSpec(memory_space=place if x.dtype != jnp.int32 else pltpu.SMEM) for x in outs],
        scratch_shapes=[pltpu.VMEM(s, BF) for s in scratch] + ([pltpu.SemaphoreType.DMA((sems,))] if sems else []),
        input_output_aliases=aliases or {},
        compiler_params=pltpu.CompilerParams(vmem_limit_bytes=32 * 1024 * 1024),
        cost_estimate=pl.CostEstimate(flops=flops, bytes_accessed=0, transcendentals=0),
    )(*smem, *inputs)


def on_device(rhs, inflow, diag_tiles, off_tiles, cols, inverse_tiles, coupling, iface):
    faces, slabs = lax.axis_size("face"), lax.axis_size("slab")
    ticks, _, sources, _ = rhs.shape
    _, count, neigh, width, _ = off_tiles.shape
    nq = coupling.shape[1]
    d = Dims(ticks, sources, count, neigh, width, nq, faces)
    diag, off, inv, couple, cols = diag_tiles[0], off_tiles[0], inverse_tiles[0], coupling[0], cols[0].T
    face = lax.axis_index("face").astype(jnp.int32)[None]
    tile = width * width

    pairing = [(i, i ^ 1) for i in range(faces) if i ^ 1 < faces]
    crossing = [(i, ((i + 1) ^ 1) - 1) for i in range(faces) if 0 <= ((i + 1) ^ 1) - 1 < faces]

    def exchange(pair, cross):
        got = lax.ppermute(cross, "face", crossing)
        return lax.ppermute(pair, "face", pairing), got

    def swap(block):
        return lax.ppermute(block, "face", pairing)

    def onward(block, beside=lambda: None):
        own = []
        for hops in chip_hops(faces):
            route = []
            for s in range(1, slabs):
                for f in range(faces):
                    hop = hops[f % 2]
                    g = -1 if hop is None else hop_face(faces, f, hop)
                    if 0 <= g < faces:
                        route.append(((s - 1) * faces + g, s * faces + f))
            own.append(lax.ppermute(block, ("slab", "face"), route))
        made = beside()
        if made is not None:
            *own, made = lax.optimization_barrier((*own, made))
        return own + [swap(x) for x in own], made

    early, later, group, ext, wide = d.early, d.later, d.group, d.ext, d.wide
    sweep_flops = 2 * count * tile * (neigh + 1)
    ints = [jax.ShapeDtypeStruct(x.shape, x.dtype) for x in (iface, cols)]
    on_hbm = (iface, cols, inflow[0], couple, inv, rhs[:, 0], diag, off)
    field, field_later, gfield, pair, cross, pair_later, cross_later, inv, diag, off, iface, cols = call(
        functools.partial(first_kernel, d),
        "first",
        [face],
        [pltpu.with_memory_space_constraint(x, pltpu.HBM) for x in on_hbm],
        [(count, early, width), (count, later, width), (nq, width, width)]
        + [(HALO, early, width)] * 2
        + [(HALO, d.first_rows, width)] * 2
        + [x.shape for x in (inv, diag, off)]
        + ints,
        [(ticks, sources, count * width), (sources, group), (nq, width, width)],
        anywhere=range(8),
        sems=7 + ticks,
    )
    pair0, cross0 = exchange(pair, cross)
    folded, met = call(
        functools.partial(fold_kernel, d),
        "fold",
        [face, iface, cols],
        [inv, diag, off],
        [(count, d.depth, width), (2 * HALO + nq, width, count * width)],
    )
    pair_later, cross_later, folded = lax.optimization_barrier((pair_later, cross_later, folded))
    pair_later0, cross_later0 = exchange(pair_later, cross_later)
    edges, pair, cross, ext0 = call(
        functools.partial(second_edges_kernel, d),
        "second_edges",
        [face, cols],
        [field, pair0, cross0, folded],
        [(2 * HALO, early, width)] + [(HALO, early, width)] * 2 + [(ext, early, width)],
        flops=12 * early * sweep_flops,
    )
    pair1, cross1 = exchange(pair, cross)
    edges_later, gfirst, pair, cross, ext_later0 = call(
        functools.partial(behind_kernel, d),
        "behind",
        [face, iface, cols],
        [field_later, gfield, pair_later0, cross_later0, met, folded, pair1],
        [(2 * HALO, later, width), (count, wide, width)] + [(HALO, later + 3 * group, width)] * 2 + [(ext, later, width)],
        anywhere=(6,),
    )
    (inner,) = call(
        functools.partial(second_inner_kernel, d),
        "second_inner",
        [face, cols],
        [field, ext0, folded, gfirst],
        [(count - 2 * HALO, early, width)],
        anywhere=(3,),
    )
    pair, cross, inner = lax.optimization_barrier((pair, cross, inner))
    pair_later1, cross_later1 = exchange(pair, cross)
    early_parts = (edges, inner, field, pair1, cross1)
    (own_first,) = call(
        functools.partial(third_rows_kernel, d),
        "third_rows",
        [face, iface, cols],
        [*early_parts, folded],
        [(nq, sources, width)],
        [(ext, sources, width)],
        flops=12 * early * sweep_flops,
    )
    (sent,) = call(
        functools.partial(merge_kernel, d),
        "merge",
        [face],
        [own_first, swap(own_first)],
        [(2 * nq, sources, width)],
    )

    def beside_first():
        *rows, faces_out, inner_later = call(
            functools.partial(interface_kernel, d),
            "interface",
            [face, iface, cols],
            [*early_parts, edges_later, field_later, ext_later0, pair_later1, cross_later1, folded, gfield, gfirst, sent],
            [(d.part, group)] * d.parts + [(ticks - 2, nq, sources, width), (count - 2 * HALO, later, width)],
            [(ext, wide, width), (ext, max(early, later), width)],
            anywhere=(13,),
        )
        return rows, [swap(x) for x in rows], faces_out, inner_later

    arrived, (chain, other_chain, faces_out, inner_later) = onward(sent, beside_first)
    other_faces = swap(faces_out)

    def fields(after):
        return call(
            functools.partial(third_kernel, d),
            "third",
            [face, cols],
            [*early_parts, edges_later, inner_later, field_later, pair_later1, cross_later1, folded, after],
            [(count, early, width), (count, later, width)],
            [(ext, early, width), (ext, later, width)],
            anywhere=(11,),
        )

    whole = (ticks, sources, count * width)

    def operator():
        return call(
            functools.partial(coupling_last_kernel, d),
            "coupling_last",
            [face, iface, cols],
            [gfield, gfirst, pair_later1, cross_later1, folded, chain[0]],
            [(wide, count * width)],
            [(ext, wide, width)],
            flops=wide * sweep_flops,
            anywhere=(5,),
        )[0]

    def output(blocks):
        return call(
            functools.partial(output_kernel, d),
            "output",
            [face],
            [*twice, coupled] + blocks,
            [whole],
            [(ticks - 1, sources, count * width)],
            sems=ticks - 1,
            place=pl.ANY,
        )[0]

    everything = []
    coupled = most = None
    for tick in range(1, ticks):
        everything += arrived
        if tick == ticks - 1:
            break
        (sent,) = call(
            functools.partial(chain_kernel, d, tick),
            "chain",
            [face],
            [*chain, *other_chain, faces_out, other_faces] + arrived,
            [(2 * nq, sources, width)],
            [(wide, 2 * group)],
            flops=4 * sources * wide * group,
        )
        if tick == 1:
            arrived, coupled = onward(sent, operator)
        else:
            twice = fields(sent)
            arrived, most = onward(sent, lambda: output(everything))
    half = len(arrived) // 2
    (own_part,) = call(
        functools.partial(last_own_kernel, d),
        "last_own",
        [face],
        [*twice, coupled] + arrived[:half],
        [jax.ShapeDtypeStruct((sources, count * width), F32)],
    )
    (out,) = call(
        functools.partial(last_other_kernel, d),
        "last_other",
        [face],
        [own_part, coupled, most] + arrived[half:],
        [whole],
        [(sources, count * width)],
        anywhere=(2,),
        sems=count,
        place=pl.ANY,
        aliases={3: 0},
    )
    return out[:, None]


def solution(mesh):
    placed = (
        P(None, "slab", None, "face"),
        P("slab", None, "face"),
        P("slab", "face", None, None),
        P("slab", "face", None, None, None),
        P("slab", "face", None),
        P("slab", "face", None, None),
        P("slab", "face", None, None),
        P("face"),
    )
    return jax.shard_map(
        on_device,
        mesh=mesh,
        in_specs=placed,
        out_specs=P(None, "slab", None, "face"),
        check_vma=False,
    )
```

```python
import functools
import math

import jax
import jax.numpy as jnp
from jax import lax
from jax.experimental import pallas as pl
from jax.experimental.pallas import tpu as pltpu
from jax.sharding import PartitionSpec as P

HALO = 2
BF = jnp.bfloat16
F32 = jnp.float32


def dot_nt(a, b):
    return lax.dot_general(a, b, (((1,), (1,)), ((), ())), preferred_element_type=F32)


def dot_nn(a, b):
    return lax.dot_general(a, b, (((1,), (0,)), ((), ())), preferred_element_type=F32)


class Dims:
    def __init__(self, ticks, sources, count, neigh, width, nq, faces):
        self.ticks, self.sources, self.count, self.neigh = ticks, sources, count, neigh
        self.width, self.nq, self.faces = width, nq, faces
        self.split = max(ticks // 2, 1)
        self.early, self.later = self.split * sources, (ticks - self.split) * sources
        self.group = nq * width
        self.ext = count + 2 * HALO
        self.depth = (1 + neigh) * width
        self.slots = 4 if faces <= 4 else 6
        self.wide = self.slots * self.group
        self.parts = 4 if self.slots % 4 == 0 else 3
        self.part = self.wide // self.parts
        self.mark = 16
        self.share = -(-nq // HALO) * width
        self.first_rows = self.later + self.share + nq * self.mark
        self.last = count - HALO
        self.up = count + HALO

    def start(self, face):
        return pl.multiple_of(lax.rem(face + 2 * self.slots, self.slots) * self.group, self.group)

    def first_col(self, face):
        return face * self.count - HALO


def spans(rows):
    parts = -(-rows // 256)
    return [pl.ds(i * (rows // parts), rows // parts) for i in range(parts)]


def edge_rows(d, parity):
    return d.last * (1 - parity), d.last * parity


def first_kernel(
    d, face_ref, iface_hbm, cols_hbm, inflow, coupling, inv, rhs, diag_hbm, off_hbm, *rest
):
    early, later, gfield, *buffers, tiles, diag, off, iface, cols, right, flow, couple, sems = rest
    w = d.width
    moves = [(iface_hbm, iface), (inflow, flow), (coupling, couple), (inv, tiles)]
    moves += [(rhs.at[t], right.at[t]) for t in range(d.ticks)]
    moves += [(cols_hbm, cols), (diag_hbm, diag), (off_hbm, off)]
    copies = [pltpu.make_async_copy(a, b, sems.at[i]) for i, (a, b) in enumerate(moves)]
    for copy in copies:
        copy.start()
    for copy in copies[:4]:
        copy.wait()
    coupled = []
    for q in range(d.nq):
        turned = couple[q].astype(F32).T.astype(BF)
        gfield[q] = dot_nt(turned, tiles[iface[q]]).astype(BF)
        coupled.append(dot_nn(flow[:, q * w : (q + 1) * w], turned))
    for copy in copies[4 : 4 + d.ticks]:
        copy.wait()
    for r in range(d.count):
        x = jnp.concatenate([right[t, :, r * w : (r + 1) * w] for t in range(d.ticks)], axis=0)
        value = dot_nt(x, tiles[r]).astype(BF)
        early[r] = value[: d.early]
        later[r] = value[d.early :]
    for q in range(d.nq):
        row = iface[q]
        corrected = right[0, :, pl.ds(pl.multiple_of(row * w, w), w)].astype(F32) - coupled[q]
        early[row, 0 : d.sources, :] = dot_nt(corrected.astype(BF), tiles[row]).astype(BF)
    for i, start in enumerate(edge_rows(d, lax.rem(face_ref[0], 2))):
        buffers[i][...] = early[pl.ds(start, HALO)]
        buffer = buffers[2 + i]
        buffer[:, 0 : d.later, :] = later[pl.ds(start, HALO)]
        for q in range(d.nq):
            at = d.later + q // HALO * w
            buffer[q % HALO, at : at + w, :] = gfield[q]
            at = d.later + d.share + q * d.mark
            for e in range(HALO):
                buffer[e, at : at + d.mark, :] = jnp.full((d.mark, w), iface[q] == start + e).astype(F32).astype(BF)
    for copy in copies[4 + d.ticks :]:
        copy.wait()


def fold_kernel(d, face_ref, iface, cols, inv, diag, off, folded, met):
    w = d.width
    for r in range(d.count):
        tiles = jnp.concatenate([diag[r]] + [off[r, k] for k in range(d.neigh)], axis=1)
        product = dot_nn(inv[r], tiles)
        rows = lax.broadcasted_iota(jnp.int32, (w, w), 0)
        unit = (rows == lax.broadcasted_iota(jnp.int32, (w, w), 1)).astype(F32)
        for k in range(1 + d.neigh):
            part = product[:, k * w : (k + 1) * w].T
            folded[r, k * w : (k + 1) * w, :] = ((unit if k == 0 else 0.0) - part).astype(BF)
    met[...] = jnp.zeros_like(met)
    for r in range(d.count):
        lanes = slice(r * w, (r + 1) * w)
        for q in range(d.nq):
            met[2 * HALO + q, :, lanes] = jnp.where(iface[q] == r, folded[r, 0:w, :], jnp.zeros((w, w), BF))
        for k in range(d.neigh):
            c = cols[k, r] - d.first_col(face_ref[0])
            inside = jnp.logical_and(c >= HALO, c < d.up)
            at = jnp.where(c < HALO, c, c - d.count)
            hit = jnp.logical_not(inside)
            for q in range(d.nq):
                here = c == iface[q] + HALO
                at = jnp.where(here, 2 * HALO + q, at)
                hit = jnp.logical_or(hit, here)

            @pl.when(hit)
            def _():
                met[at, :, lanes] += folded[r, (1 + k) * w : (2 + k) * w, :]


def sweep(d, cols, face, ext, span, r, folded):
    x = [ext[r + HALO, span, :]] + [ext[cols[k, r] - d.first_col(face), span, :] for k in range(d.neigh)]
    return dot_nn(jnp.concatenate(x, axis=1), folded[r])


def place_halo(d, face, pair_in, cross_in, ext, rows):
    parity = lax.rem(face, 2)
    ext[pl.ds(d.up * (1 - parity), HALO)] = pair_in[:, rows, :]
    ext[pl.ds(d.up * parity, HALO)] = cross_in[:, rows, :]


def extend(d, face, edges, inner, pair_in, cross_in, ext, rows):
    ext[HALO : 2 * HALO] = edges[0:HALO, rows, :]
    ext[2 * HALO : d.count] = inner[:, rows, :]
    ext[d.count : d.up] = edges[HALO : 2 * HALO, rows, :]
    place_halo(d, face, pair_in, cross_in, ext, rows)


def correct(d, cols, face, base, folded, out, ext, rows):
    for i, r in enumerate(rows):
        for span in spans(out.shape[1]):
            value = base[r, span, :].astype(F32) + sweep(d, cols, face, ext, span, r, folded)
            out[i, span, :] = value.astype(BF)


def correct_edges(d, cols, face, field, pair_in, cross_in, folded, edges, ext):
    ext[HALO : HALO + d.count] = field[...]
    place_halo(d, face, pair_in, cross_in, ext, pl.ds(0, field.shape[1]))
    correct(d, cols, face, field, folded, edges, ext, list(range(HALO)) + list(range(d.last, d.count)))


def second_edges_kernel(d, face_ref, cols, field, pair_in, cross_in, folded, edges, pair, cross, ext):
    face = face_ref[0]
    parity = lax.rem(face, 2)
    correct_edges(d, cols, face, field, pair_in, cross_in, folded, edges, ext)
    pair[...] = edges[pl.ds(HALO * (1 - parity), HALO)]
    cross[...] = edges[pl.ds(HALO * parity, HALO)]


def second_inner_kernel(d, face_ref, cols, field, ext, folded, after, out):
    correct(d, cols, face_ref[0], field, folded, out, ext, range(HALO, d.last))


def interface_rows(d, face, iface, cols, edges, inner, field, pair_in, cross_in, folded, first, outs, ext):
    ticks = pl.ds(first * d.sources, len(outs) * d.sources)
    extend(d, face, edges, inner, pair_in, cross_in, ext, ticks)
    for q in range(d.nq):
        row = iface[q]
        value = sweep(d, cols, face, ext, pl.ds(0, len(outs) * d.sources), row, folded)
        value = (field[row, ticks, :].astype(F32) + value).astype(BF)
        for t, out in enumerate(outs):
            out[q] = value[t * d.sources : (t + 1) * d.sources]


def third_rows_kernel(d, face_ref, iface, cols, edges, inner, field, pair_in, cross_in, folded, sent, ext):
    interface_rows(d, face_ref[0], iface, cols, edges, inner, field, pair_in, cross_in, folded, 0, [sent], ext)


def third_kernel(d, face_ref, cols, *rest):
    *inputs, folded, after, early, later, early_ext, later_ext = rest
    face = face_ref[0]
    for i, (out, ext) in enumerate(((early, early_ext), (later, later_ext))):
        edges, inner, field, pair_in, cross_in = inputs[5 * i : 5 * i + 5]
        extend(d, face, edges, inner, pair_in, cross_in, ext, pl.ds(0, out.shape[1]))
        correct(d, cols, face, field, folded, out, ext, range(d.count))


def marked(d, block, e):
    parts = []
    for q in range(d.nq):
        at = d.later + q // HALO * d.width
        mark = d.later + d.share + q * d.mark
        mark = block[e, mark : mark + d.mark, :]
        parts.append(block[q % HALO, at : at + d.width, :] * jnp.concatenate([mark] * (d.width // d.mark), axis=0))
    return jnp.concatenate(parts, axis=0)


def behind_kernel(
    d, face_ref, iface, cols, field, gfield, pair_in, cross_in, met, folded, after, edges, out, pair, cross, field_ext
):
    face = face_ref[0]
    parity = lax.rem(face, 2)
    correct_edges(d, cols, face, field, pair_in, cross_in, folded, edges, field_ext)
    pair[:, 0 : d.later, :] = edges[pl.ds(HALO * (1 - parity), HALO)]
    cross[:, 0 : d.later, :] = edges[pl.ds(HALO * parity, HALO)]
    w = d.width
    for shift in range(2, d.slots - 1):
        out[:, pl.ds(d.start(face + shift), d.group), :] = jnp.zeros((d.count, d.group, w), BF)

    def put(start, rows, value):
        for r in range(d.count):
            out[r, pl.ds(start, rows), :] = value[:, r * w : (r + 1) * w].astype(BF)

    pair_face, cross_face = face + 1 - 2 * parity, face - 1 + 2 * parity
    for at, other, block in ((HALO * (1 - parity), pair_face, pair_in), (HALO * parity, cross_face, cross_in)):
        x = jnp.concatenate([marked(d, block, e) for e in range(HALO)], axis=1)
        tiles = jnp.concatenate([met[at + e] for e in range(HALO)], axis=0)
        put(d.start(other), d.group, dot_nn(x, tiles))
    for q in range(d.nq):
        start = d.start(face) + q * w
        put(start, w, dot_nn(gfield[q], met[2 * HALO + q]))
        row = iface[q]
        span = pl.ds(pl.multiple_of(start, w), w)
        out[row, span, :] = (out[row, span, :].astype(F32) + gfield[q].astype(F32)).astype(BF)
    for start, buffer in zip(edge_rows(d, parity), (pair, cross)):
        for i, shift in enumerate((-1, 0, 1)):
            at = d.later + i * d.group
            buffer[:, at : at + d.group, :] = out[pl.ds(start, HALO), pl.ds(d.start(face + shift), d.group), :]


def coupling_ext(d, face, gfirst, pair_in, cross_in, ext):
    parity = lax.rem(face, 2)
    ext[0:HALO] = jnp.zeros((HALO, d.wide, d.width), BF)
    ext[d.up : d.ext] = jnp.zeros((HALO, d.wide, d.width), BF)
    ext[HALO : HALO + d.count] = gfirst[...]
    neighbours = ((d.up * (1 - parity), face + 1 - 2 * parity, pair_in), (d.up * parity, face - 1 + 2 * parity, cross_in))
    for start, other, block in neighbours:
        for i, shift in enumerate((-1, 0, 1)):
            at = d.later + i * d.group
            ext[pl.ds(start, HALO), pl.ds(d.start(other + shift), d.group), :] = block[:, at : at + d.group, :]


def second_rest_kernel(d, face_ref, iface, cols, edges, field, ext0, pair_in, cross_in, later, later_ext0, folded, after, *rest):
    inner, inner_later, *faces_out, ext = rest
    face = face_ref[0]
    correct(d, cols, face, field, folded, inner, ext0, range(HALO, d.last))
    correct(d, cols, face, later, folded, inner_later, later_ext0, range(HALO, d.last))
    for out in faces_out:
        outs = [out.at[t] for t in range(d.split - 1)]
        held = ext.at[:, pl.ds(0, len(outs) * d.sources), :]
        interface_rows(d, face, iface, cols, edges, inner, field, pair_in, cross_in, folded, 1, outs, held)


def interface_kernel(d, face_ref, iface, cols, *rest):
    later, (folded, gfield, gfirst) = rest[:5], rest[5:8]
    chain, (faces_out, ext, small) = rest[8 : 8 + d.parts], rest[8 + d.parts :]
    face = face_ref[0]
    w = d.width
    pair_in, cross_in = later[3:]
    outs = [faces_out.at[t] for t in range(d.ticks - 1 - d.split)]
    interface_rows(d, face, iface, cols, *later, folded, 0, outs, small.at[:, pl.ds(0, len(outs) * d.sources), :])
    coupling_ext(d, face, gfirst, pair_in, cross_in, ext)
    for i in range(d.slots):
        start = i * d.group % d.part
        part = chain[i * d.group // d.part]
        for q in range(d.nq):
            value = sweep(d, cols, face, ext, pl.ds(i * d.group, d.group), iface[q], folded)
            part[start : start + d.group, q * w : (q + 1) * w] = value.astype(BF)

        @pl.when(lax.rem(face, d.slots) == i)
        def _():
            for q in range(d.nq):
                block = (slice(start + q * w, start + (q + 1) * w), slice(q * w, (q + 1) * w))
                part[block] = (part[block].astype(F32) + gfield[q].astype(F32)).astype(BF)


def coupling_last_kernel(d, face_ref, iface, cols, gfield, gfirst, pair_in, cross_in, folded, after, out, ext):
    face = face_ref[0]
    w = d.width
    coupling_ext(d, face, gfirst, pair_in, cross_in, ext)
    for r in range(d.count):
        for s in range(0, d.wide, d.group):
            span = pl.ds(s, d.group)
            out[span, r * w : (r + 1) * w] = sweep(d, cols, face, ext, span, r, folded).astype(BF)
    for q in range(d.nq):
        lane = pl.ds(pl.multiple_of(iface[q] * w, w), w)
        span = pl.ds(pl.multiple_of(d.start(face) + q * w, w), w)
        out[span, lane] = (out[span, lane].astype(F32) + gfield[q].astype(F32)).astype(BF)


def chip_hops(faces):
    return [(0, None)] if faces <= 2 else [(0, 1)] if faces <= 4 else [(0, 1), (-1, None)]


def hop_face(faces, face, hop):
    return face ^ (2 * hop) if faces <= 4 else face + 2 * hop


def arrived_blocks(d, face, own, other):
    parity = lax.rem(face, 2)
    for i, hops in enumerate(chip_hops(d.faces)):
        starts = [0 if hop is None else d.start(hop_face(d.faces, face - parity, hop)) for hop in hops]
        for block, odd in ((own[i], parity), (other[i], 1 - parity)):
            start = pl.multiple_of(jnp.where(odd == 1, starts[1], starts[0]), d.group)
            yield jnp.concatenate([block[j] for j in range(2 * d.nq)], axis=1), start


def chain_kernel(d, tick, face_ref, *rest):
    own_chain, other_chain, rest = rest[: d.parts], rest[d.parts : 2 * d.parts], rest[2 * d.parts :]
    own_faces, other_faces, *arrived, sent, chain = rest
    face = face_ref[0]
    parity = lax.rem(face, 2)
    for i in range(d.parts):
        for j, part in enumerate((own_chain[i], other_chain[i])):
            chain[i * d.part : (i + 1) * d.part, j * d.group : (j + 1) * d.group] = part[...]
    half = len(arrived) // 2
    total = jnp.zeros((d.sources, 2 * d.group), F32)
    for x, start in arrived_blocks(d, face, arrived[:half], arrived[half:]):
        total += dot_nn(x, chain[pl.ds(start, 2 * d.group), :])
    for j, (base, odd) in enumerate(((own_faces, parity), (other_faces, 1 - parity))):
        for q in range(d.nq):
            at = j * d.group + q * d.width
            sent[odd * d.nq + q] = (base[tick, q].astype(F32) - total[:, at : at + d.width]).astype(BF)


def merge_kernel(d, face_ref, own, other, sent):
    parity = lax.rem(face_ref[0], 2)
    for q in range(d.nq):
        sent[parity * d.nq + q] = own[q]
        sent[(1 - parity) * d.nq + q] = other[q]


def tick_rows(d, early, later, tick, row):
    fields, at = (early, tick) if tick < d.split else (later, tick - d.split)
    return fields[row, at * d.sources : (at + 1) * d.sources, :].astype(F32)


def output_kernel(d, face_ref, early, later, coupled, *rest):
    *arrived, out, held, sems = rest
    w = d.width
    each = 2 * len(chip_hops(d.faces))
    copies = []
    part = 2 * w
    for t in range(d.ticks - 1):
        blocks = []
        if t:
            mine, arrived = arrived[:each], arrived[each:]
            blocks = list(arrived_blocks(d, face_ref[0], mine[: each // 2], mine[each // 2 :]))
        for c in range(0, d.count * w, part):
            total = jnp.zeros((d.sources, part), F32)
            for x, start in blocks:
                total += dot_nn(x, coupled[pl.ds(start, 2 * d.group), c : c + part])
            for j in range(0, part, w):
                value = tick_rows(d, early, later, t, (c + j) // w) - total[:, j : j + w]
                held[t, :, c + j : c + j + w] = value.astype(BF)
        copies.append(pltpu.make_async_copy(held.at[t], out.at[t], sems.at[t]))
        copies[-1].start()
    for copy in copies:
        copy.wait()


def last_own_kernel(d, face_ref, early, later, coupled, *rest):
    own, out = rest[:-1], rest[-1]
    w = d.width
    total = jnp.zeros((d.sources, d.count * w), F32)
    for x, start in list(arrived_blocks(d, face_ref[0], own, own))[0::2]:
        total += dot_nn(x, coupled[pl.ds(start, 2 * d.group), :])
    for r in range(d.count):
        out[:, r * w : (r + 1) * w] = tick_rows(d, early, later, d.ticks - 1, r) - total[:, r * w : (r + 1) * w]


def last_other_kernel(d, face_ref, own_part, coupled, earlier, *rest):
    other, (out, held, sems) = rest[:-3], rest[-3:]
    blocks = list(arrived_blocks(d, face_ref[0], other, other))[1::2]
    part = 2 * d.width
    copies = []
    for i, c in enumerate(range(0, d.count * d.width, part)):
        total = own_part[:, c : c + part]
        for x, start in blocks:
            total -= dot_nn(x, coupled[pl.ds(start, 2 * d.group), c : c + part])
        held[:, c : c + part] = total.astype(BF)
        here = held.at[:, c : c + part]
        copies.append(pltpu.make_async_copy(here, out.at[d.ticks - 1, :, c : c + part], sems.at[i]))
        copies[-1].start()
    for copy in copies:
        copy.wait()


def call(body, name, smem, inputs, outs, scratch=(), flops=0, anywhere=(), sems=0, place=pltpu.VMEM, aliases=None):
    outs = [x if isinstance(x, jax.ShapeDtypeStruct) else jax.ShapeDtypeStruct(x, BF) for x in outs]
    specs = [pl.BlockSpec(memory_space=pl.ANY if i in anywhere else pltpu.VMEM) for i in range(len(inputs))]
    return pl.pallas_call(
        body,
        name=name,
        out_shape=outs,
        in_specs=[pl.BlockSpec(memory_space=pltpu.SMEM)] * len(smem) + specs,
        out_specs=[pl.BlockSpec(memory_space=place if x.dtype != jnp.int32 else pltpu.SMEM) for x in outs],
        scratch_shapes=[pltpu.VMEM(s, BF) for s in scratch] + ([pltpu.SemaphoreType.DMA((sems,))] if sems else []),
        input_output_aliases=aliases or {},
        compiler_params=pltpu.CompilerParams(vmem_limit_bytes=32 * 1024 * 1024),
        cost_estimate=pl.CostEstimate(flops=flops, bytes_accessed=0, transcendentals=0),
    )(*smem, *inputs)


def on_device(rhs, inflow, diag_tiles, off_tiles, cols, inverse_tiles, coupling, iface):
    faces, slabs = lax.axis_size("face"), lax.axis_size("slab")
    ticks, _, sources, _ = rhs.shape
    _, count, neigh, width, _ = off_tiles.shape
    nq = coupling.shape[1]
    d = Dims(ticks, sources, count, neigh, width, nq, faces)
    diag, off, inv, couple, cols = diag_tiles[0], off_tiles[0], inverse_tiles[0], coupling[0], cols[0].T
    face = lax.axis_index("face").astype(jnp.int32)[None]
    tile = width * width

    pairing = [(i, i ^ 1) for i in range(faces) if i ^ 1 < faces]
    crossing = [(i, ((i + 1) ^ 1) - 1) for i in range(faces) if 0 <= ((i + 1) ^ 1) - 1 < faces]

    def exchange(pair, cross):
        got = lax.ppermute(cross, "face", crossing)
        return lax.ppermute(pair, "face", pairing), got

    def swap(block):
        return lax.ppermute(block, "face", pairing)

    def onward(block, beside=lambda: None):
        own = []
        for hops in chip_hops(faces):
            route = []
            for s in range(1, slabs):
                for f in range(faces):
                    hop = hops[f % 2]
                    g = -1 if hop is None else hop_face(faces, f, hop)
                    if 0 <= g < faces:
                        route.append(((s - 1) * faces + g, s * faces + f))
            own.append(lax.ppermute(block, ("slab", "face"), route))
        made = beside()
        if made is not None:
            *own, made = lax.optimization_barrier((*own, made))
        return own + [swap(x) for x in own], made

    split, early, later, group, ext, wide = d.split, d.early, d.later, d.group, d.ext, d.wide
    sweep_flops = 2 * count * tile * (neigh + 1)
    ints = [jax.ShapeDtypeStruct(x.shape, x.dtype) for x in (iface, cols)]
    on_hbm = (iface, cols, inflow[0], couple, inv, rhs[:, 0], diag, off)
    field, field_later, gfield, pair, cross, pair_later, cross_later, inv, diag, off, iface, cols = call(
        functools.partial(first_kernel, d),
        "first",
        [face],
        [pltpu.with_memory_space_constraint(x, pltpu.HBM) for x in on_hbm],
        [(count, early, width), (count, later, width), (nq, width, width)]
        + [(HALO, early, width)] * 2
        + [(HALO, d.first_rows, width)] * 2
        + [x.shape for x in (inv, diag, off)]
        + ints,
        [(ticks, sources, count * width), (sources, group), (nq, width, width)],
        anywhere=range(8),
        sems=7 + ticks,
    )
    pair0, cross0 = exchange(pair, cross)
    pair_later0, cross_later0 = exchange(pair_later, cross_later)
    folded, met = call(
        functools.partial(fold_kernel, d),
        "fold",
        [face, iface, cols],
        [inv, diag, off],
        [(count, d.depth, width), (2 * HALO + nq, width, count * width)],
    )
    edges, pair, cross, ext0 = call(
        functools.partial(second_edges_kernel, d),
        "second_edges",
        [face, cols],
        [field, pair0, cross0, folded],
        [(2 * HALO, early, width)] + [(HALO, early, width)] * 2 + [(ext, early, width)],
    )
    pair1, cross1 = exchange(pair, cross)
    edges_later, gfirst, pair, cross, ext_later0 = call(
        functools.partial(behind_kernel, d),
        "behind",
        [face, iface, cols],
        [field_later, gfield, pair_later0, cross_later0, met, folded, pair1],
        [(2 * HALO, later, width), (count, wide, width)] + [(HALO, later + 3 * group, width)] * 2 + [(ext, later, width)],
        anywhere=(6,),
    )
    pair_later1, cross_later1 = exchange(pair, cross)
    (inner_first,) = call(
        functools.partial(second_inner_kernel, d),
        "second_inner",
        [face, cols],
        [field, ext0, folded, gfirst],
        [(count - 2 * HALO, sources, width)],
        anywhere=(3,),
    )
    cross1, inner_first = lax.optimization_barrier((cross1, inner_first))
    (own_first,) = call(
        functools.partial(third_rows_kernel, d),
        "third_rows",
        [face, iface, cols],
        [edges, inner_first, field, pair1, cross1, folded],
        [(nq, sources, width)],
        [(ext, sources, width)],
        flops=12 * early * sweep_flops,
    )
    (sent,) = call(
        functools.partial(merge_kernel, d),
        "merge",
        [face],
        [own_first, swap(own_first)],
        [(2 * nq, sources, width)],
    )

    inner, inner_later, *faces_early = call(
        functools.partial(second_rest_kernel, d),
        "second_rest",
        [face, iface, cols],
        [edges, field, ext0, pair1, cross1, field_later, ext_later0, folded, sent],
        [(count - 2 * HALO, early, width), (count - 2 * HALO, later, width)]
        + [(split - 1, nq, sources, width)] * (split > 1),
        [(ext, early, width)],
        anywhere=(8,),
    )
    other_early = [swap(x) for x in faces_early]
    early_parts = (edges, inner, field, pair1, cross1)
    later_parts = (edges_later, inner_later, field_later, pair_later1, cross_later1)

    def beside_first():
        *rows, faces_later = call(
            functools.partial(interface_kernel, d),
            "interface",
            [face, iface, cols],
            [*later_parts, folded, gfield, gfirst],
            [(d.part, group)] * d.parts + [(ticks - 1 - split, nq, sources, width)],
            [(ext, wide, width), (ext, later, width)],
        )
        return rows, [swap(x) for x in rows], faces_later

    arrived, (chain, other_chain, faces_later) = onward(sent, beside_first)

    def fields(after):
        return call(
            functools.partial(third_kernel, d),
            "third",
            [face, cols],
            [*early_parts, *later_parts, folded, after],
            [(count, early, width), (count, later, width)],
            [(ext, early, width), (ext, later, width)],
            anywhere=(11,),
        )

    whole = (ticks, sources, count * width)

    def operator():
        return call(
            functools.partial(coupling_last_kernel, d),
            "coupling_last",
            [face, iface, cols],
            [gfield, gfirst, pair_later1, cross_later1, folded, chain[0]],
            [(wide, count * width)],
            [(ext, wide, width)],
            flops=wide * sweep_flops,
            anywhere=(5,),
        )[0]

    def output(blocks):
        return call(
            functools.partial(output_kernel, d),
            "output",
            [face],
            [*twice, coupled] + blocks,
            [whole],
            [(ticks - 1, sources, count * width)],
            sems=ticks - 1,
            place=pl.ANY,
        )[0]

    everything = []
    coupled = most = None
    for tick in range(1, ticks):
        everything += arrived
        if tick == ticks - 1:
            break
        early_tick = tick < split
        bases = (faces_early[0], other_early[0]) if early_tick else (faces_later, other_later)
        (sent,) = call(
            functools.partial(chain_kernel, d, tick - 1 if early_tick else tick - split),
            "chain",
            [face],
            [*chain, *other_chain, *bases] + arrived,
            [(2 * nq, sources, width)],
            [(wide, 2 * group)],
            flops=4 * sources * wide * group,
        )
        if tick == 1:
            arrived, (coupled, other_later) = onward(sent, lambda: (operator(), swap(faces_later)))
        else:
            twice = fields(sent)
            arrived, most = onward(sent, lambda: output(everything))
    half = len(arrived) // 2
    (own_part,) = call(
        functools.partial(last_own_kernel, d),
        "last_own",
        [face],
        [*twice, coupled] + arrived[:half],
        [jax.ShapeDtypeStruct((sources, count * width), F32)],
    )
    (out,) = call(
        functools.partial(last_other_kernel, d),
        "last_other",
        [face],
        [own_part, coupled, most] + arrived[half:],
        [whole],
        [(sources, count * width)],
        anywhere=(2,),
        sems=count,
        place=pl.ANY,
        aliases={3: 0},
    )
    return out[:, None]


def solution(mesh):
    placed = (
        P(None, "slab", None, "face"),
        P("slab", None, "face"),
        P("slab", "face", None, None),
        P("slab", "face", None, None, None),
        P("slab", "face", None),
        P("slab", "face", None, None),
        P("slab", "face", None, None),
        P("face"),
    )
    return jax.shard_map(
        on_device,
        mesh=mesh,
        in_specs=placed,
        out_specs=P(None, "slab", None, "face"),
        check_vma=False,
    )
```

```python
import functools
import math

import jax
import jax.numpy as jnp
from jax import lax
from jax.experimental import pallas as pl
from jax.experimental.pallas import tpu as pltpu
from jax.sharding import PartitionSpec as P

HALO = 2
BF = jnp.bfloat16
F32 = jnp.float32


def dot_nt(a, b):
    return lax.dot_general(a, b, (((1,), (1,)), ((), ())), preferred_element_type=F32)


def dot_nn(a, b):
    return lax.dot_general(a, b, (((1,), (0,)), ((), ())), preferred_element_type=F32)


class Dims:
    def __init__(self, ticks, sources, count, neigh, width, nq, faces):
        self.ticks, self.sources, self.count, self.neigh = ticks, sources, count, neigh
        self.width, self.nq, self.faces = width, nq, faces
        self.split = max(ticks // 2, 1)
        self.early, self.later = self.split * sources, (ticks - self.split) * sources
        self.group = nq * width
        self.ext = count + 2 * HALO
        self.depth = (1 + neigh) * width
        self.slots = 4 if faces <= 4 else 6
        self.wide = self.slots * self.group
        self.parts = 4 if self.slots % 4 == 0 else 3
        self.part = self.wide // self.parts
        self.mark = 16
        self.share = -(-nq // HALO) * width
        self.first_rows = self.later + self.share + nq * self.mark
        self.last = count - HALO
        self.up = count + HALO

    def start(self, face):
        return pl.multiple_of(lax.rem(face + 2 * self.slots, self.slots) * self.group, self.group)

    def first_col(self, face):
        return face * self.count - HALO


def spans(rows):
    parts = -(-rows // 256)
    return [pl.ds(i * (rows // parts), rows // parts) for i in range(parts)]


def edge_rows(d, parity):
    return d.last * (1 - parity), d.last * parity


def first_kernel(
    d, face_ref, iface_hbm, cols_hbm, inflow, coupling, inv, rhs, diag_hbm, off_hbm, *rest
):
    early, later, gfield, *buffers, tiles, diag, off, iface, cols, right, flow, couple, sems = rest
    w = d.width
    moves = [(iface_hbm, iface), (inflow, flow), (coupling, couple), (inv, tiles)]
    moves += [(rhs.at[t], right.at[t]) for t in range(d.ticks)]
    moves += [(cols_hbm, cols), (diag_hbm, diag), (off_hbm, off)]
    copies = [pltpu.make_async_copy(a, b, sems.at[i]) for i, (a, b) in enumerate(moves)]
    for copy in copies:
        copy.start()
    for copy in copies[:4]:
        copy.wait()
    coupled = []
    for q in range(d.nq):
        turned = couple[q].astype(F32).T.astype(BF)
        gfield[q] = dot_nt(turned, tiles[iface[q]]).astype(BF)
        coupled.append(dot_nn(flow[:, q * w : (q + 1) * w], turned))
    for copy in copies[4 : 4 + d.ticks]:
        copy.wait()
    for r in range(d.count):
        x = jnp.concatenate([right[t, :, r * w : (r + 1) * w] for t in range(d.ticks)], axis=0)
        value = dot_nt(x, tiles[r]).astype(BF)
        early[r] = value[: d.early]
        later[r] = value[d.early :]
    for q in range(d.nq):
        row = iface[q]
        corrected = right[0, :, pl.ds(pl.multiple_of(row * w, w), w)].astype(F32) - coupled[q]
        early[row, 0 : d.sources, :] = dot_nt(corrected.astype(BF), tiles[row]).astype(BF)
    for i, start in enumerate(edge_rows(d, lax.rem(face_ref[0], 2))):
        buffers[i][...] = early[pl.ds(start, HALO)]
        buffer = buffers[2 + i]
        buffer[:, 0 : d.later, :] = later[pl.ds(start, HALO)]
        for q in range(d.nq):
            at = d.later + q // HALO * w
            buffer[q % HALO, at : at + w, :] = gfield[q]
            at = d.later + d.share + q * d.mark
            for e in range(HALO):
                buffer[e, at : at + d.mark, :] = jnp.full((d.mark, w), iface[q] == start + e).astype(F32).astype(BF)
    for copy in copies[4 + d.ticks :]:
        copy.wait()


def fold_kernel(d, face_ref, iface, cols, inv, diag, off, folded, met):
    w = d.width
    for r in range(d.count):
        tiles = jnp.concatenate([diag[r]] + [off[r, k] for k in range(d.neigh)], axis=1)
        product = dot_nn(inv[r], tiles)
        rows = lax.broadcasted_iota(jnp.int32, (w, w), 0)
        unit = (rows == lax.broadcasted_iota(jnp.int32, (w, w), 1)).astype(F32)
        for k in range(1 + d.neigh):
            part = product[:, k * w : (k + 1) * w].T
            folded[r, k * w : (k + 1) * w, :] = ((unit if k == 0 else 0.0) - part).astype(BF)
    met[...] = jnp.zeros_like(met)
    for r in range(d.count):
        lanes = slice(r * w, (r + 1) * w)
        for q in range(d.nq):
            met[2 * HALO + q, :, lanes] = jnp.where(iface[q] == r, folded[r, 0:w, :], jnp.zeros((w, w), BF))
        for k in range(d.neigh):
            c = cols[k, r] - d.first_col(face_ref[0])
            inside = jnp.logical_and(c >= HALO, c < d.up)
            at = jnp.where(c < HALO, c, c - d.count)
            hit = jnp.logical_not(inside)
            for q in range(d.nq):
                here = c == iface[q] + HALO
                at = jnp.where(here, 2 * HALO + q, at)
                hit = jnp.logical_or(hit, here)

            @pl.when(hit)
            def _():
                met[at, :, lanes] += folded[r, (1 + k) * w : (2 + k) * w, :]


def sweep(d, cols, face, ext, span, r, folded):
    x = [ext[r + HALO, span, :]] + [ext[cols[k, r] - d.first_col(face), span, :] for k in range(d.neigh)]
    return dot_nn(jnp.concatenate(x, axis=1), folded[r])


def place_halo(d, face, pair_in, cross_in, ext, rows):
    parity = lax.rem(face, 2)
    ext[pl.ds(d.up * (1 - parity), HALO)] = pair_in[:, rows, :]
    ext[pl.ds(d.up * parity, HALO)] = cross_in[:, rows, :]


def extend(d, face, edges, inner, pair_in, cross_in, ext, rows):
    ext[HALO : 2 * HALO] = edges[0:HALO, rows, :]
    ext[2 * HALO : d.count] = inner[:, rows, :]
    ext[d.count : d.up] = edges[HALO : 2 * HALO, rows, :]
    place_halo(d, face, pair_in, cross_in, ext, rows)


def correct(d, cols, face, base, folded, out, ext, rows):
    for i, r in enumerate(rows):
        for span in spans(out.shape[1]):
            value = base[r, span, :].astype(F32) + sweep(d, cols, face, ext, span, r, folded)
            out[i, span, :] = value.astype(BF)


def correct_edges(d, cols, face, field, pair_in, cross_in, folded, edges, ext):
    ext[HALO : HALO + d.count] = field[...]
    place_halo(d, face, pair_in, cross_in, ext, pl.ds(0, field.shape[1]))
    correct(d, cols, face, field, folded, edges, ext, list(range(HALO)) + list(range(d.last, d.count)))


def second_edges_kernel(d, face_ref, cols, field, pair_in, cross_in, folded, edges, pair, cross, ext):
    face = face_ref[0]
    parity = lax.rem(face, 2)
    correct_edges(d, cols, face, field, pair_in, cross_in, folded, edges, ext)
    pair[...] = edges[pl.ds(HALO * (1 - parity), HALO)]
    cross[...] = edges[pl.ds(HALO * parity, HALO)]


def second_inner_kernel(d, face_ref, cols, field, ext, folded, after, out):
    correct(d, cols, face_ref[0], field, folded, out, ext, range(HALO, d.last))


def interface_rows(d, face, iface, cols, edges, inner, field, pair_in, cross_in, folded, first, outs, ext):
    ticks = pl.ds(first * d.sources, len(outs) * d.sources)
    extend(d, face, edges, inner, pair_in, cross_in, ext, ticks)
    for q in range(d.nq):
        row = iface[q]
        value = sweep(d, cols, face, ext, pl.ds(0, len(outs) * d.sources), row, folded)
        value = (field[row, ticks, :].astype(F32) + value).astype(BF)
        for t, out in enumerate(outs):
            out[q] = value[t * d.sources : (t + 1) * d.sources]


def third_rows_kernel(d, face_ref, iface, cols, edges, inner, field, pair_in, cross_in, folded, sent, ext):
    interface_rows(d, face_ref[0], iface, cols, edges, inner, field, pair_in, cross_in, folded, 0, [sent], ext)


def third_kernel(d, face_ref, cols, *rest):
    *inputs, folded, after, early, later, early_ext, later_ext = rest
    face = face_ref[0]
    for i, (out, ext) in enumerate(((early, early_ext), (later, later_ext))):
        edges, inner, field, pair_in, cross_in = inputs[5 * i : 5 * i + 5]
        extend(d, face, edges, inner, pair_in, cross_in, ext, pl.ds(0, out.shape[1]))
        correct(d, cols, face, field, folded, out, ext, range(d.count))


def marked(d, block, e):
    parts = []
    for q in range(d.nq):
        at = d.later + q // HALO * d.width
        mark = d.later + d.share + q * d.mark
        mark = block[e, mark : mark + d.mark, :]
        parts.append(block[q % HALO, at : at + d.width, :] * jnp.concatenate([mark] * (d.width // d.mark), axis=0))
    return jnp.concatenate(parts, axis=0)


def behind_kernel(
    d, face_ref, iface, cols, field, gfield, pair_in, cross_in, met, folded, after, edges, out, pair, cross, field_ext
):
    face = face_ref[0]
    parity = lax.rem(face, 2)
    correct_edges(d, cols, face, field, pair_in, cross_in, folded, edges, field_ext)
    pair[:, 0 : d.later, :] = edges[pl.ds(HALO * (1 - parity), HALO)]
    cross[:, 0 : d.later, :] = edges[pl.ds(HALO * parity, HALO)]
    w = d.width
    for shift in range(2, d.slots - 1):
        out[:, pl.ds(d.start(face + shift), d.group), :] = jnp.zeros((d.count, d.group, w), BF)

    def put(start, rows, value):
        for r in range(d.count):
            out[r, pl.ds(start, rows), :] = value[:, r * w : (r + 1) * w].astype(BF)

    pair_face, cross_face = face + 1 - 2 * parity, face - 1 + 2 * parity
    for at, other, block in ((HALO * (1 - parity), pair_face, pair_in), (HALO * parity, cross_face, cross_in)):
        x = jnp.concatenate([marked(d, block, e) for e in range(HALO)], axis=1)
        tiles = jnp.concatenate([met[at + e] for e in range(HALO)], axis=0)
        put(d.start(other), d.group, dot_nn(x, tiles))
    for q in range(d.nq):
        start = d.start(face) + q * w
        put(start, w, dot_nn(gfield[q], met[2 * HALO + q]))
        row = iface[q]
        span = pl.ds(pl.multiple_of(start, w), w)
        out[row, span, :] = (out[row, span, :].astype(F32) + gfield[q].astype(F32)).astype(BF)
    for start, buffer in zip(edge_rows(d, parity), (pair, cross)):
        for i, shift in enumerate((-1, 0, 1)):
            at = d.later + i * d.group
            buffer[:, at : at + d.group, :] = out[pl.ds(start, HALO), pl.ds(d.start(face + shift), d.group), :]


def coupling_ext(d, face, gfirst, pair_in, cross_in, ext):
    parity = lax.rem(face, 2)
    ext[0:HALO] = jnp.zeros((HALO, d.wide, d.width), BF)
    ext[d.up : d.ext] = jnp.zeros((HALO, d.wide, d.width), BF)
    ext[HALO : HALO + d.count] = gfirst[...]
    neighbours = ((d.up * (1 - parity), face + 1 - 2 * parity, pair_in), (d.up * parity, face - 1 + 2 * parity, cross_in))
    for start, other, block in neighbours:
        for i, shift in enumerate((-1, 0, 1)):
            at = d.later + i * d.group
            ext[pl.ds(start, HALO), pl.ds(d.start(other + shift), d.group), :] = block[:, at : at + d.group, :]


def second_rest_kernel(d, face_ref, iface, cols, *rest):
    edges, field, ext0, pair_in, cross_in = rest[:5]
    later_edges, later, later_ext0, later_pair_in, later_cross_in, folded, after = rest[5:12]
    inner, inner_later, faces_later, *faces_early, ext = rest[12:]
    face = face_ref[0]
    correct(d, cols, face, field, folded, inner, ext0, range(HALO, d.last))
    correct(d, cols, face, later, folded, inner_later, later_ext0, range(HALO, d.last))
    groups = [((later_edges, inner_later, later, later_pair_in, later_cross_in), 0, faces_later, d.ticks - 1 - d.split)]
    groups += [((edges, inner, field, pair_in, cross_in), 1, out, d.split - 1) for out in faces_early]
    for group, first, out, ticks in groups:
        outs = [out.at[t] for t in range(ticks)]
        interface_rows(d, face, iface, cols, *group, folded, first, outs, ext.at[:, pl.ds(0, ticks * d.sources), :])


def interface_kernel(d, face_ref, iface, cols, gfield, gfirst, pair_in, cross_in, folded, after, *rest):
    *chain, ext = rest
    face = face_ref[0]
    w = d.width
    coupling_ext(d, face, gfirst, pair_in, cross_in, ext)
    for i in range(d.slots):
        start = i * d.group % d.part
        part = chain[i * d.group // d.part]
        for q in range(d.nq):
            value = sweep(d, cols, face, ext, pl.ds(i * d.group, d.group), iface[q], folded)
            part[start : start + d.group, q * w : (q + 1) * w] = value.astype(BF)

        @pl.when(lax.rem(face, d.slots) == i)
        def _():
            for q in range(d.nq):
                block = (slice(start + q * w, start + (q + 1) * w), slice(q * w, (q + 1) * w))
                part[block] = (part[block].astype(F32) + gfield[q].astype(F32)).astype(BF)


def coupling_last_kernel(d, face_ref, iface, cols, gfield, gfirst, pair_in, cross_in, folded, after, out, ext):
    face = face_ref[0]
    w = d.width
    coupling_ext(d, face, gfirst, pair_in, cross_in, ext)
    for r in range(d.count):
        for s in range(0, d.wide, d.group):
            span = pl.ds(s, d.group)
            out[span, r * w : (r + 1) * w] = sweep(d, cols, face, ext, span, r, folded).astype(BF)
    for q in range(d.nq):
        lane = pl.ds(pl.multiple_of(iface[q] * w, w), w)
        span = pl.ds(pl.multiple_of(d.start(face) + q * w, w), w)
        out[span, lane] = (out[span, lane].astype(F32) + gfield[q].astype(F32)).astype(BF)


def chip_hops(faces):
    return [(0, None)] if faces <= 2 else [(0, 1)] if faces <= 4 else [(0, 1), (-1, None)]


def hop_face(faces, face, hop):
    return face ^ (2 * hop) if faces <= 4 else face + 2 * hop


def arrived_blocks(d, face, own, other):
    parity = lax.rem(face, 2)
    for i, hops in enumerate(chip_hops(d.faces)):
        starts = [0 if hop is None else d.start(hop_face(d.faces, face - parity, hop)) for hop in hops]
        for block, odd in ((own[i], parity), (other[i], 1 - parity)):
            start = pl.multiple_of(jnp.where(odd == 1, starts[1], starts[0]), d.group)
            yield jnp.concatenate([block[j] for j in range(2 * d.nq)], axis=1), start


def chain_kernel(d, tick, face_ref, *rest):
    own_chain, other_chain, rest = rest[: d.parts], rest[d.parts : 2 * d.parts], rest[2 * d.parts :]
    own_faces, other_faces, *arrived, sent, chain = rest
    face = face_ref[0]
    parity = lax.rem(face, 2)
    for i in range(d.parts):
        for j, part in enumerate((own_chain[i], other_chain[i])):
            chain[i * d.part : (i + 1) * d.part, j * d.group : (j + 1) * d.group] = part[...]
    half = len(arrived) // 2
    total = jnp.zeros((d.sources, 2 * d.group), F32)
    for x, start in arrived_blocks(d, face, arrived[:half], arrived[half:]):
        total += dot_nn(x, chain[pl.ds(start, 2 * d.group), :])
    for j, (base, odd) in enumerate(((own_faces, parity), (other_faces, 1 - parity))):
        for q in range(d.nq):
            at = j * d.group + q * d.width
            sent[odd * d.nq + q] = (base[tick, q].astype(F32) - total[:, at : at + d.width]).astype(BF)


def merge_kernel(d, face_ref, own, other, sent):
    parity = lax.rem(face_ref[0], 2)
    for q in range(d.nq):
        sent[parity * d.nq + q] = own[q]
        sent[(1 - parity) * d.nq + q] = other[q]


def tick_rows(d, early, later, tick, row):
    fields, at = (early, tick) if tick < d.split else (later, tick - d.split)
    return fields[row, at * d.sources : (at + 1) * d.sources, :].astype(F32)


def output_kernel(d, face_ref, early, later, coupled, *rest):
    *arrived, out, held, sems = rest
    w = d.width
    each = 2 * len(chip_hops(d.faces))
    copies = []
    part = 2 * w
    for t in range(d.ticks - 1):
        blocks = []
        if t:
            mine, arrived = arrived[:each], arrived[each:]
            blocks = list(arrived_blocks(d, face_ref[0], mine[: each // 2], mine[each // 2 :]))
        for c in range(0, d.count * w, part):
            total = jnp.zeros((d.sources, part), F32)
            for x, start in blocks:
                total += dot_nn(x, coupled[pl.ds(start, 2 * d.group), c : c + part])
            for j in range(0, part, w):
                value = tick_rows(d, early, later, t, (c + j) // w) - total[:, j : j + w]
                held[t, :, c + j : c + j + w] = value.astype(BF)
        copies.append(pltpu.make_async_copy(held.at[t], out.at[t], sems.at[t]))
        copies[-1].start()
    for copy in copies:
        copy.wait()


def last_own_kernel(d, face_ref, early, later, coupled, *rest):
    own, out = rest[:-1], rest[-1]
    w = d.width
    total = jnp.zeros((d.sources, d.count * w), F32)
    for x, start in list(arrived_blocks(d, face_ref[0], own, own))[0::2]:
        total += dot_nn(x, coupled[pl.ds(start, 2 * d.group), :])
    for r in range(d.count):
        out[:, r * w : (r + 1) * w] = tick_rows(d, early, later, d.ticks - 1, r) - total[:, r * w : (r + 1) * w]


def last_other_kernel(d, face_ref, own_part, coupled, earlier, *rest):
    other, (out, held, sems) = rest[:-3], rest[-3:]
    blocks = list(arrived_blocks(d, face_ref[0], other, other))[1::2]
    part = 2 * d.width
    copies = []
    for i, c in enumerate(range(0, d.count * d.width, part)):
        total = own_part[:, c : c + part]
        for x, start in blocks:
            total -= dot_nn(x, coupled[pl.ds(start, 2 * d.group), c : c + part])
        held[:, c : c + part] = total.astype(BF)
        here = held.at[:, c : c + part]
        copies.append(pltpu.make_async_copy(here, out.at[d.ticks - 1, :, c : c + part], sems.at[i]))
        copies[-1].start()
    for copy in copies:
        copy.wait()


def call(body, name, smem, inputs, outs, scratch=(), flops=0, anywhere=(), sems=0, place=pltpu.VMEM, aliases=None):
    outs = [x if isinstance(x, jax.ShapeDtypeStruct) else jax.ShapeDtypeStruct(x, BF) for x in outs]
    specs = [pl.BlockSpec(memory_space=pl.ANY if i in anywhere else pltpu.VMEM) for i in range(len(inputs))]
    return pl.pallas_call(
        body,
        name=name,
        out_shape=outs,
        in_specs=[pl.BlockSpec(memory_space=pltpu.SMEM)] * len(smem) + specs,
        out_specs=[pl.BlockSpec(memory_space=place if x.dtype != jnp.int32 else pltpu.SMEM) for x in outs],
        scratch_shapes=[pltpu.VMEM(s, BF) for s in scratch] + ([pltpu.SemaphoreType.DMA((sems,))] if sems else []),
        input_output_aliases=aliases or {},
        compiler_params=pltpu.CompilerParams(vmem_limit_bytes=32 * 1024 * 1024),
        cost_estimate=pl.CostEstimate(flops=flops, bytes_accessed=0, transcendentals=0),
    )(*smem, *inputs)


def on_device(rhs, inflow, diag_tiles, off_tiles, cols, inverse_tiles, coupling, iface):
    faces, slabs = lax.axis_size("face"), lax.axis_size("slab")
    ticks, _, sources, _ = rhs.shape
    _, count, neigh, width, _ = off_tiles.shape
    nq = coupling.shape[1]
    d = Dims(ticks, sources, count, neigh, width, nq, faces)
    diag, off, inv, couple, cols = diag_tiles[0], off_tiles[0], inverse_tiles[0], coupling[0], cols[0].T
    face = lax.axis_index("face").astype(jnp.int32)[None]
    tile = width * width

    pairing = [(i, i ^ 1) for i in range(faces) if i ^ 1 < faces]
    crossing = [(i, ((i + 1) ^ 1) - 1) for i in range(faces) if 0 <= ((i + 1) ^ 1) - 1 < faces]

    def exchange(pair, cross):
        got = lax.ppermute(cross, "face", crossing)
        return lax.ppermute(pair, "face", pairing), got

    def swap(block):
        return lax.ppermute(block, "face", pairing)

    def onward(block, beside=lambda: None):
        own = []
        for hops in chip_hops(faces):
            route = []
            for s in range(1, slabs):
                for f in range(faces):
                    hop = hops[f % 2]
                    g = -1 if hop is None else hop_face(faces, f, hop)
                    if 0 <= g < faces:
                        route.append(((s - 1) * faces + g, s * faces + f))
            own.append(lax.ppermute(block, ("slab", "face"), route))
        made = beside()
        if made is not None:
            *own, made = lax.optimization_barrier((*own, made))
        return own + [swap(x) for x in own], made

    split, early, later, group, ext, wide = d.split, d.early, d.later, d.group, d.ext, d.wide
    sweep_flops = 2 * count * tile * (neigh + 1)
    ints = [jax.ShapeDtypeStruct(x.shape, x.dtype) for x in (iface, cols)]
    on_hbm = (iface, cols, inflow[0], couple, inv, rhs[:, 0], diag, off)
    field, field_later, gfield, pair, cross, pair_later, cross_later, inv, diag, off, iface, cols = call(
        functools.partial(first_kernel, d),
        "first",
        [face],
        [pltpu.with_memory_space_constraint(x, pltpu.HBM) for x in on_hbm],
        [(count, early, width), (count, later, width), (nq, width, width)]
        + [(HALO, early, width)] * 2
        + [(HALO, d.first_rows, width)] * 2
        + [x.shape for x in (inv, diag, off)]
        + ints,
        [(ticks, sources, count * width), (sources, group), (nq, width, width)],
        anywhere=range(8),
        sems=7 + ticks,
    )
    pair0, cross0 = exchange(pair, cross)
    pair_later0, cross_later0 = exchange(pair_later, cross_later)
    folded, met = call(
        functools.partial(fold_kernel, d),
        "fold",
        [face, iface, cols],
        [inv, diag, off],
        [(count, d.depth, width), (2 * HALO + nq, width, count * width)],
    )
    edges, pair, cross, ext0 = call(
        functools.partial(second_edges_kernel, d),
        "second_edges",
        [face, cols],
        [field, pair0, cross0, folded],
        [(2 * HALO, early, width)] + [(HALO, early, width)] * 2 + [(ext, early, width)],
    )
    pair1, cross1 = exchange(pair, cross)
    edges_later, gfirst, pair, cross, ext_later0 = call(
        functools.partial(behind_kernel, d),
        "behind",
        [face, iface, cols],
        [field_later, gfield, pair_later0, cross_later0, met, folded, pair1],
        [(2 * HALO, later, width), (count, wide, width)] + [(HALO, later + 3 * group, width)] * 2 + [(ext, later, width)],
        anywhere=(6,),
    )
    pair_later1, cross_later1 = exchange(pair, cross)
    (inner_first,) = call(
        functools.partial(second_inner_kernel, d),
        "second_inner",
        [face, cols],
        [field, ext0, folded, gfirst],
        [(count - 2 * HALO, sources, width)],
        anywhere=(3,),
    )
    cross1, inner_first = lax.optimization_barrier((cross1, inner_first))
    (own_first,) = call(
        functools.partial(third_rows_kernel, d),
        "third_rows",
        [face, iface, cols],
        [edges, inner_first, field, pair1, cross1, folded],
        [(nq, sources, width)],
        [(ext, sources, width)],
        flops=12 * early * sweep_flops,
    )
    (sent,) = call(
        functools.partial(merge_kernel, d),
        "merge",
        [face],
        [own_first, swap(own_first)],
        [(2 * nq, sources, width)],
    )

    def beside_first():
        rows = call(
            functools.partial(interface_kernel, d),
            "interface",
            [face, iface, cols],
            [gfield, gfirst, pair_later1, cross_later1, folded, sent],
            [(d.part, group)] * d.parts,
            [(ext, wide, width)],
            anywhere=(5,),
        )
        rest = call(
            functools.partial(second_rest_kernel, d),
            "second_rest",
            [face, iface, cols],
            [edges, field, ext0, pair1, cross1, edges_later, field_later, ext_later0, pair_later1, cross_later1, folded, rows[0]],
            [(count - 2 * HALO, early, width), (count - 2 * HALO, later, width), (ticks - 1 - split, nq, sources, width)]
            + [(split - 1, nq, sources, width)] * (split > 1),
            [(ext, max(early, later), width)],
            anywhere=(11,),
        )
        return rows, [swap(x) for x in rows], rest

    arrived, (chain, other_chain, (inner, inner_later, faces_later, *faces_early)) = onward(sent, beside_first)
    other_early = [swap(x) for x in faces_early]
    early_parts = (edges, inner, field, pair1, cross1)
    later_parts = (edges_later, inner_later, field_later, pair_later1, cross_later1)

    def fields(after):
        return call(
            functools.partial(third_kernel, d),
            "third",
            [face, cols],
            [*early_parts, *later_parts, folded, after],
            [(count, early, width), (count, later, width)],
            [(ext, early, width), (ext, later, width)],
            anywhere=(11,),
        )

    whole = (ticks, sources, count * width)

    def operator():
        return call(
            functools.partial(coupling_last_kernel, d),
            "coupling_last",
            [face, iface, cols],
            [gfield, gfirst, pair_later1, cross_later1, folded, chain[0]],
            [(wide, count * width)],
            [(ext, wide, width)],
            flops=wide * sweep_flops,
            anywhere=(5,),
        )[0]

    def output(blocks):
        return call(
            functools.partial(output_kernel, d),
            "output",
            [face],
            [*twice, coupled] + blocks,
            [whole],
            [(ticks - 1, sources, count * width)],
            sems=ticks - 1,
            place=pl.ANY,
        )[0]

    everything = []
    coupled = most = None
    for tick in range(1, ticks):
        everything += arrived
        if tick == ticks - 1:
            break
        early_tick = tick < split
        bases = (faces_early[0], other_early[0]) if early_tick else (faces_later, other_later)
        (sent,) = call(
            functools.partial(chain_kernel, d, tick - 1 if early_tick else tick - split),
            "chain",
            [face],
            [*chain, *other_chain, *bases] + arrived,
            [(2 * nq, sources, width)],
            [(wide, 2 * group)],
            flops=4 * sources * wide * group,
        )
        if tick == 1:
            arrived, (coupled, other_later) = onward(sent, lambda: (operator(), swap(faces_later)))
        else:
            twice = fields(sent)
            arrived, most = onward(sent, lambda: output(everything))
    half = len(arrived) // 2
    (own_part,) = call(
        functools.partial(last_own_kernel, d),
        "last_own",
        [face],
        [*twice, coupled] + arrived[:half],
        [jax.ShapeDtypeStruct((sources, count * width), F32)],
    )
    (out,) = call(
        functools.partial(last_other_kernel, d),
        "last_other",
        [face],
        [own_part, coupled, most] + arrived[half:],
        [whole],
        [(sources, count * width)],
        anywhere=(2,),
        sems=count,
        place=pl.ANY,
        aliases={3: 0},
    )
    return out[:, None]


def solution(mesh):
    placed = (
        P(None, "slab", None, "face"),
        P("slab", None, "face"),
        P("slab", "face", None, None),
        P("slab", "face", None, None, None),
        P("slab", "face", None),
        P("slab", "face", None, None),
        P("slab", "face", None, None),
        P("face"),
    )
    return jax.shard_map(
        on_device,
        mesh=mesh,
        in_specs=placed,
        out_specs=P(None, "slab", None, "face"),
        check_vma=False,
    )
```

```python
import functools
import math

import jax
import jax.numpy as jnp
from jax import lax
from jax.experimental import pallas as pl
from jax.experimental.pallas import tpu as pltpu
from jax.sharding import PartitionSpec as P

HALO = 2
BF = jnp.bfloat16
F32 = jnp.float32


def dot_nt(a, b):
    return lax.dot_general(a, b, (((1,), (1,)), ((), ())), preferred_element_type=F32)


def dot_nn(a, b):
    return lax.dot_general(a, b, (((1,), (0,)), ((), ())), preferred_element_type=F32)


class Dims:
    def __init__(self, ticks, sources, count, neigh, width, nq, faces):
        self.ticks, self.sources, self.count, self.neigh = ticks, sources, count, neigh
        self.width, self.nq, self.faces = width, nq, faces
        self.split = max(ticks // 2, 1)
        self.early, self.later = self.split * sources, (ticks - self.split) * sources
        self.group = nq * width
        self.ext = count + 2 * HALO
        self.depth = (1 + neigh) * width
        self.slots = 4 if faces <= 4 else 6
        self.wide = self.slots * self.group
        self.parts = 4 if self.slots % 4 == 0 else 3
        self.part = self.wide // self.parts
        self.mark = 16
        self.share = -(-nq // HALO) * width
        self.first_rows = self.later + self.share + nq * self.mark
        self.last = count - HALO
        self.up = count + HALO

    def start(self, face):
        return pl.multiple_of(lax.rem(face + 2 * self.slots, self.slots) * self.group, self.group)

    def first_col(self, face):
        return face * self.count - HALO


def spans(rows):
    parts = -(-rows // 256)
    return [pl.ds(i * (rows // parts), rows // parts) for i in range(parts)]


def edge_rows(d, parity):
    return d.last * (1 - parity), d.last * parity


def first_kernel(
    d, face_ref, iface_hbm, cols_hbm, inflow, coupling, inv, rhs, diag_hbm, off_hbm, *rest
):
    early, later, gfield, *buffers, tiles, diag, off, iface, cols, right, flow, couple, sems = rest
    w = d.width
    moves = [(iface_hbm, iface), (inflow, flow), (coupling, couple), (inv, tiles)]
    moves += [(rhs.at[t], right.at[t]) for t in range(d.ticks)]
    moves += [(cols_hbm, cols), (diag_hbm, diag), (off_hbm, off)]
    copies = [pltpu.make_async_copy(a, b, sems.at[i]) for i, (a, b) in enumerate(moves)]
    for copy in copies:
        copy.start()
    for copy in copies[:4]:
        copy.wait()
    coupled = []
    for q in range(d.nq):
        turned = couple[q].astype(F32).T.astype(BF)
        gfield[q] = dot_nt(turned, tiles[iface[q]]).astype(BF)
        coupled.append(dot_nn(flow[:, q * w : (q + 1) * w], turned))
    for copy in copies[4 : 4 + d.ticks]:
        copy.wait()
    for r in range(d.count):
        x = jnp.concatenate([right[t, :, r * w : (r + 1) * w] for t in range(d.ticks)], axis=0)
        value = dot_nt(x, tiles[r]).astype(BF)
        early[r] = value[: d.early]
        later[r] = value[d.early :]
    for q in range(d.nq):
        row = iface[q]
        corrected = right[0, :, pl.ds(pl.multiple_of(row * w, w), w)].astype(F32) - coupled[q]
        early[row, 0 : d.sources, :] = dot_nt(corrected.astype(BF), tiles[row]).astype(BF)
    for i, start in enumerate(edge_rows(d, lax.rem(face_ref[0], 2))):
        buffers[i][...] = early[pl.ds(start, HALO)]
        buffer = buffers[2 + i]
        buffer[:, 0 : d.later, :] = later[pl.ds(start, HALO)]
        for q in range(d.nq):
            at = d.later + q // HALO * w
            buffer[q % HALO, at : at + w, :] = gfield[q]
            at = d.later + d.share + q * d.mark
            for e in range(HALO):
                buffer[e, at : at + d.mark, :] = jnp.full((d.mark, w), iface[q] == start + e).astype(F32).astype(BF)
    for copy in copies[4 + d.ticks :]:
        copy.wait()


def fold_kernel(d, face_ref, iface, cols, inv, diag, off, folded, met):
    w = d.width
    for r in range(d.count):
        tiles = jnp.concatenate([diag[r]] + [off[r, k] for k in range(d.neigh)], axis=1)
        product = dot_nn(inv[r], tiles)
        rows = lax.broadcasted_iota(jnp.int32, (w, w), 0)
        unit = (rows == lax.broadcasted_iota(jnp.int32, (w, w), 1)).astype(F32)
        for k in range(1 + d.neigh):
            part = product[:, k * w : (k + 1) * w].T
            folded[r, k * w : (k + 1) * w, :] = ((unit if k == 0 else 0.0) - part).astype(BF)
    met[...] = jnp.zeros_like(met)
    for r in range(d.count):
        lanes = slice(r * w, (r + 1) * w)
        for q in range(d.nq):
            met[2 * HALO + q, :, lanes] = jnp.where(iface[q] == r, folded[r, 0:w, :], jnp.zeros((w, w), BF))
        for k in range(d.neigh):
            c = cols[k, r] - d.first_col(face_ref[0])
            inside = jnp.logical_and(c >= HALO, c < d.up)
            at = jnp.where(c < HALO, c, c - d.count)
            hit = jnp.logical_not(inside)
            for q in range(d.nq):
                here = c == iface[q] + HALO
                at = jnp.where(here, 2 * HALO + q, at)
                hit = jnp.logical_or(hit, here)

            @pl.when(hit)
            def _():
                met[at, :, lanes] += folded[r, (1 + k) * w : (2 + k) * w, :]


def sweep(d, cols, face, ext, span, r, folded):
    x = [ext[r + HALO, span, :]] + [ext[cols[k, r] - d.first_col(face), span, :] for k in range(d.neigh)]
    return dot_nn(jnp.concatenate(x, axis=1), folded[r])


def place_halo(d, face, pair_in, cross_in, ext, rows):
    parity = lax.rem(face, 2)
    ext[pl.ds(d.up * (1 - parity), HALO)] = pair_in[:, rows, :]
    ext[pl.ds(d.up * parity, HALO)] = cross_in[:, rows, :]


def extend(d, face, edges, inner, pair_in, cross_in, ext, rows):
    ext[HALO : 2 * HALO] = edges[0:HALO, rows, :]
    ext[2 * HALO : d.count] = inner[:, rows, :]
    ext[d.count : d.up] = edges[HALO : 2 * HALO, rows, :]
    place_halo(d, face, pair_in, cross_in, ext, rows)


def correct(d, cols, face, base, folded, out, ext, rows):
    for i, r in enumerate(rows):
        for span in spans(out.shape[1]):
            value = base[r, span, :].astype(F32) + sweep(d, cols, face, ext, span, r, folded)
            out[i, span, :] = value.astype(BF)


def correct_edges(d, cols, face, field, pair_in, cross_in, folded, edges, ext):
    ext[HALO : HALO + d.count] = field[...]
    place_halo(d, face, pair_in, cross_in, ext, pl.ds(0, field.shape[1]))
    correct(d, cols, face, field, folded, edges, ext, list(range(HALO)) + list(range(d.last, d.count)))


def second_edges_kernel(d, face_ref, cols, field, pair_in, cross_in, folded, edges, pair, cross, ext):
    face = face_ref[0]
    parity = lax.rem(face, 2)
    correct_edges(d, cols, face, field, pair_in, cross_in, folded, edges, ext)
    pair[...] = edges[pl.ds(HALO * (1 - parity), HALO)]
    cross[...] = edges[pl.ds(HALO * parity, HALO)]


def second_inner_kernel(d, face_ref, cols, field, ext, folded, after, out):
    correct(d, cols, face_ref[0], field, folded, out, ext, range(HALO, d.last))


def interface_rows(d, face, iface, cols, edges, inner, field, pair_in, cross_in, folded, first, outs, ext):
    ticks = pl.ds(first * d.sources, len(outs) * d.sources)
    extend(d, face, edges, inner, pair_in, cross_in, ext, ticks)
    for q in range(d.nq):
        row = iface[q]
        value = sweep(d, cols, face, ext, pl.ds(0, len(outs) * d.sources), row, folded)
        value = (field[row, ticks, :].astype(F32) + value).astype(BF)
        for t, out in enumerate(outs):
            out[q] = value[t * d.sources : (t + 1) * d.sources]


def third_rows_kernel(d, face_ref, iface, cols, edges, inner, field, pair_in, cross_in, folded, sent, ext):
    interface_rows(d, face_ref[0], iface, cols, edges, inner, field, pair_in, cross_in, folded, 0, [sent], ext)


def third_kernel(d, face_ref, cols, *rest):
    *inputs, folded, after, early, later, early_ext, later_ext = rest
    face = face_ref[0]
    for i, (out, ext) in enumerate(((early, early_ext), (later, later_ext))):
        edges, inner, field, pair_in, cross_in = inputs[5 * i : 5 * i + 5]
        extend(d, face, edges, inner, pair_in, cross_in, ext, pl.ds(0, out.shape[1]))
        correct(d, cols, face, field, folded, out, ext, range(d.count))


def marked(d, block, e):
    parts = []
    for q in range(d.nq):
        at = d.later + q // HALO * d.width
        mark = d.later + d.share + q * d.mark
        mark = block[e, mark : mark + d.mark, :]
        parts.append(block[q % HALO, at : at + d.width, :] * jnp.concatenate([mark] * (d.width // d.mark), axis=0))
    return jnp.concatenate(parts, axis=0)


def behind_kernel(
    d, face_ref, iface, cols, field, gfield, pair_in, cross_in, met, folded, after, edges, out, pair, cross, field_ext
):
    face = face_ref[0]
    parity = lax.rem(face, 2)
    correct_edges(d, cols, face, field, pair_in, cross_in, folded, edges, field_ext)
    pair[:, 0 : d.later, :] = edges[pl.ds(HALO * (1 - parity), HALO)]
    cross[:, 0 : d.later, :] = edges[pl.ds(HALO * parity, HALO)]
    w = d.width
    for shift in range(2, d.slots - 1):
        out[:, pl.ds(d.start(face + shift), d.group), :] = jnp.zeros((d.count, d.group, w), BF)

    def put(start, rows, value):
        for r in range(d.count):
            out[r, pl.ds(start, rows), :] = value[:, r * w : (r + 1) * w].astype(BF)

    pair_face, cross_face = face + 1 - 2 * parity, face - 1 + 2 * parity
    for at, other, block in ((HALO * (1 - parity), pair_face, pair_in), (HALO * parity, cross_face, cross_in)):
        x = jnp.concatenate([marked(d, block, e) for e in range(HALO)], axis=1)
        tiles = jnp.concatenate([met[at + e] for e in range(HALO)], axis=0)
        put(d.start(other), d.group, dot_nn(x, tiles))
    for q in range(d.nq):
        start = d.start(face) + q * w
        put(start, w, dot_nn(gfield[q], met[2 * HALO + q]))
        row = iface[q]
        span = pl.ds(pl.multiple_of(start, w), w)
        out[row, span, :] = (out[row, span, :].astype(F32) + gfield[q].astype(F32)).astype(BF)
    for start, buffer in zip(edge_rows(d, parity), (pair, cross)):
        for i, shift in enumerate((-1, 0, 1)):
            at = d.later + i * d.group
            buffer[:, at : at + d.group, :] = out[pl.ds(start, HALO), pl.ds(d.start(face + shift), d.group), :]


def coupling_ext(d, face, gfirst, pair_in, cross_in, ext):
    parity = lax.rem(face, 2)
    ext[0:HALO] = jnp.zeros((HALO, d.wide, d.width), BF)
    ext[d.up : d.ext] = jnp.zeros((HALO, d.wide, d.width), BF)
    ext[HALO : HALO + d.count] = gfirst[...]
    neighbours = ((d.up * (1 - parity), face + 1 - 2 * parity, pair_in), (d.up * parity, face - 1 + 2 * parity, cross_in))
    for start, other, block in neighbours:
        for i, shift in enumerate((-1, 0, 1)):
            at = d.later + i * d.group
            ext[pl.ds(start, HALO), pl.ds(d.start(other + shift), d.group), :] = block[:, at : at + d.group, :]


def rest_kernel(d, first, face_ref, iface, cols, edges, field, ext0, pair_in, cross_in, folded, after, inner, faces_out, ext):
    face = face_ref[0]
    correct(d, cols, face, field, folded, inner, ext0, range(HALO, d.last))
    outs = [faces_out.at[t] for t in range(faces_out.shape[0])]
    interface_rows(d, face, iface, cols, edges, inner, field, pair_in, cross_in, folded, first, outs, ext)


def interface_kernel(d, face_ref, iface, cols, gfield, gfirst, pair_in, cross_in, folded, after, *rest):
    *chain, ext = rest
    face = face_ref[0]
    w = d.width
    coupling_ext(d, face, gfirst, pair_in, cross_in, ext)
    for i in range(d.slots):
        start = i * d.group % d.part
        part = chain[i * d.group // d.part]
        for q in range(d.nq):
            value = sweep(d, cols, face, ext, pl.ds(i * d.group, d.group), iface[q], folded)
            part[start : start + d.group, q * w : (q + 1) * w] = value.astype(BF)

        @pl.when(lax.rem(face, d.slots) == i)
        def _():
            for q in range(d.nq):
                block = (slice(start + q * w, start + (q + 1) * w), slice(q * w, (q + 1) * w))
                part[block] = (part[block].astype(F32) + gfield[q].astype(F32)).astype(BF)


def coupling_last_kernel(d, face_ref, iface, cols, gfield, gfirst, pair_in, cross_in, folded, after, out, ext):
    face = face_ref[0]
    w = d.width
    coupling_ext(d, face, gfirst, pair_in, cross_in, ext)
    for r in range(d.count):
        for s in range(0, d.wide, d.group):
            span = pl.ds(s, d.group)
            out[span, r * w : (r + 1) * w] = sweep(d, cols, face, ext, span, r, folded).astype(BF)
    for q in range(d.nq):
        lane = pl.ds(pl.multiple_of(iface[q] * w, w), w)
        span = pl.ds(pl.multiple_of(d.start(face) + q * w, w), w)
        out[span, lane] = (out[span, lane].astype(F32) + gfield[q].astype(F32)).astype(BF)


def chip_hops(faces):
    return [(0, None)] if faces <= 2 else [(0, 1)] if faces <= 4 else [(0, 1), (-1, None)]


def hop_face(faces, face, hop):
    return face ^ (2 * hop) if faces <= 4 else face + 2 * hop


def arrived_blocks(d, face, own, other):
    parity = lax.rem(face, 2)
    for i, hops in enumerate(chip_hops(d.faces)):
        starts = [0 if hop is None else d.start(hop_face(d.faces, face - parity, hop)) for hop in hops]
        for block, odd in ((own[i], parity), (other[i], 1 - parity)):
            start = pl.multiple_of(jnp.where(odd == 1, starts[1], starts[0]), d.group)
            yield jnp.concatenate([block[j] for j in range(2 * d.nq)], axis=1), start


def chain_kernel(d, tick, face_ref, *rest):
    own_chain, other_chain, rest = rest[: d.parts], rest[d.parts : 2 * d.parts], rest[2 * d.parts :]
    own_faces, other_faces, *arrived, sent, chain = rest
    face = face_ref[0]
    parity = lax.rem(face, 2)
    for i in range(d.parts):
        for j, part in enumerate((own_chain[i], other_chain[i])):
            chain[i * d.part : (i + 1) * d.part, j * d.group : (j + 1) * d.group] = part[...]
    half = len(arrived) // 2
    total = jnp.zeros((d.sources, 2 * d.group), F32)
    for x, start in arrived_blocks(d, face, arrived[:half], arrived[half:]):
        total += dot_nn(x, chain[pl.ds(start, 2 * d.group), :])
    for j, (base, odd) in enumerate(((own_faces, parity), (other_faces, 1 - parity))):
        for q in range(d.nq):
            at = j * d.group + q * d.width
            sent[odd * d.nq + q] = (base[tick, q].astype(F32) - total[:, at : at + d.width]).astype(BF)


def merge_kernel(d, face_ref, own, other, sent):
    parity = lax.rem(face_ref[0], 2)
    for q in range(d.nq):
        sent[parity * d.nq + q] = own[q]
        sent[(1 - parity) * d.nq + q] = other[q]


def tick_rows(d, early, later, tick, row):
    fields, at = (early, tick) if tick < d.split else (later, tick - d.split)
    return fields[row, at * d.sources : (at + 1) * d.sources, :].astype(F32)


def output_kernel(d, face_ref, early, later, coupled, *rest):
    *arrived, out, held, sems = rest
    w = d.width
    each = 2 * len(chip_hops(d.faces))
    copies = []
    part = 2 * w
    for t in range(d.ticks - 1):
        blocks = []
        if t:
            mine, arrived = arrived[:each], arrived[each:]
            blocks = list(arrived_blocks(d, face_ref[0], mine[: each // 2], mine[each // 2 :]))
        for c in range(0, d.count * w, part):
            total = jnp.zeros((d.sources, part), F32)
            for x, start in blocks:
                total += dot_nn(x, coupled[pl.ds(start, 2 * d.group), c : c + part])
            for j in range(0, part, w):
                value = tick_rows(d, early, later, t, (c + j) // w) - total[:, j : j + w]
                held[t, :, c + j : c + j + w] = value.astype(BF)
        copies.append(pltpu.make_async_copy(held.at[t], out.at[t], sems.at[t]))
        copies[-1].start()
    for copy in copies:
        copy.wait()


def last_own_kernel(d, face_ref, early, later, coupled, *rest):
    own, out = rest[:-1], rest[-1]
    w = d.width
    total = jnp.zeros((d.sources, d.count * w), F32)
    for x, start in list(arrived_blocks(d, face_ref[0], own, own))[0::2]:
        total += dot_nn(x, coupled[pl.ds(start, 2 * d.group), :])
    for r in range(d.count):
        out[:, r * w : (r + 1) * w] = tick_rows(d, early, later, d.ticks - 1, r) - total[:, r * w : (r + 1) * w]


def last_other_kernel(d, face_ref, own_part, coupled, earlier, *rest):
    other, (out, held, sems) = rest[:-3], rest[-3:]
    blocks = list(arrived_blocks(d, face_ref[0], other, other))[1::2]
    part = 2 * d.width
    copies = []
    for i, c in enumerate(range(0, d.count * d.width, part)):
        total = own_part[:, c : c + part]
        for x, start in blocks:
            total -= dot_nn(x, coupled[pl.ds(start, 2 * d.group), c : c + part])
        held[:, c : c + part] = total.astype(BF)
        here = held.at[:, c : c + part]
        copies.append(pltpu.make_async_copy(here, out.at[d.ticks - 1, :, c : c + part], sems.at[i]))
        copies[-1].start()
    for copy in copies:
        copy.wait()


def call(body, name, smem, inputs, outs, scratch=(), flops=0, anywhere=(), sems=0, place=pltpu.VMEM, aliases=None):
    outs = [x if isinstance(x, jax.ShapeDtypeStruct) else jax.ShapeDtypeStruct(x, BF) for x in outs]
    specs = [pl.BlockSpec(memory_space=pl.ANY if i in anywhere else pltpu.VMEM) for i in range(len(inputs))]
    return pl.pallas_call(
        body,
        name=name,
        out_shape=outs,
        in_specs=[pl.BlockSpec(memory_space=pltpu.SMEM)] * len(smem) + specs,
        out_specs=[pl.BlockSpec(memory_space=place if x.dtype != jnp.int32 else pltpu.SMEM) for x in outs],
        scratch_shapes=[pltpu.VMEM(s, BF) for s in scratch] + ([pltpu.SemaphoreType.DMA((sems,))] if sems else []),
        input_output_aliases=aliases or {},
        compiler_params=pltpu.CompilerParams(vmem_limit_bytes=32 * 1024 * 1024),
        cost_estimate=pl.CostEstimate(flops=flops, bytes_accessed=0, transcendentals=0),
    )(*smem, *inputs)


def on_device(rhs, inflow, diag_tiles, off_tiles, cols, inverse_tiles, coupling, iface):
    faces, slabs = lax.axis_size("face"), lax.axis_size("slab")
    ticks, _, sources, _ = rhs.shape
    _, count, neigh, width, _ = off_tiles.shape
    nq = coupling.shape[1]
    d = Dims(ticks, sources, count, neigh, width, nq, faces)
    diag, off, inv, couple, cols = diag_tiles[0], off_tiles[0], inverse_tiles[0], coupling[0], cols[0].T
    face = lax.axis_index("face").astype(jnp.int32)[None]
    tile = width * width

    pairing = [(i, i ^ 1) for i in range(faces) if i ^ 1 < faces]
    crossing = [(i, ((i + 1) ^ 1) - 1) for i in range(faces) if 0 <= ((i + 1) ^ 1) - 1 < faces]

    def exchange(pair, cross):
        got = lax.ppermute(cross, "face", crossing)
        return lax.ppermute(pair, "face", pairing), got

    def swap(block):
        return lax.ppermute(block, "face", pairing)

    def onward(block, beside=lambda: None):
        own = []
        for hops in chip_hops(faces):
            route = []
            for s in range(1, slabs):
                for f in range(faces):
                    hop = hops[f % 2]
                    g = -1 if hop is None else hop_face(faces, f, hop)
                    if 0 <= g < faces:
                        route.append(((s - 1) * faces + g, s * faces + f))
            own.append(lax.ppermute(block, ("slab", "face"), route))
        made = beside()
        if made is not None:
            *own, made = lax.optimization_barrier((*own, made))
        return own + [swap(x) for x in own], made

    split, early, later, group, ext, wide = d.split, d.early, d.later, d.group, d.ext, d.wide
    sweep_flops = 2 * count * tile * (neigh + 1)
    ints = [jax.ShapeDtypeStruct(x.shape, x.dtype) for x in (iface, cols)]
    on_hbm = (iface, cols, inflow[0], couple, inv, rhs[:, 0], diag, off)
    field, field_later, gfield, pair, cross, pair_later, cross_later, inv, diag, off, iface, cols = call(
        functools.partial(first_kernel, d),
        "first",
        [face],
        [pltpu.with_memory_space_constraint(x, pltpu.HBM) for x in on_hbm],
        [(count, early, width), (count, later, width), (nq, width, width)]
        + [(HALO, early, width)] * 2
        + [(HALO, d.first_rows, width)] * 2
        + [x.shape for x in (inv, diag, off)]
        + ints,
        [(ticks, sources, count * width), (sources, group), (nq, width, width)],
        anywhere=range(8),
        sems=7 + ticks,
    )
    pair0, cross0 = exchange(pair, cross)
    pair_later0, cross_later0 = exchange(pair_later, cross_later)
    folded, met = call(
        functools.partial(fold_kernel, d),
        "fold",
        [face, iface, cols],
        [inv, diag, off],
        [(count, d.depth, width), (2 * HALO + nq, width, count * width)],
    )
    edges, pair, cross, ext0 = call(
        functools.partial(second_edges_kernel, d),
        "second_edges",
        [face, cols],
        [field, pair0, cross0, folded],
        [(2 * HALO, early, width)] + [(HALO, early, width)] * 2 + [(ext, early, width)],
    )
    pair1, cross1 = exchange(pair, cross)
    edges_later, gfirst, pair, cross, ext_later0 = call(
        functools.partial(behind_kernel, d),
        "behind",
        [face, iface, cols],
        [field_later, gfield, pair_later0, cross_later0, met, folded, pair1],
        [(2 * HALO, later, width), (count, wide, width)] + [(HALO, later + 3 * group, width)] * 2 + [(ext, later, width)],
        anywhere=(6,),
    )
    pair_later1, cross_later1 = exchange(pair, cross)
    (inner_first,) = call(
        functools.partial(second_inner_kernel, d),
        "second_inner",
        [face, cols],
        [field, ext0, folded, gfirst],
        [(count - 2 * HALO, sources, width)],
        anywhere=(3,),
    )
    cross1, inner_first = lax.optimization_barrier((cross1, inner_first))
    (own_first,) = call(
        functools.partial(third_rows_kernel, d),
        "third_rows",
        [face, iface, cols],
        [edges, inner_first, field, pair1, cross1, folded],
        [(nq, sources, width)],
        [(ext, sources, width)],
        flops=12 * early * sweep_flops,
    )
    (sent,) = call(
        functools.partial(merge_kernel, d),
        "merge",
        [face],
        [own_first, swap(own_first)],
        [(2 * nq, sources, width)],
    )

    def rest(first, ticks, rows, edges, field, ext0, pair, cross, after):
        return call(
            functools.partial(rest_kernel, d, first),
            "rest",
            [face, iface, cols],
            [edges, field, ext0, pair, cross, folded, after],
            [(count - 2 * HALO, rows, width), (ticks, nq, sources, width)],
            [(ext, ticks * sources, width)],
            anywhere=(6,),
        )

    inner, faces_early = rest(1, split - 1, early, edges, field, ext0, pair1, cross1, sent)
    early_parts = (edges, inner, field, pair1, cross1)

    def beside_first():
        rows = call(
            functools.partial(interface_kernel, d),
            "interface",
            [face, iface, cols],
            [gfield, gfirst, pair_later1, cross_later1, folded, inner],
            [(d.part, group)] * d.parts,
            [(ext, wide, width)],
            anywhere=(5,),
        )
        return rows, [swap(x) for x in rows]

    arrived, (chain, other_chain) = onward(sent, beside_first)
    other_early = swap(faces_early)

    def beside_second(sent):
        made = rest(0, ticks - 1 - split, later, edges_later, field_later, ext_later0, pair_later1, cross_later1, sent)
        return operator(), *made, swap(made[1])

    def fields(after):
        return call(
            functools.partial(third_kernel, d),
            "third",
            [face, cols],
            [*early_parts, *later_parts, folded, after],
            [(count, early, width), (count, later, width)],
            [(ext, early, width), (ext, later, width)],
            anywhere=(11,),
        )

    whole = (ticks, sources, count * width)

    def operator():
        return call(
            functools.partial(coupling_last_kernel, d),
            "coupling_last",
            [face, iface, cols],
            [gfield, gfirst, pair_later1, cross_later1, folded, chain[0]],
            [(wide, count * width)],
            [(ext, wide, width)],
            flops=wide * sweep_flops,
            anywhere=(5,),
        )[0]

    def output(blocks):
        return call(
            functools.partial(output_kernel, d),
            "output",
            [face],
            [*twice, coupled] + blocks,
            [whole],
            [(ticks - 1, sources, count * width)],
            sems=ticks - 1,
            place=pl.ANY,
        )[0]

    everything = []
    coupled = most = None
    for tick in range(1, ticks):
        everything += arrived
        if tick == ticks - 1:
            break
        early_tick = tick < split
        bases = (faces_early, other_early) if early_tick else (faces_later, other_later)
        (sent,) = call(
            functools.partial(chain_kernel, d, tick - 1 if early_tick else tick - split),
            "chain",
            [face],
            [*chain, *other_chain, *bases] + arrived,
            [(2 * nq, sources, width)],
            [(wide, 2 * group)],
            flops=4 * sources * wide * group,
        )
        if tick == 1:
            arrived, (coupled, inner_later, faces_later, other_later) = onward(sent, functools.partial(beside_second, sent))
            later_parts = (edges_later, inner_later, field_later, pair_later1, cross_later1)
        else:
            twice = fields(sent)
            arrived, most = onward(sent, lambda: output(everything))
    half = len(arrived) // 2
    (own_part,) = call(
        functools.partial(last_own_kernel, d),
        "last_own",
        [face],
        [*twice, coupled] + arrived[:half],
        [jax.ShapeDtypeStruct((sources, count * width), F32)],
    )
    (out,) = call(
        functools.partial(last_other_kernel, d),
        "last_other",
        [face],
        [own_part, coupled, most] + arrived[half:],
        [whole],
        [(sources, count * width)],
        anywhere=(2,),
        sems=count,
        place=pl.ANY,
        aliases={3: 0},
    )
    return out[:, None]


def solution(mesh):
    placed = (
        P(None, "slab", None, "face"),
        P("slab", None, "face"),
        P("slab", "face", None, None),
        P("slab", "face", None, None, None),
        P("slab", "face", None),
        P("slab", "face", None, None),
        P("slab", "face", None, None),
        P("face"),
    )
    return jax.shard_map(
        on_device,
        mesh=mesh,
        in_specs=placed,
        out_specs=P(None, "slab", None, "face"),
        check_vma=False,
    )
```

```python
import functools
import math

import jax
import jax.numpy as jnp
from jax import lax
from jax.experimental import pallas as pl
from jax.experimental.pallas import tpu as pltpu
from jax.sharding import PartitionSpec as P

HALO = 2
BF = jnp.bfloat16
F32 = jnp.float32


def dot_nt(a, b):
    return lax.dot_general(a, b, (((1,), (1,)), ((), ())), preferred_element_type=F32)


def dot_nn(a, b):
    return lax.dot_general(a, b, (((1,), (0,)), ((), ())), preferred_element_type=F32)


class Dims:
    def __init__(self, ticks, sources, count, neigh, width, nq, faces):
        self.ticks, self.sources, self.count, self.neigh = ticks, sources, count, neigh
        self.width, self.nq, self.faces = width, nq, faces
        self.split = max(ticks // 2, 1)
        self.early, self.later = self.split * sources, (ticks - self.split) * sources
        self.group = nq * width
        self.ext = count + 2 * HALO
        self.depth = (1 + neigh) * width
        self.slots = 4 if faces <= 4 else 6
        self.wide = self.slots * self.group
        self.parts = 4 if self.slots % 4 == 0 else 3
        self.part = self.wide // self.parts
        self.mark = 16
        self.share = -(-nq // HALO) * width
        self.first_rows = self.later + self.share + nq * self.mark
        self.last = count - HALO
        self.up = count + HALO

    def start(self, face):
        return pl.multiple_of(lax.rem(face + 2 * self.slots, self.slots) * self.group, self.group)

    def first_col(self, face):
        return face * self.count - HALO


def spans(rows):
    parts = -(-rows // 256)
    return [pl.ds(i * (rows // parts), rows // parts) for i in range(parts)]


def edge_rows(d, parity):
    return d.last * (1 - parity), d.last * parity


def first_kernel(
    d, face_ref, iface_hbm, cols_hbm, inflow, coupling, inv, rhs, diag_hbm, off_hbm, *rest
):
    early, later, gfield, *buffers, tiles, diag, off, iface, cols, right, flow, couple, sems = rest
    w = d.width
    moves = [(iface_hbm, iface), (inflow, flow), (coupling, couple), (inv, tiles)]
    moves += [(rhs.at[t], right.at[t]) for t in range(d.ticks)]
    moves += [(cols_hbm, cols), (diag_hbm, diag), (off_hbm, off)]
    copies = [pltpu.make_async_copy(a, b, sems.at[i]) for i, (a, b) in enumerate(moves)]
    for copy in copies:
        copy.start()
    for copy in copies[:4]:
        copy.wait()
    coupled = []
    for q in range(d.nq):
        turned = couple[q].astype(F32).T.astype(BF)
        gfield[q] = dot_nt(turned, tiles[iface[q]]).astype(BF)
        coupled.append(dot_nn(flow[:, q * w : (q + 1) * w], turned))
    for copy in copies[4 : 4 + d.ticks]:
        copy.wait()
    for r in range(d.count):
        x = jnp.concatenate([right[t, :, r * w : (r + 1) * w] for t in range(d.ticks)], axis=0)
        value = dot_nt(x, tiles[r]).astype(BF)
        early[r] = value[: d.early]
        later[r] = value[d.early :]
    for q in range(d.nq):
        row = iface[q]
        corrected = right[0, :, pl.ds(pl.multiple_of(row * w, w), w)].astype(F32) - coupled[q]
        early[row, 0 : d.sources, :] = dot_nt(corrected.astype(BF), tiles[row]).astype(BF)
    for i, start in enumerate(edge_rows(d, lax.rem(face_ref[0], 2))):
        buffers[i][...] = early[pl.ds(start, HALO)]
        buffer = buffers[2 + i]
        buffer[:, 0 : d.later, :] = later[pl.ds(start, HALO)]
        for q in range(d.nq):
            at = d.later + q // HALO * w
            buffer[q % HALO, at : at + w, :] = gfield[q]
            at = d.later + d.share + q * d.mark
            for e in range(HALO):
                buffer[e, at : at + d.mark, :] = jnp.full((d.mark, w), iface[q] == start + e).astype(F32).astype(BF)
    for copy in copies[4 + d.ticks :]:
        copy.wait()


def fold_kernel(d, face_ref, iface, cols, inv, diag, off, folded, met):
    w = d.width
    for r in range(d.count):
        tiles = jnp.concatenate([diag[r]] + [off[r, k] for k in range(d.neigh)], axis=1)
        product = dot_nn(inv[r], tiles)
        rows = lax.broadcasted_iota(jnp.int32, (w, w), 0)
        unit = (rows == lax.broadcasted_iota(jnp.int32, (w, w), 1)).astype(F32)
        for k in range(1 + d.neigh):
            part = product[:, k * w : (k + 1) * w].T
            folded[r, k * w : (k + 1) * w, :] = ((unit if k == 0 else 0.0) - part).astype(BF)
    met[...] = jnp.zeros_like(met)
    for r in range(d.count):
        lanes = slice(r * w, (r + 1) * w)
        for q in range(d.nq):
            met[2 * HALO + q, :, lanes] = jnp.where(iface[q] == r, folded[r, 0:w, :], jnp.zeros((w, w), BF))
        for k in range(d.neigh):
            c = cols[k, r] - d.first_col(face_ref[0])
            inside = jnp.logical_and(c >= HALO, c < d.up)
            at = jnp.where(c < HALO, c, c - d.count)
            hit = jnp.logical_not(inside)
            for q in range(d.nq):
                here = c == iface[q] + HALO
                at = jnp.where(here, 2 * HALO + q, at)
                hit = jnp.logical_or(hit, here)

            @pl.when(hit)
            def _():
                met[at, :, lanes] += folded[r, (1 + k) * w : (2 + k) * w, :]


def sweep(d, cols, face, ext, span, r, folded):
    x = [ext[r + HALO, span, :]] + [ext[cols[k, r] - d.first_col(face), span, :] for k in range(d.neigh)]
    return dot_nn(jnp.concatenate(x, axis=1), folded[r])


def place_halo(d, face, pair_in, cross_in, ext, rows):
    parity = lax.rem(face, 2)
    ext[pl.ds(d.up * (1 - parity), HALO)] = pair_in[:, rows, :]
    ext[pl.ds(d.up * parity, HALO)] = cross_in[:, rows, :]


def extend(d, face, edges, inner, pair_in, cross_in, ext, rows):
    ext[HALO : 2 * HALO] = edges[0:HALO, rows, :]
    ext[2 * HALO : d.count] = inner[:, rows, :]
    ext[d.count : d.up] = edges[HALO : 2 * HALO, rows, :]
    place_halo(d, face, pair_in, cross_in, ext, rows)


def correct(d, cols, face, base, folded, out, ext, rows):
    for i, r in enumerate(rows):
        for span in spans(out.shape[1]):
            value = base[r, span, :].astype(F32) + sweep(d, cols, face, ext, span, r, folded)
            out[i, span, :] = value.astype(BF)


def correct_edges(d, cols, face, field, pair_in, cross_in, folded, edges, ext):
    ext[HALO : HALO + d.count] = field[...]
    place_halo(d, face, pair_in, cross_in, ext, pl.ds(0, field.shape[1]))
    correct(d, cols, face, field, folded, edges, ext, list(range(HALO)) + list(range(d.last, d.count)))


def second_edges_kernel(d, face_ref, cols, field, pair_in, cross_in, folded, edges, pair, cross, ext):
    face = face_ref[0]
    parity = lax.rem(face, 2)
    correct_edges(d, cols, face, field, pair_in, cross_in, folded, edges, ext)
    pair[...] = edges[pl.ds(HALO * (1 - parity), HALO)]
    cross[...] = edges[pl.ds(HALO * parity, HALO)]


def second_inner_kernel(d, face_ref, cols, field, ext, folded, after, out):
    correct(d, cols, face_ref[0], field, folded, out, ext, range(HALO, d.last))


def interface_rows(d, face, iface, cols, edges, inner, field, pair_in, cross_in, folded, first, outs, ext):
    ticks = pl.ds(first * d.sources, len(outs) * d.sources)
    extend(d, face, edges, inner, pair_in, cross_in, ext, ticks)
    for q in range(d.nq):
        row = iface[q]
        value = sweep(d, cols, face, ext, pl.ds(0, len(outs) * d.sources), row, folded)
        value = (field[row, ticks, :].astype(F32) + value).astype(BF)
        for t, out in enumerate(outs):
            out[q] = value[t * d.sources : (t + 1) * d.sources]


def third_rows_kernel(d, face_ref, iface, cols, edges, inner, field, pair_in, cross_in, folded, sent, ext):
    interface_rows(d, face_ref[0], iface, cols, edges, inner, field, pair_in, cross_in, folded, 0, [sent], ext)


def third_kernel(d, face_ref, cols, *rest):
    *inputs, folded, after, early, later, early_ext, later_ext = rest
    face = face_ref[0]
    for i, (out, ext) in enumerate(((early, early_ext), (later, later_ext))):
        edges, inner, field, pair_in, cross_in = inputs[5 * i : 5 * i + 5]
        extend(d, face, edges, inner, pair_in, cross_in, ext, pl.ds(0, out.shape[1]))
        correct(d, cols, face, field, folded, out, ext, range(d.count))


def marked(d, block, e):
    parts = []
    for q in range(d.nq):
        at = d.later + q // HALO * d.width
        mark = d.later + d.share + q * d.mark
        mark = block[e, mark : mark + d.mark, :]
        parts.append(block[q % HALO, at : at + d.width, :] * jnp.concatenate([mark] * (d.width // d.mark), axis=0))
    return jnp.concatenate(parts, axis=0)


def behind_kernel(
    d, face_ref, iface, cols, field, gfield, pair_in, cross_in, met, folded, after, edges, out, pair, cross, field_ext
):
    face = face_ref[0]
    parity = lax.rem(face, 2)
    correct_edges(d, cols, face, field, pair_in, cross_in, folded, edges, field_ext)
    pair[:, 0 : d.later, :] = edges[pl.ds(HALO * (1 - parity), HALO)]
    cross[:, 0 : d.later, :] = edges[pl.ds(HALO * parity, HALO)]
    w = d.width
    for shift in range(2, d.slots - 1):
        out[:, pl.ds(d.start(face + shift), d.group), :] = jnp.zeros((d.count, d.group, w), BF)

    def put(start, rows, value):
        for r in range(d.count):
            out[r, pl.ds(start, rows), :] = value[:, r * w : (r + 1) * w].astype(BF)

    pair_face, cross_face = face + 1 - 2 * parity, face - 1 + 2 * parity
    for at, other, block in ((HALO * (1 - parity), pair_face, pair_in), (HALO * parity, cross_face, cross_in)):
        x = jnp.concatenate([marked(d, block, e) for e in range(HALO)], axis=1)
        tiles = jnp.concatenate([met[at + e] for e in range(HALO)], axis=0)
        put(d.start(other), d.group, dot_nn(x, tiles))
    for q in range(d.nq):
        start = d.start(face) + q * w
        put(start, w, dot_nn(gfield[q], met[2 * HALO + q]))
        row = iface[q]
        span = pl.ds(pl.multiple_of(start, w), w)
        out[row, span, :] = (out[row, span, :].astype(F32) + gfield[q].astype(F32)).astype(BF)
    for start, buffer in zip(edge_rows(d, parity), (pair, cross)):
        for i, shift in enumerate((-1, 0, 1)):
            at = d.later + i * d.group
            buffer[:, at : at + d.group, :] = out[pl.ds(start, HALO), pl.ds(d.start(face + shift), d.group), :]


def coupling_ext(d, face, gfirst, pair_in, cross_in, ext):
    parity = lax.rem(face, 2)
    ext[0:HALO] = jnp.zeros((HALO, d.wide, d.width), BF)
    ext[d.up : d.ext] = jnp.zeros((HALO, d.wide, d.width), BF)
    ext[HALO : HALO + d.count] = gfirst[...]
    neighbours = ((d.up * (1 - parity), face + 1 - 2 * parity, pair_in), (d.up * parity, face - 1 + 2 * parity, cross_in))
    for start, other, block in neighbours:
        for i, shift in enumerate((-1, 0, 1)):
            at = d.later + i * d.group
            ext[pl.ds(start, HALO), pl.ds(d.start(other + shift), d.group), :] = block[:, at : at + d.group, :]


def rest_kernel(d, first, face_ref, iface, cols, edges, field, ext0, pair_in, cross_in, folded, after, inner, faces_out, ext):
    face = face_ref[0]
    correct(d, cols, face, field, folded, inner, ext0, range(HALO, d.last))
    outs = [faces_out.at[t] for t in range(faces_out.shape[0])]
    interface_rows(d, face, iface, cols, edges, inner, field, pair_in, cross_in, folded, first, outs, ext)


def interface_kernel(d, face_ref, iface, cols, gfield, gfirst, pair_in, cross_in, folded, after, *rest):
    *chain, ext = rest
    face = face_ref[0]
    w = d.width
    coupling_ext(d, face, gfirst, pair_in, cross_in, ext)
    for i in range(d.slots):
        start = i * d.group % d.part
        part = chain[i * d.group // d.part]
        for q in range(d.nq):
            value = sweep(d, cols, face, ext, pl.ds(i * d.group, d.group), iface[q], folded)
            part[start : start + d.group, q * w : (q + 1) * w] = value.astype(BF)

        @pl.when(lax.rem(face, d.slots) == i)
        def _():
            for q in range(d.nq):
                block = (slice(start + q * w, start + (q + 1) * w), slice(q * w, (q + 1) * w))
                part[block] = (part[block].astype(F32) + gfield[q].astype(F32)).astype(BF)


def operator_rows(d, face, iface, cols, gfield, folded, ext, rows, out):
    w = d.width
    for i, r in enumerate(rows):
        for s in range(0, d.wide, d.group):
            span = pl.ds(s, d.group)
            out[span, i * w : (i + 1) * w] = sweep(d, cols, face, ext, span, r, folded).astype(BF)
    for q in range(d.nq):

        @pl.when(jnp.logical_and(iface[q] >= rows[0], iface[q] <= rows[-1]))
        def _():
            lane = pl.ds(pl.multiple_of((iface[q] - rows[0]) * w, w), w)
            span = pl.ds(pl.multiple_of(d.start(face) + q * w, w), w)
            out[span, lane] = (out[span, lane].astype(F32) + gfield[q].astype(F32)).astype(BF)


def operator_kernel(d, face_ref, iface, cols, gfield, gfirst, pair_in, cross_in, folded, after, out, ext):
    coupling_ext(d, face_ref[0], gfirst, pair_in, cross_in, ext)
    operator_rows(d, face_ref[0], iface, cols, gfield, folded, ext, range(d.count // 2), out)


def operator_rest_kernel(d, face_ref, iface, cols, gfield, folded, ext, after, out):
    operator_rows(d, face_ref[0], iface, cols, gfield, folded, ext, range(d.count // 2, d.count), out)


def operator_part(d, halves, row, depth, lane, lanes):
    width = halves[0].shape[1]
    half = halves[lane // width]
    return half[pl.ds(row, depth), lane % width : lane % width + lanes]


def chip_hops(faces):
    return [(0, None)] if faces <= 2 else [(0, 1)] if faces <= 4 else [(0, 1), (-1, None)]


def hop_face(faces, face, hop):
    return face ^ (2 * hop) if faces <= 4 else face + 2 * hop


def arrived_blocks(d, face, own, other):
    parity = lax.rem(face, 2)
    for i, hops in enumerate(chip_hops(d.faces)):
        starts = [0 if hop is None else d.start(hop_face(d.faces, face - parity, hop)) for hop in hops]
        for block, odd in ((own[i], parity), (other[i], 1 - parity)):
            start = pl.multiple_of(jnp.where(odd == 1, starts[1], starts[0]), d.group)
            yield jnp.concatenate([block[j] for j in range(2 * d.nq)], axis=1), start


def chain_kernel(d, tick, face_ref, *rest):
    own_chain, other_chain, rest = rest[: d.parts], rest[d.parts : 2 * d.parts], rest[2 * d.parts :]
    own_faces, other_faces, *arrived, sent, chain = rest
    face = face_ref[0]
    parity = lax.rem(face, 2)
    for i in range(d.parts):
        for j, part in enumerate((own_chain[i], other_chain[i])):
            chain[i * d.part : (i + 1) * d.part, j * d.group : (j + 1) * d.group] = part[...]
    half = len(arrived) // 2
    total = jnp.zeros((d.sources, 2 * d.group), F32)
    for x, start in arrived_blocks(d, face, arrived[:half], arrived[half:]):
        total += dot_nn(x, chain[pl.ds(start, 2 * d.group), :])
    for j, (base, odd) in enumerate(((own_faces, parity), (other_faces, 1 - parity))):
        for q in range(d.nq):
            at = j * d.group + q * d.width
            sent[odd * d.nq + q] = (base[tick, q].astype(F32) - total[:, at : at + d.width]).astype(BF)


def merge_kernel(d, face_ref, own, other, sent):
    parity = lax.rem(face_ref[0], 2)
    for q in range(d.nq):
        sent[parity * d.nq + q] = own[q]
        sent[(1 - parity) * d.nq + q] = other[q]


def tick_rows(d, early, later, tick, row):
    fields, at = (early, tick) if tick < d.split else (later, tick - d.split)
    return fields[row, at * d.sources : (at + 1) * d.sources, :].astype(F32)


def output_kernel(d, face_ref, early, later, first_half, second_half, *rest):
    *arrived, out, held, sems = rest
    w = d.width
    each = 2 * len(chip_hops(d.faces))
    copies = []
    part = 2 * w
    for t in range(d.ticks - 1):
        blocks = []
        if t:
            mine, arrived = arrived[:each], arrived[each:]
            blocks = list(arrived_blocks(d, face_ref[0], mine[: each // 2], mine[each // 2 :]))
        for c in range(0, d.count * w, part):
            total = jnp.zeros((d.sources, part), F32)
            for x, start in blocks:
                total += dot_nn(x, operator_part(d, (first_half, second_half), start, 2 * d.group, c, part))
            for j in range(0, part, w):
                value = tick_rows(d, early, later, t, (c + j) // w) - total[:, j : j + w]
                held[t, :, c + j : c + j + w] = value.astype(BF)
        copies.append(pltpu.make_async_copy(held.at[t], out.at[t], sems.at[t]))
        copies[-1].start()
    for copy in copies:
        copy.wait()


def last_own_kernel(d, face_ref, early, later, first_half, second_half, *rest):
    own, out = rest[:-1], rest[-1]
    w = d.width
    blocks = list(arrived_blocks(d, face_ref[0], own, own))[0::2]
    for c in range(0, d.count * w, 2 * w):
        total = jnp.zeros((d.sources, 2 * w), F32)
        for x, start in blocks:
            total += dot_nn(x, operator_part(d, (first_half, second_half), start, 2 * d.group, c, 2 * w))
        for j in range(0, 2 * w, w):
            out[:, c + j : c + j + w] = tick_rows(d, early, later, d.ticks - 1, (c + j) // w) - total[:, j : j + w]


def last_other_kernel(d, face_ref, own_part, first_half, second_half, earlier, *rest):
    other, (out, held, sems) = rest[:-3], rest[-3:]
    blocks = list(arrived_blocks(d, face_ref[0], other, other))[1::2]
    part = 2 * d.width
    copies = []
    for i, c in enumerate(range(0, d.count * d.width, part)):
        total = own_part[:, c : c + part]
        for x, start in blocks:
            total -= dot_nn(x, operator_part(d, (first_half, second_half), start, 2 * d.group, c, part))
        held[:, c : c + part] = total.astype(BF)
        here = held.at[:, c : c + part]
        copies.append(pltpu.make_async_copy(here, out.at[d.ticks - 1, :, c : c + part], sems.at[i]))
        copies[-1].start()
    for copy in copies:
        copy.wait()


def call(body, name, smem, inputs, outs, scratch=(), flops=0, anywhere=(), sems=0, place=pltpu.VMEM, aliases=None):
    outs = [x if isinstance(x, jax.ShapeDtypeStruct) else jax.ShapeDtypeStruct(x, BF) for x in outs]
    specs = [pl.BlockSpec(memory_space=pl.ANY if i in anywhere else pltpu.VMEM) for i in range(len(inputs))]
    return pl.pallas_call(
        body,
        name=name,
        out_shape=outs,
        in_specs=[pl.BlockSpec(memory_space=pltpu.SMEM)] * len(smem) + specs,
        out_specs=[pl.BlockSpec(memory_space=place if x.dtype != jnp.int32 else pltpu.SMEM) for x in outs],
        scratch_shapes=[pltpu.VMEM(s, BF) for s in scratch] + ([pltpu.SemaphoreType.DMA((sems,))] if sems else []),
        input_output_aliases=aliases or {},
        compiler_params=pltpu.CompilerParams(vmem_limit_bytes=32 * 1024 * 1024),
        cost_estimate=pl.CostEstimate(flops=flops, bytes_accessed=0, transcendentals=0),
    )(*smem, *inputs)


def on_device(rhs, inflow, diag_tiles, off_tiles, cols, inverse_tiles, coupling, iface):
    faces, slabs = lax.axis_size("face"), lax.axis_size("slab")
    ticks, _, sources, _ = rhs.shape
    _, count, neigh, width, _ = off_tiles.shape
    nq = coupling.shape[1]
    d = Dims(ticks, sources, count, neigh, width, nq, faces)
    diag, off, inv, couple, cols = diag_tiles[0], off_tiles[0], inverse_tiles[0], coupling[0], cols[0].T
    face = lax.axis_index("face").astype(jnp.int32)[None]
    tile = width * width

    pairing = [(i, i ^ 1) for i in range(faces) if i ^ 1 < faces]
    crossing = [(i, ((i + 1) ^ 1) - 1) for i in range(faces) if 0 <= ((i + 1) ^ 1) - 1 < faces]

    def exchange(pair, cross):
        got = lax.ppermute(cross, "face", crossing)
        return lax.ppermute(pair, "face", pairing), got

    def swap(block):
        return lax.ppermute(block, "face", pairing)

    def onward(block, beside=lambda: None):
        own = []
        for hops in chip_hops(faces):
            route = []
            for s in range(1, slabs):
                for f in range(faces):
                    hop = hops[f % 2]
                    g = -1 if hop is None else hop_face(faces, f, hop)
                    if 0 <= g < faces:
                        route.append(((s - 1) * faces + g, s * faces + f))
            own.append(lax.ppermute(block, ("slab", "face"), route))
        made = beside()
        if made is not None:
            *own, made = lax.optimization_barrier((*own, made))
        return own + [swap(x) for x in own], made

    split, early, later, group, ext, wide = d.split, d.early, d.later, d.group, d.ext, d.wide
    sweep_flops = 2 * count * tile * (neigh + 1)
    ints = [jax.ShapeDtypeStruct(x.shape, x.dtype) for x in (iface, cols)]
    on_hbm = (iface, cols, inflow[0], couple, inv, rhs[:, 0], diag, off)
    field, field_later, gfield, pair, cross, pair_later, cross_later, inv, diag, off, iface, cols = call(
        functools.partial(first_kernel, d),
        "first",
        [face],
        [pltpu.with_memory_space_constraint(x, pltpu.HBM) for x in on_hbm],
        [(count, early, width), (count, later, width), (nq, width, width)]
        + [(HALO, early, width)] * 2
        + [(HALO, d.first_rows, width)] * 2
        + [x.shape for x in (inv, diag, off)]
        + ints,
        [(ticks, sources, count * width), (sources, group), (nq, width, width)],
        anywhere=range(8),
        sems=7 + ticks,
    )
    pair0, cross0 = exchange(pair, cross)
    pair_later0, cross_later0 = exchange(pair_later, cross_later)
    folded, met = call(
        functools.partial(fold_kernel, d),
        "fold",
        [face, iface, cols],
        [inv, diag, off],
        [(count, d.depth, width), (2 * HALO + nq, width, count * width)],
    )
    edges, pair, cross, ext0 = call(
        functools.partial(second_edges_kernel, d),
        "second_edges",
        [face, cols],
        [field, pair0, cross0, folded],
        [(2 * HALO, early, width)] + [(HALO, early, width)] * 2 + [(ext, early, width)],
    )
    pair1, cross1 = exchange(pair, cross)
    edges_later, gfirst, pair, cross, ext_later0 = call(
        functools.partial(behind_kernel, d),
        "behind",
        [face, iface, cols],
        [field_later, gfield, pair_later0, cross_later0, met, folded, pair1],
        [(2 * HALO, later, width), (count, wide, width)] + [(HALO, later + 3 * group, width)] * 2 + [(ext, later, width)],
        anywhere=(6,),
    )
    pair_later1, cross_later1 = exchange(pair, cross)
    (inner_first,) = call(
        functools.partial(second_inner_kernel, d),
        "second_inner",
        [face, cols],
        [field, ext0, folded, gfirst],
        [(count - 2 * HALO, sources, width)],
        anywhere=(3,),
    )
    cross1, inner_first = lax.optimization_barrier((cross1, inner_first))
    (own_first,) = call(
        functools.partial(third_rows_kernel, d),
        "third_rows",
        [face, iface, cols],
        [edges, inner_first, field, pair1, cross1, folded],
        [(nq, sources, width)],
        [(ext, sources, width)],
        flops=12 * early * sweep_flops,
    )
    (sent,) = call(
        functools.partial(merge_kernel, d),
        "merge",
        [face],
        [own_first, swap(own_first)],
        [(2 * nq, sources, width)],
    )

    def rest(first, ticks, rows, edges, field, ext0, pair, cross, after):
        return call(
            functools.partial(rest_kernel, d, first),
            "rest",
            [face, iface, cols],
            [edges, field, ext0, pair, cross, folded, after],
            [(count - 2 * HALO, rows, width), (ticks, nq, sources, width)],
            [(ext, ticks * sources, width)],
            anywhere=(6,),
        )

    inner, faces_early = rest(1, split - 1, early, edges, field, ext0, pair1, cross1, sent)
    early_parts = (edges, inner, field, pair1, cross1)

    def beside_first():
        rows = call(
            functools.partial(interface_kernel, d),
            "interface",
            [face, iface, cols],
            [gfield, gfirst, pair_later1, cross_later1, folded, inner],
            [(d.part, group)] * d.parts,
            [(ext, wide, width)],
            anywhere=(5,),
        )
        return rows, [swap(x) for x in rows]

    arrived, (chain, other_chain) = onward(sent, beside_first)
    other_early = swap(faces_early)

    def beside_second(sent):
        made = rest(0, ticks - 1 - split, later, edges_later, field_later, ext_later0, pair_later1, cross_later1, sent)
        return *operator(), *made, swap(made[1])

    def fields(after):
        return call(
            functools.partial(third_kernel, d),
            "third",
            [face, cols],
            [*early_parts, *later_parts, folded, after],
            [(count, early, width), (count, later, width)],
            [(ext, early, width), (ext, later, width)],
            anywhere=(11,),
        )

    whole = (ticks, sources, count * width)

    def operator():
        return call(
            functools.partial(operator_kernel, d),
            "operator",
            [face, iface, cols],
            [gfield, gfirst, pair_later1, cross_later1, folded, chain[0]],
            [(wide, count // 2 * width), (ext, wide, width)],
            flops=wide * sweep_flops // 2,
            anywhere=(5,),
        )

    def operator_rest(after):
        return call(
            functools.partial(operator_rest_kernel, d),
            "operator_rest",
            [face, iface, cols],
            [gfield, folded, read, after],
            [(wide, (count - count // 2) * width)],
            anywhere=(3,),
        )[0]

    def output(blocks):
        return call(
            functools.partial(output_kernel, d),
            "output",
            [face],
            [*twice, first_half, second_half] + blocks,
            [whole],
            [(ticks - 1, sources, count * width)],
            sems=ticks - 1,
            place=pl.ANY,
        )[0]

    everything = []
    most = None
    for tick in range(1, ticks):
        everything += arrived
        if tick == ticks - 1:
            break
        early_tick = tick < split
        bases = (faces_early, other_early) if early_tick else (faces_later, other_later)
        (sent,) = call(
            functools.partial(chain_kernel, d, tick - 1 if early_tick else tick - split),
            "chain",
            [face],
            [*chain, *other_chain, *bases] + arrived,
            [(2 * nq, sources, width)],
            [(wide, 2 * group)],
            flops=4 * sources * wide * group,
        )
        if tick == 1:
            arrived, (first_half, read, inner_later, faces_later, other_later) = onward(sent, functools.partial(beside_second, sent))
            later_parts = (edges_later, inner_later, field_later, pair_later1, cross_later1)
        else:
            twice = fields(sent)
            second_half = operator_rest(sent)
            arrived, most = onward(sent, lambda: output(everything))
    half = len(arrived) // 2
    (own_part,) = call(
        functools.partial(last_own_kernel, d),
        "last_own",
        [face],
        [*twice, first_half, second_half] + arrived[:half],
        [jax.ShapeDtypeStruct((sources, count * width), F32)],
    )
    (out,) = call(
        functools.partial(last_other_kernel, d),
        "last_other",
        [face],
        [own_part, first_half, second_half, most] + arrived[half:],
        [whole],
        [(sources, count * width)],
        anywhere=(3,),
        sems=count,
        place=pl.ANY,
        aliases={4: 0},
    )
    return out[:, None]


def solution(mesh):
    placed = (
        P(None, "slab", None, "face"),
        P("slab", None, "face"),
        P("slab", "face", None, None),
        P("slab", "face", None, None, None),
        P("slab", "face", None),
        P("slab", "face", None, None),
        P("slab", "face", None, None),
        P("face"),
    )
    return jax.shard_map(
        on_device,
        mesh=mesh,
        in_specs=placed,
        out_specs=P(None, "slab", None, "face"),
        check_vma=False,
    )
```

```python
import functools
import math

import jax
import jax.numpy as jnp
from jax import lax
from jax.experimental import pallas as pl
from jax.experimental.pallas import tpu as pltpu
from jax.sharding import PartitionSpec as P

HALO = 2
BF = jnp.bfloat16
F32 = jnp.float32


def dot_nt(a, b):
    return lax.dot_general(a, b, (((1,), (1,)), ((), ())), preferred_element_type=F32)


def dot_nn(a, b):
    return lax.dot_general(a, b, (((1,), (0,)), ((), ())), preferred_element_type=F32)


class Dims:
    def __init__(self, ticks, sources, count, neigh, width, nq, faces):
        self.ticks, self.sources, self.count, self.neigh = ticks, sources, count, neigh
        self.width, self.nq, self.faces = width, nq, faces
        self.split = max(ticks // 2, 1)
        self.early, self.later = self.split * sources, (ticks - self.split) * sources
        self.group = nq * width
        self.ext = count + 2 * HALO
        self.depth = (1 + neigh) * width
        self.slots = 4 if faces <= 4 else 6
        self.wide = self.slots * self.group
        self.parts = 4 if self.slots % 4 == 0 else 3
        self.part = self.wide // self.parts
        self.mark = 16
        self.share = -(-nq // HALO) * width
        self.first_rows = self.later + self.share + nq * self.mark
        self.last = count - HALO
        self.up = count + HALO

    def start(self, face):
        return pl.multiple_of(lax.rem(face + 2 * self.slots, self.slots) * self.group, self.group)

    def first_col(self, face):
        return face * self.count - HALO


def spans(rows):
    parts = -(-rows // 256)
    return [pl.ds(i * (rows // parts), rows // parts) for i in range(parts)]


def edge_rows(d, parity):
    return d.last * (1 - parity), d.last * parity


def first_kernel(
    d, face_ref, iface_hbm, cols_hbm, inflow, coupling, inv, rhs, diag_hbm, off_hbm, *rest
):
    early, later, gfield, *buffers, tiles, diag, off, iface, cols, right, flow, couple, sems = rest
    w = d.width
    moves = [(iface_hbm, iface), (inflow, flow), (coupling, couple), (inv, tiles)]
    moves += [(rhs.at[t], right.at[t]) for t in range(d.ticks)]
    moves += [(cols_hbm, cols), (diag_hbm, diag), (off_hbm, off)]
    copies = [pltpu.make_async_copy(a, b, sems.at[i]) for i, (a, b) in enumerate(moves)]
    for copy in copies:
        copy.start()
    for copy in copies[:4]:
        copy.wait()
    coupled = []
    for q in range(d.nq):
        turned = couple[q].astype(F32).T.astype(BF)
        gfield[q] = dot_nt(turned, tiles[iface[q]]).astype(BF)
        coupled.append(dot_nn(flow[:, q * w : (q + 1) * w], turned))
    for copy in copies[4 : 4 + d.ticks]:
        copy.wait()
    for r in range(d.count):
        x = jnp.concatenate([right[t, :, r * w : (r + 1) * w] for t in range(d.ticks)], axis=0)
        value = dot_nt(x, tiles[r]).astype(BF)
        early[r] = value[: d.early]
        later[r] = value[d.early :]
    for q in range(d.nq):
        row = iface[q]
        corrected = right[0, :, pl.ds(pl.multiple_of(row * w, w), w)].astype(F32) - coupled[q]
        early[row, 0 : d.sources, :] = dot_nt(corrected.astype(BF), tiles[row]).astype(BF)
    for i, start in enumerate(edge_rows(d, lax.rem(face_ref[0], 2))):
        buffers[i][...] = early[pl.ds(start, HALO)]
        buffer = buffers[2 + i]
        buffer[:, 0 : d.later, :] = later[pl.ds(start, HALO)]
        for q in range(d.nq):
            at = d.later + q // HALO * w
            buffer[q % HALO, at : at + w, :] = gfield[q]
            at = d.later + d.share + q * d.mark
            for e in range(HALO):
                buffer[e, at : at + d.mark, :] = jnp.full((d.mark, w), iface[q] == start + e).astype(F32).astype(BF)
    for copy in copies[4 + d.ticks :]:
        copy.wait()


def fold_kernel(d, face_ref, iface, cols, inv, diag, off, folded, met):
    w = d.width
    for r in range(d.count):
        tiles = jnp.concatenate([diag[r]] + [off[r, k] for k in range(d.neigh)], axis=1)
        product = dot_nn(inv[r], tiles)
        rows = lax.broadcasted_iota(jnp.int32, (w, w), 0)
        unit = (rows == lax.broadcasted_iota(jnp.int32, (w, w), 1)).astype(F32)
        for k in range(1 + d.neigh):
            part = product[:, k * w : (k + 1) * w].T
            folded[r, k * w : (k + 1) * w, :] = ((unit if k == 0 else 0.0) - part).astype(BF)
    spare = 2 * HALO + d.nq
    met[0 : 2 * HALO] = jnp.zeros((2 * HALO, w, d.count * w), BF)
    for r in range(d.count):
        lanes = slice(r * w, (r + 1) * w)
        for q in range(d.nq):
            met[2 * HALO + q, :, lanes] = jnp.where(iface[q] == r, folded[r, 0:w, :], jnp.zeros((w, w), BF))
        for k in range(d.neigh):
            c = cols[k, r] - d.first_col(face_ref[0])
            at = jnp.where(c < HALO, c, jnp.where(c >= d.up, c - d.count, spare))
            for q in range(d.nq):
                at = jnp.where(c == iface[q] + HALO, 2 * HALO + q, at)
            met[at, :, lanes] += folded[r, (1 + k) * w : (2 + k) * w, :]


def sweep(d, cols, face, ext, span, r, folded):
    x = [ext[r + HALO, span, :]] + [ext[cols[k, r] - d.first_col(face), span, :] for k in range(d.neigh)]
    return dot_nn(jnp.concatenate(x, axis=1), folded[r])


def place_halo(d, face, pair_in, cross_in, ext, rows):
    parity = lax.rem(face, 2)
    ext[pl.ds(d.up * (1 - parity), HALO)] = pair_in[:, rows, :]
    ext[pl.ds(d.up * parity, HALO)] = cross_in[:, rows, :]


def extend(d, face, edges, inner, pair_in, cross_in, ext, rows):
    ext[HALO : 2 * HALO] = edges[0:HALO, rows, :]
    ext[2 * HALO : d.count] = inner[:, rows, :]
    ext[d.count : d.up] = edges[HALO : 2 * HALO, rows, :]
    place_halo(d, face, pair_in, cross_in, ext, rows)


def correct(d, cols, face, base, folded, out, ext, rows):
    for i, r in enumerate(rows):
        for span in spans(out.shape[1]):
            value = base[r, span, :].astype(F32) + sweep(d, cols, face, ext, span, r, folded)
            out[i, span, :] = value.astype(BF)


def correct_edges(d, cols, face, field, pair_in, cross_in, folded, edges, ext):
    ext[HALO : HALO + d.count] = field[...]
    place_halo(d, face, pair_in, cross_in, ext, pl.ds(0, field.shape[1]))
    correct(d, cols, face, field, folded, edges, ext, list(range(HALO)) + list(range(d.last, d.count)))


def second_edges_kernel(d, face_ref, cols, field, pair_in, cross_in, folded, edges, pair, cross, ext):
    face = face_ref[0]
    parity = lax.rem(face, 2)
    correct_edges(d, cols, face, field, pair_in, cross_in, folded, edges, ext)
    pair[...] = edges[pl.ds(HALO * (1 - parity), HALO)]
    cross[...] = edges[pl.ds(HALO * parity, HALO)]


def interface_rows(d, face, iface, cols, edges, inner, field, pair_in, cross_in, folded, first, outs, ext):
    ticks = pl.ds(first * d.sources, len(outs) * d.sources)
    extend(d, face, edges, inner, pair_in, cross_in, ext, ticks)
    for q in range(d.nq):
        row = iface[q]
        value = sweep(d, cols, face, ext, pl.ds(0, len(outs) * d.sources), row, folded)
        value = (field[row, ticks, :].astype(F32) + value).astype(BF)
        for t, out in enumerate(outs):
            out[q] = value[t * d.sources : (t + 1) * d.sources]


def third_rows_kernel(d, face_ref, iface, cols, edges, field, ext0, pair_in, cross_in, folded, after, sent, inner, ext):
    face = face_ref[0]
    correct(d, cols, face, field, folded, inner, ext0, range(HALO, d.last))
    interface_rows(d, face, iface, cols, edges, inner, field, pair_in, cross_in, folded, 0, [sent], ext)


def third_kernel(d, face_ref, cols, *rest):
    *inputs, folded, after, early, later, early_ext, later_ext = rest
    face = face_ref[0]
    for i, (out, ext) in enumerate(((early, early_ext), (later, later_ext))):
        edges, inner, field, pair_in, cross_in = inputs[5 * i : 5 * i + 5]
        extend(d, face, edges, inner, pair_in, cross_in, ext, pl.ds(0, out.shape[1]))
        correct(d, cols, face, field, folded, out, ext, range(d.count))


def marked(d, block, e):
    parts = []
    for q in range(d.nq):
        at = d.later + q // HALO * d.width
        mark = d.later + d.share + q * d.mark
        mark = block[e, mark : mark + d.mark, :]
        parts.append(block[q % HALO, at : at + d.width, :] * jnp.concatenate([mark] * (d.width // d.mark), axis=0))
    return jnp.concatenate(parts, axis=0)


def behind_kernel(
    d, face_ref, iface, cols, field, gfield, pair_in, cross_in, met, folded, after, edges, out, pair, cross, field_ext
):
    face = face_ref[0]
    parity = lax.rem(face, 2)
    correct_edges(d, cols, face, field, pair_in, cross_in, folded, edges, field_ext)
    pair[:, 0 : d.later, :] = edges[pl.ds(HALO * (1 - parity), HALO)]
    cross[:, 0 : d.later, :] = edges[pl.ds(HALO * parity, HALO)]
    w = d.width
    for shift in range(2, d.slots - 1):
        out[:, pl.ds(d.start(face + shift), d.group), :] = jnp.zeros((d.count, d.group, w), BF)

    def put(start, rows, value):
        for r in range(d.count):
            out[r, pl.ds(start, rows), :] = value[:, r * w : (r + 1) * w].astype(BF)

    pair_face, cross_face = face + 1 - 2 * parity, face - 1 + 2 * parity
    for at, other, block in ((HALO * (1 - parity), pair_face, pair_in), (HALO * parity, cross_face, cross_in)):
        x = jnp.concatenate([marked(d, block, e) for e in range(HALO)], axis=1)
        tiles = jnp.concatenate([met[at + e] for e in range(HALO)], axis=0)
        put(d.start(other), d.group, dot_nn(x, tiles))
    for q in range(d.nq):
        start = d.start(face) + q * w
        put(start, w, dot_nn(gfield[q], met[2 * HALO + q]))
        row = iface[q]
        span = pl.ds(pl.multiple_of(start, w), w)
        out[row, span, :] = (out[row, span, :].astype(F32) + gfield[q].astype(F32)).astype(BF)
    for start, buffer in zip(edge_rows(d, parity), (pair, cross)):
        for i, shift in enumerate((-1, 0, 1)):
            at = d.later + i * d.group
            buffer[:, at : at + d.group, :] = out[pl.ds(start, HALO), pl.ds(d.start(face + shift), d.group), :]


def coupling_ext(d, face, gfirst, pair_in, cross_in, ext):
    parity = lax.rem(face, 2)
    ext[0:HALO] = jnp.zeros((HALO, d.wide, d.width), BF)
    ext[d.up : d.ext] = jnp.zeros((HALO, d.wide, d.width), BF)
    ext[HALO : HALO + d.count] = gfirst[...]
    neighbours = ((d.up * (1 - parity), face + 1 - 2 * parity, pair_in), (d.up * parity, face - 1 + 2 * parity, cross_in))
    for start, other, block in neighbours:
        for i, shift in enumerate((-1, 0, 1)):
            at = d.later + i * d.group
            ext[pl.ds(start, HALO), pl.ds(d.start(other + shift), d.group), :] = block[:, at : at + d.group, :]


def rest_kernel(d, first, face_ref, iface, cols, edges, field, ext0, pair_in, cross_in, folded, after, inner, faces_out, ext):
    face = face_ref[0]
    correct(d, cols, face, field, folded, inner, ext0, range(HALO, d.last))
    outs = [faces_out.at[t] for t in range(faces_out.shape[0])]
    interface_rows(d, face, iface, cols, edges, inner, field, pair_in, cross_in, folded, first, outs, ext)


def interface_kernel(d, face_ref, iface, cols, gfield, gfirst, pair_in, cross_in, folded, after, *rest):
    *chain, ext = rest
    face = face_ref[0]
    w = d.width
    coupling_ext(d, face, gfirst, pair_in, cross_in, ext)
    for i in range(d.slots):
        start = i * d.group % d.part
        part = chain[i * d.group // d.part]
        for q in range(d.nq):
            value = sweep(d, cols, face, ext, pl.ds(i * d.group, d.group), iface[q], folded)
            part[start : start + d.group, q * w : (q + 1) * w] = value.astype(BF)

        @pl.when(lax.rem(face, d.slots) == i)
        def _():
            for q in range(d.nq):
                block = (slice(start + q * w, start + (q + 1) * w), slice(q * w, (q + 1) * w))
                part[block] = (part[block].astype(F32) + gfield[q].astype(F32)).astype(BF)


def coupling_last_kernel(d, face_ref, iface, cols, gfield, gfirst, pair_in, cross_in, folded, after, out, ext):
    face = face_ref[0]
    w = d.width
    coupling_ext(d, face, gfirst, pair_in, cross_in, ext)
    for r in range(d.count):
        for s in range(0, d.wide, d.group):
            span = pl.ds(s, d.group)
            out[span, r * w : (r + 1) * w] = sweep(d, cols, face, ext, span, r, folded).astype(BF)
    for q in range(d.nq):
        lane = pl.ds(pl.multiple_of(iface[q] * w, w), w)
        span = pl.ds(pl.multiple_of(d.start(face) + q * w, w), w)
        out[span, lane] = (out[span, lane].astype(F32) + gfield[q].astype(F32)).astype(BF)


def chip_hops(faces):
    return [(0, None)] if faces <= 2 else [(0, 1)] if faces <= 4 else [(0, 1), (-1, None)]


def hop_face(faces, face, hop):
    return face ^ (2 * hop) if faces <= 4 else face + 2 * hop


def arrived_blocks(d, face, own, other):
    parity = lax.rem(face, 2)
    for i, hops in enumerate(chip_hops(d.faces)):
        starts = [0 if hop is None else d.start(hop_face(d.faces, face - parity, hop)) for hop in hops]
        for block, odd in ((own[i], parity), (other[i], 1 - parity)):
            start = pl.multiple_of(jnp.where(odd == 1, starts[1], starts[0]), d.group)
            yield jnp.concatenate([block[j] for j in range(2 * d.nq)], axis=1), start


def chain_kernel(d, tick, face_ref, *rest):
    own_chain, other_chain, rest = rest[: d.parts], rest[d.parts : 2 * d.parts], rest[2 * d.parts :]
    own_faces, other_faces, *arrived, sent, chain = rest
    face = face_ref[0]
    parity = lax.rem(face, 2)
    for i in range(d.parts):
        for j, part in enumerate((own_chain[i], other_chain[i])):
            chain[i * d.part : (i + 1) * d.part, j * d.group : (j + 1) * d.group] = part[...]
    half = len(arrived) // 2
    total = jnp.zeros((d.sources, 2 * d.group), F32)
    for x, start in arrived_blocks(d, face, arrived[:half], arrived[half:]):
        total += dot_nn(x, chain[pl.ds(start, 2 * d.group), :])
    for j, (base, odd) in enumerate(((own_faces, parity), (other_faces, 1 - parity))):
        for q in range(d.nq):
            at = j * d.group + q * d.width
            sent[odd * d.nq + q] = (base[tick, q].astype(F32) - total[:, at : at + d.width]).astype(BF)


def merge_kernel(d, face_ref, own, other, sent):
    parity = lax.rem(face_ref[0], 2)
    for q in range(d.nq):
        sent[parity * d.nq + q] = own[q]
        sent[(1 - parity) * d.nq + q] = other[q]


def tick_rows(d, early, later, tick, row):
    fields, at = (early, tick) if tick < d.split else (later, tick - d.split)
    return fields[row, at * d.sources : (at + 1) * d.sources, :].astype(F32)


def output_kernel(d, face_ref, early, later, coupled, *rest):
    *arrived, out, held, sems = rest
    w = d.width
    each = 2 * len(chip_hops(d.faces))
    copies = []
    part = 2 * w
    for t in range(d.ticks - 1):
        blocks = []
        if t:
            mine, arrived = arrived[:each], arrived[each:]
            blocks = list(arrived_blocks(d, face_ref[0], mine[: each // 2], mine[each // 2 :]))
        for c in range(0, d.count * w, part):
            total = jnp.zeros((d.sources, part), F32)
            for x, start in blocks:
                total += dot_nn(x, coupled[pl.ds(start, 2 * d.group), c : c + part])
            for j in range(0, part, w):
                value = tick_rows(d, early, later, t, (c + j) // w) - total[:, j : j + w]
                held[t, :, c + j : c + j + w] = value.astype(BF)
        copies.append(pltpu.make_async_copy(held.at[t], out.at[t], sems.at[t]))
        copies[-1].start()
    for copy in copies:
        copy.wait()


def last_own_kernel(d, face_ref, early, later, coupled, *rest):
    own, out = rest[:-1], rest[-1]
    w = d.width
    total = jnp.zeros((d.sources, d.count * w), F32)
    for x, start in list(arrived_blocks(d, face_ref[0], own, own))[0::2]:
        total += dot_nn(x, coupled[pl.ds(start, 2 * d.group), :])
    for r in range(d.count):
        out[:, r * w : (r + 1) * w] = tick_rows(d, early, later, d.ticks - 1, r) - total[:, r * w : (r + 1) * w]


def last_other_kernel(d, face_ref, own_part, coupled, earlier, *rest):
    other, (out, held, sems) = rest[:-3], rest[-3:]
    blocks = list(arrived_blocks(d, face_ref[0], other, other))[1::2]
    part = 2 * d.width
    copies = []
    for i, c in enumerate(range(0, d.count * d.width, part)):
        total = own_part[:, c : c + part]
        for x, start in blocks:
            total -= dot_nn(x, coupled[pl.ds(start, 2 * d.group), c : c + part])
        held[:, c : c + part] = total.astype(BF)
        here = held.at[:, c : c + part]
        copies.append(pltpu.make_async_copy(here, out.at[d.ticks - 1, :, c : c + part], sems.at[i]))
        copies[-1].start()
    for copy in copies:
        copy.wait()


def call(body, name, smem, inputs, outs, scratch=(), flops=0, anywhere=(), sems=0, place=pltpu.VMEM, aliases=None):
    outs = [x if isinstance(x, jax.ShapeDtypeStruct) else jax.ShapeDtypeStruct(x, BF) for x in outs]
    specs = [pl.BlockSpec(memory_space=pl.ANY if i in anywhere else pltpu.VMEM) for i in range(len(inputs))]
    return pl.pallas_call(
        body,
        name=name,
        out_shape=outs,
        in_specs=[pl.BlockSpec(memory_space=pltpu.SMEM)] * len(smem) + specs,
        out_specs=[pl.BlockSpec(memory_space=place if x.dtype != jnp.int32 else pltpu.SMEM) for x in outs],
        scratch_shapes=[pltpu.VMEM(s, BF) for s in scratch] + ([pltpu.SemaphoreType.DMA((sems,))] if sems else []),
        input_output_aliases=aliases or {},
        compiler_params=pltpu.CompilerParams(vmem_limit_bytes=32 * 1024 * 1024),
        cost_estimate=pl.CostEstimate(flops=flops, bytes_accessed=0, transcendentals=0),
    )(*smem, *inputs)


def on_device(rhs, inflow, diag_tiles, off_tiles, cols, inverse_tiles, coupling, iface):
    faces, slabs = lax.axis_size("face"), lax.axis_size("slab")
    ticks, _, sources, _ = rhs.shape
    _, count, neigh, width, _ = off_tiles.shape
    nq = coupling.shape[1]
    d = Dims(ticks, sources, count, neigh, width, nq, faces)
    diag, off, inv, couple, cols = diag_tiles[0], off_tiles[0], inverse_tiles[0], coupling[0], cols[0].T
    face = lax.axis_index("face").astype(jnp.int32)[None]
    tile = width * width

    pairing = [(i, i ^ 1) for i in range(faces) if i ^ 1 < faces]
    crossing = [(i, ((i + 1) ^ 1) - 1) for i in range(faces) if 0 <= ((i + 1) ^ 1) - 1 < faces]

    def exchange(pair, cross):
        got = lax.ppermute(cross, "face", crossing)
        return lax.ppermute(pair, "face", pairing), got

    def swap(block):
        return lax.ppermute(block, "face", pairing)

    def onward(block, beside=lambda: None):
        own = []
        for hops in chip_hops(faces):
            route = []
            for s in range(1, slabs):
                for f in range(faces):
                    hop = hops[f % 2]
                    g = -1 if hop is None else hop_face(faces, f, hop)
                    if 0 <= g < faces:
                        route.append(((s - 1) * faces + g, s * faces + f))
            own.append(lax.ppermute(block, ("slab", "face"), route))
        made = beside()
        if made is not None:
            *own, made = lax.optimization_barrier((*own, made))
        return own + [swap(x) for x in own], made

    split, early, later, group, ext, wide = d.split, d.early, d.later, d.group, d.ext, d.wide
    sweep_flops = 2 * count * tile * (neigh + 1)
    ints = [jax.ShapeDtypeStruct(x.shape, x.dtype) for x in (iface, cols)]
    on_hbm = (iface, cols, inflow[0], couple, inv, rhs[:, 0], diag, off)
    field, field_later, gfield, pair, cross, pair_later, cross_later, inv, diag, off, iface, cols = call(
        functools.partial(first_kernel, d),
        "first",
        [face],
        [pltpu.with_memory_space_constraint(x, pltpu.HBM) for x in on_hbm],
        [(count, early, width), (count, later, width), (nq, width, width)]
        + [(HALO, early, width)] * 2
        + [(HALO, d.first_rows, width)] * 2
        + [x.shape for x in (inv, diag, off)]
        + ints,
        [(ticks, sources, count * width), (sources, group), (nq, width, width)],
        anywhere=range(8),
        sems=7 + ticks,
    )
    pair0, cross0 = exchange(pair, cross)
    pair_later0, cross_later0 = exchange(pair_later, cross_later)
    folded, met = call(
        functools.partial(fold_kernel, d),
        "fold",
        [face, iface, cols],
        [inv, diag, off],
        [(count, d.depth, width), (2 * HALO + nq + 1, width, count * width)],
    )
    edges, pair, cross, ext0 = call(
        functools.partial(second_edges_kernel, d),
        "second_edges",
        [face, cols],
        [field, pair0, cross0, folded],
        [(2 * HALO, early, width)] + [(HALO, early, width)] * 2 + [(ext, early, width)],
    )
    pair1, cross1 = exchange(pair, cross)
    edges_later, gfirst, pair, cross, ext_later0 = call(
        functools.partial(behind_kernel, d),
        "behind",
        [face, iface, cols],
        [field_later, gfield, pair_later0, cross_later0, met, folded, pair1],
        [(2 * HALO, later, width), (count, wide, width)] + [(HALO, later + 3 * group, width)] * 2 + [(ext, later, width)],
        anywhere=(6,),
    )
    pair_later1, cross_later1 = exchange(pair, cross)
    cross1, gfirst = lax.optimization_barrier((cross1, gfirst))
    (own_first,) = call(
        functools.partial(third_rows_kernel, d),
        "third_rows",
        [face, iface, cols],
        [edges, field, ext0, pair1, cross1, folded, gfirst],
        [(nq, sources, width)],
        [(count - 2 * HALO, sources, width), (ext, sources, width)],
        flops=12 * early * sweep_flops,
        anywhere=(6,),
    )
    (sent,) = call(
        functools.partial(merge_kernel, d),
        "merge",
        [face],
        [own_first, swap(own_first)],
        [(2 * nq, sources, width)],
    )

    def rest(first, ticks, rows, edges, field, ext0, pair, cross, after):
        return call(
            functools.partial(rest_kernel, d, first),
            "rest",
            [face, iface, cols],
            [edges, field, ext0, pair, cross, folded, after],
            [(count - 2 * HALO, rows, width), (ticks, nq, sources, width)],
            [(ext, ticks * sources, width)],
            anywhere=(6,),
        )

    inner, faces_early = rest(1, split - 1, early, edges, field, ext0, pair1, cross1, sent)
    early_parts = (edges, inner, field, pair1, cross1)

    def beside_first():
        rows = call(
            functools.partial(interface_kernel, d),
            "interface",
            [face, iface, cols],
            [gfield, gfirst, pair_later1, cross_later1, folded, inner],
            [(d.part, group)] * d.parts,
            [(ext, wide, width)],
            anywhere=(5,),
        )
        return rows, [swap(x) for x in rows]

    arrived, (chain, other_chain) = onward(sent, beside_first)
    other_early = swap(faces_early)

    def beside_second(sent):
        made = rest(0, ticks - 1 - split, later, edges_later, field_later, ext_later0, pair_later1, cross_later1, sent)
        return operator(), *made, swap(made[1])

    def fields(after):
        return call(
            functools.partial(third_kernel, d),
            "third",
            [face, cols],
            [*early_parts, *later_parts, folded, after],
            [(count, early, width), (count, later, width)],
            [(ext, early, width), (ext, later, width)],
            anywhere=(11,),
        )

    whole = (ticks, sources, count * width)

    def operator():
        return call(
            functools.partial(coupling_last_kernel, d),
            "coupling_last",
            [face, iface, cols],
            [gfield, gfirst, pair_later1, cross_later1, folded, chain[0]],
            [(wide, count * width)],
            [(ext, wide, width)],
            flops=wide * sweep_flops,
            anywhere=(5,),
        )[0]

    def output(blocks):
        return call(
            functools.partial(output_kernel, d),
            "output",
            [face],
            [*twice, coupled] + blocks,
            [whole],
            [(ticks - 1, sources, count * width)],
            sems=ticks - 1,
            place=pl.ANY,
        )[0]

    everything = []
    coupled = most = None
    for tick in range(1, ticks):
        everything += arrived
        if tick == ticks - 1:
            break
        early_tick = tick < split
        bases = (faces_early, other_early) if early_tick else (faces_later, other_later)
        (sent,) = call(
            functools.partial(chain_kernel, d, tick - 1 if early_tick else tick - split),
            "chain",
            [face],
            [*chain, *other_chain, *bases] + arrived,
            [(2 * nq, sources, width)],
            [(wide, 2 * group)],
            flops=4 * sources * wide * group,
        )
        if tick == 1:
            arrived, (coupled, inner_later, faces_later, other_later) = onward(sent, functools.partial(beside_second, sent))
            later_parts = (edges_later, inner_later, field_later, pair_later1, cross_later1)
        else:
            twice = fields(sent)
            arrived, most = onward(sent, lambda: output(everything))
    half = len(arrived) // 2
    (own_part,) = call(
        functools.partial(last_own_kernel, d),
        "last_own",
        [face],
        [*twice, coupled] + arrived[:half],
        [jax.ShapeDtypeStruct((sources, count * width), F32)],
    )
    (out,) = call(
        functools.partial(last_other_kernel, d),
        "last_other",
        [face],
        [own_part, coupled, most] + arrived[half:],
        [whole],
        [(sources, count * width)],
        anywhere=(2,),
        sems=count,
        place=pl.ANY,
        aliases={3: 0},
    )
    return out[:, None]


def solution(mesh):
    placed = (
        P(None, "slab", None, "face"),
        P("slab", None, "face"),
        P("slab", "face", None, None),
        P("slab", "face", None, None, None),
        P("slab", "face", None),
        P("slab", "face", None, None),
        P("slab", "face", None, None),
        P("face"),
    )
    return jax.shard_map(
        on_device,
        mesh=mesh,
        in_specs=placed,
        out_specs=P(None, "slab", None, "face"),
        check_vma=False,
    )
```

```python
import functools
import math

import jax
import jax.numpy as jnp
from jax import lax
from jax.experimental import pallas as pl
from jax.experimental.pallas import tpu as pltpu
from jax.sharding import PartitionSpec as P

HALO = 2
BF = jnp.bfloat16
F32 = jnp.float32


def dot_nt(a, b):
    return lax.dot_general(a, b, (((1,), (1,)), ((), ())), preferred_element_type=F32)


def dot_nn(a, b):
    return lax.dot_general(a, b, (((1,), (0,)), ((), ())), preferred_element_type=F32)


class Dims:
    def __init__(self, ticks, sources, count, neigh, width, nq, faces):
        self.ticks, self.sources, self.count, self.neigh = ticks, sources, count, neigh
        self.width, self.nq, self.faces = width, nq, faces
        self.split = max(ticks // 2, 1)
        self.early, self.later = self.split * sources, (ticks - self.split) * sources
        self.group = nq * width
        self.ext = count + 2 * HALO
        self.depth = (1 + neigh) * width
        self.slots = 4 if faces <= 4 else 6
        self.wide = self.slots * self.group
        self.parts = 4 if self.slots % 4 == 0 else 3
        self.part = self.wide // self.parts
        self.mark = 16
        self.share = -(-nq // HALO) * width
        self.first_rows = self.later + self.share + nq * self.mark
        self.ahead = max(count * 3 // 4 // 2 * 2, 2)
        self.last = count - HALO
        self.up = count + HALO

    def start(self, face):
        return pl.multiple_of(lax.rem(face + 2 * self.slots, self.slots) * self.group, self.group)

    def first_col(self, face):
        return face * self.count - HALO


def spans(rows):
    parts = -(-rows // 256)
    return [pl.ds(i * (rows // parts), rows // parts) for i in range(parts)]


def edge_rows(d, parity):
    return d.last * (1 - parity), d.last * parity


def first_kernel(
    d, face_ref, iface_hbm, cols_hbm, inflow, coupling, inv, rhs, diag_hbm, off_hbm, *rest
):
    early, later, gfield, *buffers, tiles, diag, off, iface, cols, right, flow, couple, sems = rest
    w = d.width
    moves = [(iface_hbm, iface), (inflow, flow), (coupling, couple), (inv, tiles)]
    moves += [(rhs.at[t], right.at[t]) for t in range(d.ticks)]
    moves += [(cols_hbm, cols), (diag_hbm, diag), (off_hbm, off)]
    copies = [pltpu.make_async_copy(a, b, sems.at[i]) for i, (a, b) in enumerate(moves)]
    for copy in copies:
        copy.start()
    for copy in copies[:4]:
        copy.wait()
    coupled = []
    for q in range(d.nq):
        turned = couple[q].astype(F32).T.astype(BF)
        gfield[q] = dot_nt(turned, tiles[iface[q]]).astype(BF)
        coupled.append(dot_nn(flow[:, q * w : (q + 1) * w], turned))
    for copy in copies[4 : 4 + d.ticks]:
        copy.wait()
    for r in range(d.count):
        x = jnp.concatenate([right[t, :, r * w : (r + 1) * w] for t in range(d.ticks)], axis=0)
        value = dot_nt(x, tiles[r]).astype(BF)
        early[r] = value[: d.early]
        later[r] = value[d.early :]
    for q in range(d.nq):
        row = iface[q]
        corrected = right[0, :, pl.ds(pl.multiple_of(row * w, w), w)].astype(F32) - coupled[q]
        early[row, 0 : d.sources, :] = dot_nt(corrected.astype(BF), tiles[row]).astype(BF)
    for i, start in enumerate(edge_rows(d, lax.rem(face_ref[0], 2))):
        buffers[i][...] = early[pl.ds(start, HALO)]
        buffer = buffers[2 + i]
        buffer[:, 0 : d.later, :] = later[pl.ds(start, HALO)]
        for q in range(d.nq):
            at = d.later + q // HALO * w
            buffer[q % HALO, at : at + w, :] = gfield[q]
            at = d.later + d.share + q * d.mark
            for e in range(HALO):
                buffer[e, at : at + d.mark, :] = jnp.full((d.mark, w), iface[q] == start + e).astype(F32).astype(BF)
    for copy in copies[4 + d.ticks :]:
        copy.wait()


def fold_kernel(d, face_ref, iface, cols, inv, diag, off, folded, met):
    w = d.width
    for r in range(d.count):
        tiles = jnp.concatenate([diag[r]] + [off[r, k] for k in range(d.neigh)], axis=1)
        product = dot_nn(inv[r], tiles)
        rows = lax.broadcasted_iota(jnp.int32, (w, w), 0)
        unit = (rows == lax.broadcasted_iota(jnp.int32, (w, w), 1)).astype(F32)
        for k in range(1 + d.neigh):
            part = product[:, k * w : (k + 1) * w].T
            folded[r, k * w : (k + 1) * w, :] = ((unit if k == 0 else 0.0) - part).astype(BF)
    spare = 2 * HALO + d.nq
    met[0 : 2 * HALO] = jnp.zeros((2 * HALO, w, d.count * w), BF)
    for r in range(d.count):
        lanes = slice(r * w, (r + 1) * w)
        for q in range(d.nq):
            met[2 * HALO + q, :, lanes] = jnp.where(iface[q] == r, folded[r, 0:w, :], jnp.zeros((w, w), BF))
        for k in range(d.neigh):
            c = cols[k, r] - d.first_col(face_ref[0])
            at = jnp.where(c < HALO, c, jnp.where(c >= d.up, c - d.count, spare))
            for q in range(d.nq):
                at = jnp.where(c == iface[q] + HALO, 2 * HALO + q, at)
            met[at, :, lanes] += folded[r, (1 + k) * w : (2 + k) * w, :]


def sweep(d, cols, face, ext, span, r, folded):
    x = [ext[r + HALO, span, :]] + [ext[cols[k, r] - d.first_col(face), span, :] for k in range(d.neigh)]
    return dot_nn(jnp.concatenate(x, axis=1), folded[r])


def place_halo(d, face, pair_in, cross_in, ext, rows):
    parity = lax.rem(face, 2)
    ext[pl.ds(d.up * (1 - parity), HALO)] = pair_in[:, rows, :]
    ext[pl.ds(d.up * parity, HALO)] = cross_in[:, rows, :]


def extend(d, face, edges, inner, pair_in, cross_in, ext, rows):
    ext[HALO : 2 * HALO] = edges[0:HALO, rows, :]
    ext[2 * HALO : d.count] = inner[:, rows, :]
    ext[d.count : d.up] = edges[HALO : 2 * HALO, rows, :]
    place_halo(d, face, pair_in, cross_in, ext, rows)


def correct(d, cols, face, base, folded, out, ext, rows):
    for i, r in enumerate(rows):
        for span in spans(out.shape[1]):
            value = base[r, span, :].astype(F32) + sweep(d, cols, face, ext, span, r, folded)
            out[i, span, :] = value.astype(BF)


def correct_edges(d, cols, face, field, pair_in, cross_in, folded, edges, ext):
    ext[HALO : HALO + d.count] = field[...]
    place_halo(d, face, pair_in, cross_in, ext, pl.ds(0, field.shape[1]))
    correct(d, cols, face, field, folded, edges, ext, list(range(HALO)) + list(range(d.last, d.count)))


def second_edges_kernel(d, face_ref, cols, field, pair_in, cross_in, folded, edges, pair, cross, ext):
    face = face_ref[0]
    parity = lax.rem(face, 2)
    correct_edges(d, cols, face, field, pair_in, cross_in, folded, edges, ext)
    pair[...] = edges[pl.ds(HALO * (1 - parity), HALO)]
    cross[...] = edges[pl.ds(HALO * parity, HALO)]


def interface_rows(d, face, iface, cols, edges, inner, field, pair_in, cross_in, folded, first, outs, ext):
    ticks = pl.ds(first * d.sources, len(outs) * d.sources)
    extend(d, face, edges, inner, pair_in, cross_in, ext, ticks)
    for q in range(d.nq):
        row = iface[q]
        value = sweep(d, cols, face, ext, pl.ds(0, len(outs) * d.sources), row, folded)
        value = (field[row, ticks, :].astype(F32) + value).astype(BF)
        for t, out in enumerate(outs):
            out[q] = value[t * d.sources : (t + 1) * d.sources]


def third_rows_kernel(d, face_ref, iface, cols, edges, field, ext0, pair_in, cross_in, folded, after, sent, inner, ext):
    face = face_ref[0]
    correct(d, cols, face, field, folded, inner, ext0, range(HALO, d.last))
    interface_rows(d, face, iface, cols, edges, inner, field, pair_in, cross_in, folded, 0, [sent], ext)


def third_kernel(d, face_ref, cols, *rest):
    *inputs, folded, after, early, later, early_ext, later_ext = rest
    face = face_ref[0]
    for i, (out, ext) in enumerate(((early, early_ext), (later, later_ext))):
        edges, inner, field, pair_in, cross_in = inputs[5 * i : 5 * i + 5]
        extend(d, face, edges, inner, pair_in, cross_in, ext, pl.ds(0, out.shape[1]))
        correct(d, cols, face, field, folded, out, ext, range(d.count))


def marked(d, block, e):
    parts = []
    for q in range(d.nq):
        at = d.later + q // HALO * d.width
        mark = d.later + d.share + q * d.mark
        mark = block[e, mark : mark + d.mark, :]
        parts.append(block[q % HALO, at : at + d.width, :] * jnp.concatenate([mark] * (d.width // d.mark), axis=0))
    return jnp.concatenate(parts, axis=0)


def behind_kernel(
    d, face_ref, iface, cols, field, gfield, pair_in, cross_in, met, folded, after, edges, out, pair, cross, field_ext
):
    face = face_ref[0]
    parity = lax.rem(face, 2)
    correct_edges(d, cols, face, field, pair_in, cross_in, folded, edges, field_ext)
    pair[:, 0 : d.later, :] = edges[pl.ds(HALO * (1 - parity), HALO)]
    cross[:, 0 : d.later, :] = edges[pl.ds(HALO * parity, HALO)]
    w = d.width
    for shift in range(2, d.slots - 1):
        out[:, pl.ds(d.start(face + shift), d.group), :] = jnp.zeros((d.count, d.group, w), BF)

    def put(start, rows, value):
        for r in range(d.count):
            out[r, pl.ds(start, rows), :] = value[:, r * w : (r + 1) * w].astype(BF)

    pair_face, cross_face = face + 1 - 2 * parity, face - 1 + 2 * parity
    for at, other, block in ((HALO * (1 - parity), pair_face, pair_in), (HALO * parity, cross_face, cross_in)):
        x = jnp.concatenate([marked(d, block, e) for e in range(HALO)], axis=1)
        tiles = jnp.concatenate([met[at + e] for e in range(HALO)], axis=0)
        put(d.start(other), d.group, dot_nn(x, tiles))
    for q in range(d.nq):
        start = d.start(face) + q * w
        put(start, w, dot_nn(gfield[q], met[2 * HALO + q]))
        row = iface[q]
        span = pl.ds(pl.multiple_of(start, w), w)
        out[row, span, :] = (out[row, span, :].astype(F32) + gfield[q].astype(F32)).astype(BF)
    for start, buffer in zip(edge_rows(d, parity), (pair, cross)):
        for i, shift in enumerate((-1, 0, 1)):
            at = d.later + i * d.group
            buffer[:, at : at + d.group, :] = out[pl.ds(start, HALO), pl.ds(d.start(face + shift), d.group), :]


def coupling_ext(d, face, gfirst, pair_in, cross_in, ext):
    parity = lax.rem(face, 2)
    ext[0:HALO] = jnp.zeros((HALO, d.wide, d.width), BF)
    ext[d.up : d.ext] = jnp.zeros((HALO, d.wide, d.width), BF)
    ext[HALO : HALO + d.count] = gfirst[...]
    neighbours = ((d.up * (1 - parity), face + 1 - 2 * parity, pair_in), (d.up * parity, face - 1 + 2 * parity, cross_in))
    for start, other, block in neighbours:
        for i, shift in enumerate((-1, 0, 1)):
            at = d.later + i * d.group
            ext[pl.ds(start, HALO), pl.ds(d.start(other + shift), d.group), :] = block[:, at : at + d.group, :]


def rest_kernel(d, first, face_ref, iface, cols, edges, field, ext0, pair_in, cross_in, folded, after, inner, faces_out, ext):
    face = face_ref[0]
    correct(d, cols, face, field, folded, inner, ext0, range(HALO, d.last))
    outs = [faces_out.at[t] for t in range(faces_out.shape[0])]
    interface_rows(d, face, iface, cols, edges, inner, field, pair_in, cross_in, folded, first, outs, ext)


def interface_kernel(d, face_ref, iface, cols, gfield, gfirst, pair_in, cross_in, folded, after, *rest):
    *chain, ext = rest
    face = face_ref[0]
    w = d.width
    coupling_ext(d, face, gfirst, pair_in, cross_in, ext)
    for i in range(d.slots):
        start = i * d.group % d.part
        part = chain[i * d.group // d.part]
        for q in range(d.nq):
            value = sweep(d, cols, face, ext, pl.ds(i * d.group, d.group), iface[q], folded)
            part[start : start + d.group, q * w : (q + 1) * w] = value.astype(BF)

        @pl.when(lax.rem(face, d.slots) == i)
        def _():
            for q in range(d.nq):
                block = (slice(start + q * w, start + (q + 1) * w), slice(q * w, (q + 1) * w))
                part[block] = (part[block].astype(F32) + gfield[q].astype(F32)).astype(BF)


def operator_rows(d, face, iface, cols, gfield, folded, ext, rows, out):
    w = d.width
    for i, r in enumerate(rows):
        for s in range(0, d.wide, d.group):
            span = pl.ds(s, d.group)
            out[span, i * w : (i + 1) * w] = sweep(d, cols, face, ext, span, r, folded).astype(BF)
    for q in range(d.nq):

        @pl.when(jnp.logical_and(iface[q] >= rows[0], iface[q] <= rows[-1]))
        def _():
            lane = pl.ds(pl.multiple_of((iface[q] - rows[0]) * w, w), w)
            span = pl.ds(pl.multiple_of(d.start(face) + q * w, w), w)
            out[span, lane] = (out[span, lane].astype(F32) + gfield[q].astype(F32)).astype(BF)


def operator_kernel(d, face_ref, iface, cols, gfield, gfirst, pair_in, cross_in, folded, after, out, ext):
    coupling_ext(d, face_ref[0], gfirst, pair_in, cross_in, ext)
    operator_rows(d, face_ref[0], iface, cols, gfield, folded, ext, range(d.ahead), out)


def operator_rest_kernel(d, face_ref, iface, cols, gfield, folded, ext, after, out):
    operator_rows(d, face_ref[0], iface, cols, gfield, folded, ext, range(d.ahead, d.count), out)


def operator_part(d, halves, row, depth, lane, lanes):
    width = halves[0].shape[1]
    half = halves[lane // width]
    return half[pl.ds(row, depth), lane % width : lane % width + lanes]


def chip_hops(faces):
    return [(0, None)] if faces <= 2 else [(0, 1)] if faces <= 4 else [(0, 1), (-1, None)]


def hop_face(faces, face, hop):
    return face ^ (2 * hop) if faces <= 4 else face + 2 * hop


def arrived_blocks(d, face, own, other):
    parity = lax.rem(face, 2)
    for i, hops in enumerate(chip_hops(d.faces)):
        starts = [0 if hop is None else d.start(hop_face(d.faces, face - parity, hop)) for hop in hops]
        for block, odd in ((own[i], parity), (other[i], 1 - parity)):
            start = pl.multiple_of(jnp.where(odd == 1, starts[1], starts[0]), d.group)
            yield jnp.concatenate([block[j] for j in range(2 * d.nq)], axis=1), start


def chain_kernel(d, tick, face_ref, *rest):
    own_chain, other_chain, rest = rest[: d.parts], rest[d.parts : 2 * d.parts], rest[2 * d.parts :]
    own_faces, other_faces, *arrived, sent, chain = rest
    face = face_ref[0]
    parity = lax.rem(face, 2)
    for i in range(d.parts):
        for j, part in enumerate((own_chain[i], other_chain[i])):
            chain[i * d.part : (i + 1) * d.part, j * d.group : (j + 1) * d.group] = part[...]
    half = len(arrived) // 2
    total = jnp.zeros((d.sources, 2 * d.group), F32)
    for x, start in arrived_blocks(d, face, arrived[:half], arrived[half:]):
        total += dot_nn(x, chain[pl.ds(start, 2 * d.group), :])
    for j, (base, odd) in enumerate(((own_faces, parity), (other_faces, 1 - parity))):
        for q in range(d.nq):
            at = j * d.group + q * d.width
            sent[odd * d.nq + q] = (base[tick, q].astype(F32) - total[:, at : at + d.width]).astype(BF)


def merge_kernel(d, face_ref, own, other, sent):
    parity = lax.rem(face_ref[0], 2)
    for q in range(d.nq):
        sent[parity * d.nq + q] = own[q]
        sent[(1 - parity) * d.nq + q] = other[q]


def tick_rows(d, early, later, tick, row):
    fields, at = (early, tick) if tick < d.split else (later, tick - d.split)
    return fields[row, at * d.sources : (at + 1) * d.sources, :].astype(F32)


def output_kernel(d, face_ref, early, later, first_half, second_half, *rest):
    *arrived, out, held, sems = rest
    w = d.width
    each = 2 * len(chip_hops(d.faces))
    copies = []
    part = 2 * w
    for t in range(d.ticks - 1):
        blocks = []
        if t:
            mine, arrived = arrived[:each], arrived[each:]
            blocks = list(arrived_blocks(d, face_ref[0], mine[: each // 2], mine[each // 2 :]))
        for c in range(0, d.count * w, part):
            total = jnp.zeros((d.sources, part), F32)
            for x, start in blocks:
                total += dot_nn(x, operator_part(d, (first_half, second_half), start, 2 * d.group, c, part))
            for j in range(0, part, w):
                value = tick_rows(d, early, later, t, (c + j) // w) - total[:, j : j + w]
                held[t, :, c + j : c + j + w] = value.astype(BF)
        copies.append(pltpu.make_async_copy(held.at[t], out.at[t], sems.at[t]))
        copies[-1].start()
    for copy in copies:
        copy.wait()


def last_own_kernel(d, face_ref, early, later, first_half, second_half, *rest):
    own, out = rest[:-1], rest[-1]
    w = d.width
    blocks = list(arrived_blocks(d, face_ref[0], own, own))[0::2]
    for c in range(0, d.count * w, 2 * w):
        total = jnp.zeros((d.sources, 2 * w), F32)
        for x, start in blocks:
            total += dot_nn(x, operator_part(d, (first_half, second_half), start, 2 * d.group, c, 2 * w))
        for j in range(0, 2 * w, w):
            out[:, c + j : c + j + w] = tick_rows(d, early, later, d.ticks - 1, (c + j) // w) - total[:, j : j + w]


def last_other_kernel(d, face_ref, own_part, first_half, second_half, earlier, *rest):
    other, (out, held, sems) = rest[:-3], rest[-3:]
    blocks = list(arrived_blocks(d, face_ref[0], other, other))[1::2]
    part = 2 * d.width
    copies = []
    for i, c in enumerate(range(0, d.count * d.width, part)):
        total = own_part[:, c : c + part]
        for x, start in blocks:
            total -= dot_nn(x, operator_part(d, (first_half, second_half), start, 2 * d.group, c, part))
        held[:, c : c + part] = total.astype(BF)
        here = held.at[:, c : c + part]
        copies.append(pltpu.make_async_copy(here, out.at[d.ticks - 1, :, c : c + part], sems.at[i]))
        copies[-1].start()
    for copy in copies:
        copy.wait()


def call(body, name, smem, inputs, outs, scratch=(), flops=0, anywhere=(), sems=0, place=pltpu.VMEM, aliases=None):
    outs = [x if isinstance(x, jax.ShapeDtypeStruct) else jax.ShapeDtypeStruct(x, BF) for x in outs]
    specs = [pl.BlockSpec(memory_space=pl.ANY if i in anywhere else pltpu.VMEM) for i in range(len(inputs))]
    return pl.pallas_call(
        body,
        name=name,
        out_shape=outs,
        in_specs=[pl.BlockSpec(memory_space=pltpu.SMEM)] * len(smem) + specs,
        out_specs=[pl.BlockSpec(memory_space=place if x.dtype != jnp.int32 else pltpu.SMEM) for x in outs],
        scratch_shapes=[pltpu.VMEM(s, BF) for s in scratch] + ([pltpu.SemaphoreType.DMA((sems,))] if sems else []),
        input_output_aliases=aliases or {},
        compiler_params=pltpu.CompilerParams(vmem_limit_bytes=32 * 1024 * 1024),
        cost_estimate=pl.CostEstimate(flops=flops, bytes_accessed=0, transcendentals=0),
    )(*smem, *inputs)


def on_device(rhs, inflow, diag_tiles, off_tiles, cols, inverse_tiles, coupling, iface):
    faces, slabs = lax.axis_size("face"), lax.axis_size("slab")
    ticks, _, sources, _ = rhs.shape
    _, count, neigh, width, _ = off_tiles.shape
    nq = coupling.shape[1]
    d = Dims(ticks, sources, count, neigh, width, nq, faces)
    diag, off, inv, couple, cols = diag_tiles[0], off_tiles[0], inverse_tiles[0], coupling[0], cols[0].T
    face = lax.axis_index("face").astype(jnp.int32)[None]
    tile = width * width

    pairing = [(i, i ^ 1) for i in range(faces) if i ^ 1 < faces]
    crossing = [(i, ((i + 1) ^ 1) - 1) for i in range(faces) if 0 <= ((i + 1) ^ 1) - 1 < faces]

    def exchange(pair, cross):
        got = lax.ppermute(cross, "face", crossing)
        return lax.ppermute(pair, "face", pairing), got

    def swap(block):
        return lax.ppermute(block, "face", pairing)

    def onward(block, beside=lambda: None):
        own = []
        for hops in chip_hops(faces):
            route = []
            for s in range(1, slabs):
                for f in range(faces):
                    hop = hops[f % 2]
                    g = -1 if hop is None else hop_face(faces, f, hop)
                    if 0 <= g < faces:
                        route.append(((s - 1) * faces + g, s * faces + f))
            own.append(lax.ppermute(block, ("slab", "face"), route))
        made = beside()
        if made is not None:
            *own, made = lax.optimization_barrier((*own, made))
        return own + [swap(x) for x in own], made

    split, early, later, group, ext, wide = d.split, d.early, d.later, d.group, d.ext, d.wide
    sweep_flops = 2 * count * tile * (neigh + 1)
    ints = [jax.ShapeDtypeStruct(x.shape, x.dtype) for x in (iface, cols)]
    on_hbm = (iface, cols, inflow[0], couple, inv, rhs[:, 0], diag, off)
    field, field_later, gfield, pair, cross, pair_later, cross_later, inv, diag, off, iface, cols = call(
        functools.partial(first_kernel, d),
        "first",
        [face],
        [pltpu.with_memory_space_constraint(x, pltpu.HBM) for x in on_hbm],
        [(count, early, width), (count, later, width), (nq, width, width)]
        + [(HALO, early, width)] * 2
        + [(HALO, d.first_rows, width)] * 2
        + [x.shape for x in (inv, diag, off)]
        + ints,
        [(ticks, sources, count * width), (sources, group), (nq, width, width)],
        anywhere=range(8),
        sems=7 + ticks,
    )
    pair0, cross0 = exchange(pair, cross)
    pair_later0, cross_later0 = exchange(pair_later, cross_later)
    folded, met = call(
        functools.partial(fold_kernel, d),
        "fold",
        [face, iface, cols],
        [inv, diag, off],
        [(count, d.depth, width), (2 * HALO + nq + 1, width, count * width)],
    )
    edges, pair, cross, ext0 = call(
        functools.partial(second_edges_kernel, d),
        "second_edges",
        [face, cols],
        [field, pair0, cross0, folded],
        [(2 * HALO, early, width)] + [(HALO, early, width)] * 2 + [(ext, early, width)],
    )
    pair1, cross1 = exchange(pair, cross)
    edges_later, gfirst, pair, cross, ext_later0 = call(
        functools.partial(behind_kernel, d),
        "behind",
        [face, iface, cols],
        [field_later, gfield, pair_later0, cross_later0, met, folded, pair1],
        [(2 * HALO, later, width), (count, wide, width)] + [(HALO, later + 3 * group, width)] * 2 + [(ext, later, width)],
        anywhere=(6,),
    )
    pair_later1, cross_later1 = exchange(pair, cross)
    cross1, gfirst = lax.optimization_barrier((cross1, gfirst))
    (own_first,) = call(
        functools.partial(third_rows_kernel, d),
        "third_rows",
        [face, iface, cols],
        [edges, field, ext0, pair1, cross1, folded, gfirst],
        [(nq, sources, width)],
        [(count - 2 * HALO, sources, width), (ext, sources, width)],
        flops=12 * early * sweep_flops,
        anywhere=(6,),
    )
    (sent,) = call(
        functools.partial(merge_kernel, d),
        "merge",
        [face],
        [own_first, swap(own_first)],
        [(2 * nq, sources, width)],
    )

    def rest(first, ticks, rows, edges, field, ext0, pair, cross, after):
        return call(
            functools.partial(rest_kernel, d, first),
            "rest",
            [face, iface, cols],
            [edges, field, ext0, pair, cross, folded, after],
            [(count - 2 * HALO, rows, width), (ticks, nq, sources, width)],
            [(ext, ticks * sources, width)],
            anywhere=(6,),
        )

    inner, faces_early = rest(1, split - 1, early, edges, field, ext0, pair1, cross1, sent)
    early_parts = (edges, inner, field, pair1, cross1)

    def beside_first():
        rows = call(
            functools.partial(interface_kernel, d),
            "interface",
            [face, iface, cols],
            [gfield, gfirst, pair_later1, cross_later1, folded, inner],
            [(d.part, group)] * d.parts,
            [(ext, wide, width)],
            anywhere=(5,),
        )
        return rows, [swap(x) for x in rows]

    arrived, (chain, other_chain) = onward(sent, beside_first)
    other_early = swap(faces_early)

    def beside_second(sent):
        first_half, read = operator(sent)
        made = rest(0, ticks - 1 - split, later, edges_later, field_later, ext_later0, pair_later1, cross_later1, first_half)
        return first_half, read, *made, swap(made[1])

    def fields(after):
        return call(
            functools.partial(third_kernel, d),
            "third",
            [face, cols],
            [*early_parts, *later_parts, folded, after],
            [(count, early, width), (count, later, width)],
            [(ext, early, width), (ext, later, width)],
            anywhere=(11,),
        )

    whole = (ticks, sources, count * width)

    def operator(after):
        return call(
            functools.partial(operator_kernel, d),
            "operator",
            [face, iface, cols],
            [gfield, gfirst, pair_later1, cross_later1, folded, after],
            [(wide, d.ahead * width), (ext, wide, width)],
            flops=wide * sweep_flops // 2,
            anywhere=(5,),
        )

    def operator_rest(after):
        return call(
            functools.partial(operator_rest_kernel, d),
            "operator_rest",
            [face, iface, cols],
            [gfield, folded, read, after],
            [(wide, (count - d.ahead) * width)],
            anywhere=(3,),
        )[0]

    def output(blocks):
        return call(
            functools.partial(output_kernel, d),
            "output",
            [face],
            [*twice, first_half, second_half] + blocks,
            [whole],
            [(ticks - 1, sources, count * width)],
            sems=ticks - 1,
            place=pl.ANY,
        )[0]

    everything = []
    most = None
    for tick in range(1, ticks):
        everything += arrived
        if tick == ticks - 1:
            break
        early_tick = tick < split
        bases = (faces_early, other_early) if early_tick else (faces_later, other_later)
        (sent,) = call(
            functools.partial(chain_kernel, d, tick - 1 if early_tick else tick - split),
            "chain",
            [face],
            [*chain, *other_chain, *bases] + arrived,
            [(2 * nq, sources, width)],
            [(wide, 2 * group)],
            flops=4 * sources * wide * group,
        )
        if tick == 1:
            arrived, (first_half, read, inner_later, faces_later, other_later) = onward(sent, functools.partial(beside_second, sent))
            later_parts = (edges_later, inner_later, field_later, pair_later1, cross_later1)
        else:
            twice = fields(sent)
            second_half = operator_rest(sent)
            arrived, most = onward(sent, lambda: output(everything))
    half = len(arrived) // 2
    (own_part,) = call(
        functools.partial(last_own_kernel, d),
        "last_own",
        [face],
        [*twice, first_half, second_half] + arrived[:half],
        [jax.ShapeDtypeStruct((sources, count * width), F32)],
    )
    (out,) = call(
        functools.partial(last_other_kernel, d),
        "last_other",
        [face],
        [own_part, first_half, second_half, most] + arrived[half:],
        [whole],
        [(sources, count * width)],
        anywhere=(3,),
        sems=count,
        place=pl.ANY,
        aliases={4: 0},
    )
    return out[:, None]


def solution(mesh):
    placed = (
        P(None, "slab", None, "face"),
        P("slab", None, "face"),
        P("slab", "face", None, None),
        P("slab", "face", None, None, None),
        P("slab", "face", None),
        P("slab", "face", None, None),
        P("slab", "face", None, None),
        P("face"),
    )
    return jax.shard_map(
        on_device,
        mesh=mesh,
        in_specs=placed,
        out_specs=P(None, "slab", None, "face"),
        check_vma=False,
    )
```
